32 devices in a mesh: groups: 2 (over x), expert: 16 (over z, y, core).
Axes of the slice: x: 2, y: 2, z: 4, core: 2. Of those that a mesh axis runs over, the one named last changes fastest.
Arguments:
- tokens: bfloat16 [2048, 2048], P(('groups', 'expert')), parts along dimension 0, may hold values from -6 to 6
- expert_ids: int32 [2048, 8], P(('groups', 'expert')), parts along dimension 0, may hold values from 0 to 15, as said below
- gate_weights: float32 [2048, 8], P(('groups', 'expert')), parts along dimension 0, may hold values from 0.05 to 0.5
- w_gate: bfloat16 [16, 2048, 768], P('expert'), may hold values from -0.125 to 0.125
- w_up: bfloat16 [16, 2048, 768], P('expert'), may hold values from -0.125 to 0.125
- w_down: bfloat16 [16, 768, 2048], P('expert'), may hold values from -0.21875 to 0.21875
Outputs:
- mixed: bfloat16 [2048, 2048], P(('groups', 'expert')), parts along dimension 0
The draws below stay inside these ranges and needn't reach their ends.
There are 2 independent parts, one for each index of `groups`. The reference program is written for one: setup_inputs(seed, part) draws one part's arguments, and reference() takes and returns one part's arrays. A program takes and returns all parts, laid end to end along the dimension named above; an argument that names none is the same for every part. Nothing has to cross between parts.
Inputs may be any that keep to these rules, and one draw needn't show every extreme that they name: `expert_ids`: each token names 8 different experts. Exactly 2 experts are named exactly 64 times by the tokens of every device; every other expert is named at most 28 times by the tokens of one device, and in every draw some such expert is named exactly 28 times by the tokens of every device.
All inputs are finite; a program needn't handle non-finite values.
Results may differ from the reference program's by a relative error of at most 0.0057.
Values may be sent and summed in bfloat16 or wider, within the bound.
No kernel may reach another device: no remote copies, remote signals or barrier semaphores. Data moves between devices by JAX's collectives and lax.ppermute only.
A program may use at most 128 MiB of HBM per device.

```python
import math
from functools import partial
import jax
import jax.numpy as jnp
from jax import lax

D = 2048
FF = 768
TOP = 8
HOT = 2
TOK_DEV = 64
EXPERTS = 16
TOKENS = 1024
CAP = 64


def route_block(is_hot, base_load, extra_load, block_key):
    order_key, token_key, turn_key = jax.random.split(block_key, 3)
    shuffled = jax.random.permutation(order_key, EXPERTS).astype(jnp.int32)
    ranking = jnp.argsort(jnp.argsort(shuffled + EXPERTS * is_hot))
    expert_load = jnp.where(is_hot > 0, CAP, base_load + (ranking < extra_load).astype(jnp.int32))
    load_ends = jnp.cumsum(expert_load)
    slot_index = jnp.arange(TOK_DEV * TOP, dtype=jnp.int32)
    listing = jnp.sum((load_ends[None, :] <= slot_index[:, None]).astype(jnp.int32), axis=1)
    route_table = listing.reshape(TOP, TOK_DEV).T
    rotation = jax.random.randint(turn_key, (TOK_DEV, 1), 0, TOP)
    column = (jnp.arange(TOP, dtype=jnp.int32)[None, :] + rotation) % TOP
    route_table = jnp.take_along_axis(route_table, column, axis=1)
    return route_table[jax.random.permutation(token_key, TOK_DEV)]


def draw_expert_ids(key, part):
    hot_order = jax.random.permutation(jax.random.fold_in(key, 11), EXPERTS)
    is_hot = (hot_order < HOT).astype(jnp.int32)
    spread_rows = TOK_DEV * TOP - HOT * CAP
    base_load = spread_rows // (EXPERTS - HOT)
    extra_load = spread_rows % (EXPERTS - HOT)
    block_keys = jax.random.split(jax.random.fold_in(key, 23), TOKENS // TOK_DEV)
    routed = jax.vmap(partial(route_block, is_hot, base_load, extra_load))(block_keys)
    return routed.reshape(TOKENS, TOP).astype(jnp.int32)


def steps_of(own_key, shape, shards, least, top_value):
    loudness, own = 1.0, jax.random.fold_in(own_key, 6)
    for axis_at, parts in shards:
        steps = jnp.exp(jax.random.uniform(jax.random.fold_in(own, axis_at), (parts,), jnp.float32, least / len(shards), top_value / len(shards)))
        loudness = loudness * jnp.repeat(steps, shape[axis_at] // parts).reshape([-1 if axis == axis_at else 1 for axis in range(len(shape))])
    return loudness


def noise(rng, dims, width, most, cuts=(), kind=jnp.bfloat16):
    array = width * jax.random.normal(rng, dims, jnp.float32)
    if cuts:
        array = array * steps_of(rng, dims, cuts, -0.22, 0.18)
    return jnp.clip(array, -most, most).astype(kind)


def setup_inputs(seed: int = 0, part: int = 0) -> dict:
    key_of = jax.random.split(jax.random.key(seed), 7)
    part_keys = jax.random.split(jax.random.fold_in(key_of[6], part), 7)
    return {
        "tokens": noise(part_keys[0], (TOKENS, D), 1.0, 6.0, ((0, 16),)),
        "expert_ids": draw_expert_ids(jax.random.fold_in(jax.random.fold_in(key_of[6], part), 71), part),
        "gate_weights": jnp.clip(jnp.exp(math.log(0.5) - 2.3025851 * jax.random.uniform(part_keys[2], (TOKENS, TOP), jnp.float32) ** steps_of(part_keys[2], (TOKENS, TOP), ((0, 16),), -0.2, 0.2)), 0.05, 0.5),
        "w_gate": noise(key_of[3], (EXPERTS, D, FF), D ** -0.5, 0.125, ((0, 16),)),
        "w_up": noise(key_of[4], (EXPERTS, D, FF), D ** -0.5, 0.125, ((0, 16),)),
        "w_down": noise(key_of[5], (EXPERTS, FF, D), FF ** -0.5, 0.21875, ((0, 16),)),
    }


row_block = 128


def reference(tokens, expert_ids, gate_weights, w_gate, w_up, w_down):
    flat_ids = expert_ids.reshape(-1).astype(jnp.int32)
    slot_total = flat_ids.shape[0]
    block_count = (slot_total + row_block - 1) // row_block + EXPERTS
    total_rows = block_count * row_block
    expert_range = jnp.arange(EXPERTS, dtype=jnp.int32)
    onehot = (flat_ids[:, None] == expert_range[None, :]).astype(jnp.int32)
    per_expert = jnp.sum(onehot, axis=0)
    rank_inside = jnp.sum(jnp.cumsum(onehot, axis=0) * onehot, axis=1) - 1
    padded_count = (per_expert + row_block - 1) // row_block * row_block
    expert_start = jnp.cumsum(padded_count) - padded_count
    position = expert_start[flat_ids] + rank_inside
    token_of_slot = jnp.arange(slot_total, dtype=jnp.int32) // TOP
    source_token = jnp.full((total_rows,), -1, jnp.int32).at[position].set(token_of_slot)
    block_start = jnp.arange(block_count, dtype=jnp.int32) * row_block
    expert_end = expert_start + padded_count
    block_expert = jnp.sum((expert_end[None, :] <= block_start[:, None]).astype(jnp.int32), axis=1)
    block_expert = jnp.minimum(block_expert, EXPERTS - 1).astype(jnp.int32)

    def one_block(carry, block_pair):
        expert_now, token_slice = block_pair
        is_valid = token_slice >= 0
        picked = tokens[jnp.maximum(token_slice, 0)]
        picked = jnp.where(is_valid[:, None], picked, jnp.zeros((), tokens.dtype))
        gate_part = jnp.dot(picked, w_gate[expert_now], preferred_element_type=jnp.float32)
        up_part = jnp.dot(picked, w_up[expert_now], preferred_element_type=jnp.float32)
        hidden = (jax.nn.silu(gate_part) * up_part).astype(jnp.bfloat16)
        result = jnp.dot(hidden, w_down[expert_now], preferred_element_type=jnp.float32).astype(jnp.bfloat16)
        return carry, result

    carry_out, outputs = lax.scan(one_block, jnp.zeros((), jnp.int32), (block_expert, source_token.reshape(block_count, row_block)))
    expert_out = outputs.reshape(total_rows, D)[position].reshape(TOKENS, TOP, D)
    mixed = jnp.sum(expert_out.astype(jnp.float32) * gate_weights.astype(jnp.float32)[:, :, None], axis=1)
    return mixed.astype(jnp.bfloat16)
```

```python
import functools

import jax
import jax.numpy as jnp
from jax import lax
from jax.experimental import pallas as pl
from jax.experimental.pallas import tpu as pltpu
from jax.sharding import PartitionSpec as P

LANES = 128


def rows_per_block(rows, most):
    block = most
    while rows % block:
        block //= 2
    return block


def expert_kernel(width, top_count, me_ref, rows_ref, gate_ref, up_ref, down_ref, out_ref):
    rows = rows_ref[:, :width]
    route = rows_ref[:, width:].astype(jnp.float32)
    chosen = (route[:, :top_count] == me_ref[0].astype(jnp.float32)).astype(jnp.float32)
    weight = sum(route[:, top_count * part : top_count * (part + 1)] for part in (1, 2, 3))
    scale = jnp.sum(chosen * weight, axis=1, keepdims=True)
    gate_part = jnp.dot(rows, gate_ref[0], preferred_element_type=jnp.float32)
    up_part = jnp.dot(rows, up_ref[0], preferred_element_type=jnp.float32)
    hidden = (gate_part / (1.0 + jnp.exp(-gate_part)) * up_part).astype(jnp.bfloat16)
    result = jnp.dot(hidden, down_ref[0], preferred_element_type=jnp.float32)
    out_ref[...] = (result * scale).astype(out_ref.dtype)


def run_expert(rows, me, width, top_count, w_gate, w_up, w_down):
    total, row_width = rows.shape
    block = rows_per_block(total, 256)
    hidden_width = w_gate.shape[2]

    def whole(array):
        return pl.BlockSpec(
            array.shape, lambda i, me: (0, 0, 0), pipeline_mode=pl.Buffered(buffer_count=1)
        )

    return pl.pallas_call(
        functools.partial(expert_kernel, width, top_count),
        out_shape=jax.ShapeDtypeStruct((total, width), jnp.bfloat16),
        grid_spec=pltpu.PrefetchScalarGridSpec(
            num_scalar_prefetch=1,
            grid=(total // block,),
            in_specs=[
                pl.BlockSpec((block, row_width), lambda i, me: (i, 0)),
                whole(w_gate),
                whole(w_up),
                whole(w_down),
            ],
            out_specs=pl.BlockSpec((block, width), lambda i, me: (i, 0)),
        ),
        compiler_params=pltpu.CompilerParams(vmem_limit_bytes=48 * 1024 * 1024),
        cost_estimate=pl.CostEstimate(
            flops=6 * total * width * hidden_width,
            bytes_accessed=2 * (3 * width * hidden_width + 2 * total * width),
            transcendentals=total * hidden_width,
        ),
    )(me, rows, w_gate, w_up, w_down)


def with_routes(tokens, expert_ids, gate_weights):
    parts, rest = [], gate_weights
    for _ in range(3):
        part = lax.reduce_precision(rest, exponent_bits=8, mantissa_bits=7)
        parts.append(part.astype(jnp.bfloat16))
        rest = rest - part
    route = jnp.concatenate([expert_ids.astype(jnp.bfloat16)] + parts, axis=1)
    fill = -route.shape[1] % LANES
    return jnp.concatenate([tokens, jnp.pad(route, ((0, 0), (0, fill)))], axis=1)


def shards(tokens, expert_ids, gate_weights, w_gate, w_up, w_down):
    width = tokens.shape[1]
    me = lax.axis_index("expert").astype(jnp.int32).reshape(1)
    rows = lax.all_gather(
        with_routes(tokens, expert_ids, gate_weights), "expert", axis=0, tiled=True
    )
    partial = run_expert(rows, me, width, expert_ids.shape[1], w_gate, w_up, w_down)
    return lax.psum_scatter(partial, "expert", scatter_dimension=0, tiled=True)


def solution(mesh):
    placed = (
        P(("groups", "expert"), None),
        P(("groups", "expert"), None),
        P(("groups", "expert"), None),
        P("expert", None, None),
        P("expert", None, None),
        P("expert", None, None),
    )
    return jax.shard_map(
        shards, mesh=mesh, in_specs=placed, out_specs=P(("groups", "expert"), None), check_vma=False
    )
```

```python
import functools

import jax
import jax.numpy as jnp
from jax import lax
from jax.experimental import pallas as pl
from jax.experimental.pallas import tpu as pltpu
from jax.sharding import PartitionSpec as P

LANES = 128


def even_split(size, most):
    part = most
    while size % part:
        part //= 2
    return part


def chip_ring(chips):
    across = max(d for d in range(1, chips + 1) if chips % d == 0 and d * d <= chips)
    down = chips // across
    if across == 1 or down % 2:
        return list(range(chips))
    ring = []
    for row in range(down):
        columns = list(range(1, across))
        ring += [row * across + column for column in (columns if row % 2 == 0 else columns[::-1])]
    return [0] + ring + [row * across for row in range(down - 1, 0, -1)]


def ring_pairs(ring, way):
    count = len(ring)
    pairs = []
    for at, chip in enumerate(ring):
        for core in (0, 1):
            step = way if core == 0 else -way
            pairs.append((2 * chip + core, 2 * ring[(at + step) % count] + core))
    return pairs


def expert_kernel(blocks, experts, with_prior, width, top_count, ids_ref, *refs):
    row_refs, refs = refs[:blocks], refs[blocks:]
    weight_refs, refs = refs[: 3 * experts], refs[3 * experts :]
    prior_refs, refs = (refs[:blocks], refs[blocks:]) if with_prior else ((), refs)
    out_refs, refs = refs[:blocks], refs[blocks:]
    gate_buf, up_buf, down_buf, rows_buf, total, sems = refs
    chunk = gate_buf.shape[2]
    chunks = gate_buf.shape[0] // experts
    block_rows = row_refs[0].shape[0]

    def copies(expert, part):
        gate_ref, up_ref, down_ref = weight_refs[3 * expert : 3 * expert + 3]
        slot = expert * chunks + part
        piece = pl.ds(part * chunk, chunk)
        return (
            pltpu.make_async_copy(gate_ref.at[0, :, piece], gate_buf.at[slot], sems.at[0, slot]),
            pltpu.make_async_copy(up_ref.at[0, :, piece], up_buf.at[slot], sems.at[1, slot]),
            pltpu.make_async_copy(down_ref.at[0, piece, :], down_buf.at[slot], sems.at[2, slot]),
        )

    for expert in range(experts):
        for part in range(chunks):
            for copy in copies(expert, part):
                copy.start()
    for at in range(blocks):
        span = pl.ds(at * block_rows, block_rows)
        rows_buf[span, :] = row_refs[at][...]
        if with_prior:
            total[span, :] = prior_refs[at][...]
        else:
            total[span, :] = jnp.zeros((block_rows, width), jnp.float32)
    for expert in range(experts):
        route = rows_buf[:, width:].astype(jnp.float32)
        chosen = (route[:, :top_count] == ids_ref[expert].astype(jnp.float32)).astype(jnp.float32)
        weight = sum(route[:, top_count * part : top_count * (part + 1)] for part in (1, 2, 3))
        scale = jnp.sum(chosen * weight, axis=1, keepdims=True)
        for part in range(chunks):
            slot = expert * chunks + part
            gate_copy, up_copy, down_copy = copies(expert, part)
            rows = rows_buf[:, :width]
            gate_copy.wait()
            gate_part = jnp.dot(rows, gate_buf[slot], preferred_element_type=jnp.float32)
            up_copy.wait()
            up_part = jnp.dot(rows, up_buf[slot], preferred_element_type=jnp.float32)
            hidden = (gate_part / (1.0 + jnp.exp(-gate_part)) * up_part).astype(jnp.bfloat16)
            down_copy.wait()
            result = jnp.dot(hidden, down_buf[slot], preferred_element_type=jnp.float32)
            total[...] += result * scale
    for at in range(blocks):
        out_refs[at][...] = total[pl.ds(at * block_rows, block_rows), :].astype(out_refs[at].dtype)


def run_experts(row_blocks, ids, weights, width, top_count, prior=None, out_dtype=jnp.bfloat16):
    blocks, experts = len(row_blocks), len(weights)
    block_rows, row_width = row_blocks[0].shape
    hidden_width = weights[0][0].shape[2]
    chunk = even_split(hidden_width, 256)
    slots = experts * (hidden_width // chunk)
    total = blocks * block_rows
    in_vmem = pl.BlockSpec(memory_space=pltpu.VMEM)
    in_hbm = pl.BlockSpec(memory_space=pltpu.HBM)
    prior = prior or []
    return pl.pallas_call(
        functools.partial(expert_kernel, blocks, experts, bool(prior), width, top_count),
        out_shape=[jax.ShapeDtypeStruct((block_rows, width), out_dtype)] * blocks,
        in_specs=[pl.BlockSpec(memory_space=pltpu.SMEM)]
        + [in_vmem] * blocks
        + [in_hbm] * (3 * experts)
        + [in_vmem] * len(prior),
        out_specs=[in_vmem] * blocks,
        scratch_shapes=[
            pltpu.VMEM((slots, width, chunk), jnp.bfloat16),
            pltpu.VMEM((slots, width, chunk), jnp.bfloat16),
            pltpu.VMEM((slots, chunk, width), jnp.bfloat16),
            pltpu.VMEM((total, row_width), jnp.bfloat16),
            pltpu.VMEM((total, width), jnp.float32),
            pltpu.SemaphoreType.DMA((3, slots)),
        ],
        compiler_params=pltpu.CompilerParams(vmem_limit_bytes=48 * 1024 * 1024),
        cost_estimate=pl.CostEstimate(
            flops=6 * total * width * hidden_width * experts,
            bytes_accessed=2 * (3 * width * hidden_width * experts + 2 * total * width),
            transcendentals=total * hidden_width * experts,
        ),
    )(ids, *row_blocks, *(array for weight in weights for array in weight), *prior)


def with_routes(tokens, expert_ids, gate_weights):
    parts, rest = [], gate_weights
    for _ in range(3):
        part = lax.reduce_precision(rest, exponent_bits=8, mantissa_bits=7)
        parts.append(part.astype(jnp.bfloat16))
        rest = rest - part
    route = jnp.concatenate([expert_ids.astype(jnp.bfloat16)] + parts, axis=1)
    fill = -route.shape[1] % LANES
    return jnp.concatenate([tokens, jnp.pad(route, ((0, 0), (0, fill)))], axis=1)


def add_rounded(*terms):
    return sum(term.astype(jnp.float32) for term in terms).astype(jnp.bfloat16)


def shards(tokens, expert_ids, gate_weights, w_gate, w_up, w_down):
    width, top_count = tokens.shape[1], expert_ids.shape[1]
    devices = lax.axis_size("expert")
    ring = chip_ring(devices // 2)
    ahead, back = ring_pairs(ring, 1), ring_pairs(ring, -1)
    siblings = [(at, at ^ 1) for at in range(devices)]
    long_steps = len(ring) // 2
    short_steps = (len(ring) - 1) // 2
    me = lax.axis_index("expert").astype(jnp.int32)
    own = (w_gate, w_up, w_down)

    first = with_routes(tokens, expert_ids, gate_weights)
    long_rows, short_rows = [first], [first]
    for step in range(long_steps):
        long_rows.append(lax.ppermute(long_rows[-1], "expert", ahead))
        if step < short_steps:
            short_rows.append(lax.ppermute(short_rows[-1], "expert", back))
        if step == 0:
            other = tuple(lax.ppermute(array, "expert", siblings) for array in own)

    run = functools.partial(run_experts, width=width, top_count=top_count)
    one, both = me.reshape(1), jnp.stack([me, me ^ 1])
    near = max(long_steps - 2, 0)
    early = [first]
    sums = []
    for step in range(1, near + 1):
        group = [long_rows[step], short_rows[step]]
        if step == 1:
            group = [first] + group
        sums.append(run(group, one, [own], out_dtype=jnp.float32))
    partial = []
    pending_rows, pending_sums = [], []
    for step in range(1, near + 1):
        pending_rows += ([first] if step == 1 else []) + [long_rows[step], short_rows[step]]
        pending_sums += sums[step - 1]
        if len(pending_rows) >= 5 or step == near:
            partial += run(pending_rows, me[None] ^ 1, [other], prior=pending_sums)
            pending_rows, pending_sums = [], []
    late = [] if near else [first]
    for step in range(near + 1, long_steps + 1):
        late.append(long_rows[step])
        if step <= short_steps:
            late.append(short_rows[step])
    partial += run(late, both, [own, other])

    mine, partial = partial[0], partial[1:]
    long_parts, short_parts = [], []
    for step in range(1, long_steps + 1):
        long_parts.append(partial.pop(0))
        if step <= short_steps:
            short_parts.append(partial.pop(0))

    def gather_home(parts, pairs):
        moving = parts[-1]
        for step in range(len(parts) - 1, 0, -1):
            moving = add_rounded(lax.ppermute(moving, "expert", pairs), parts[step - 1])
        return lax.ppermute(moving, "expert", pairs)

    arrived = []
    if long_parts:
        arrived.append(gather_home(long_parts, back))
    if short_parts:
        arrived.append(gather_home(short_parts, ahead))
    return add_rounded(mine, *arrived)


def solution(mesh):
    placed = (
        P(("groups", "expert"), None),
        P(("groups", "expert"), None),
        P(("groups", "expert"), None),
        P("expert", None, None),
        P("expert", None, None),
        P("expert", None, None),
    )
    return jax.shard_map(
        shards, mesh=mesh, in_specs=placed, out_specs=P(("groups", "expert"), None), check_vma=False
    )
```

```python
import functools

import jax
import jax.numpy as jnp
from jax import lax
from jax.experimental import pallas as pl
from jax.experimental.pallas import tpu as pltpu
from jax.sharding import PartitionSpec as P

LANES = 128
IN_VMEM = pl.BlockSpec(memory_space=pltpu.VMEM)
IN_SMEM = pl.BlockSpec(memory_space=pltpu.SMEM)


def chip_ring(chips):
    across = max(d for d in range(1, chips + 1) if chips % d == 0 and d * d <= chips)
    down = chips // across
    if across == 1 or down % 2:
        return list(range(chips))
    ring = []
    for row in range(down):
        columns = list(range(1, across))
        ring += [row * across + column for column in (columns if row % 2 == 0 else columns[::-1])]
    return [0] + ring + [row * across for row in range(down - 1, 0, -1)]


def ring_pairs(ring, way):
    count = len(ring)
    pairs = []
    for at, chip in enumerate(ring):
        for core in (0, 1):
            step = way if core == 0 else -way
            pairs.append((2 * chip + core, 2 * ring[(at + step) % count] + core))
    return pairs


def pack_kernel(tokens_ref, ids_ref, gates_ref, *out_refs):
    width = tokens_ref.shape[1]
    rest = gates_ref[...]
    parts = [ids_ref[...].astype(jnp.float32)]
    for _ in range(3):
        parts.append(rest.astype(jnp.bfloat16).astype(jnp.float32))
        rest = rest - parts[-1]
    stacked = jnp.concatenate(parts, axis=0)
    shape = (stacked.shape[0], out_refs[0].shape[1] - width)
    unit = lax.broadcasted_iota(jnp.int32, shape, 0) == lax.broadcasted_iota(jnp.int32, shape, 1)
    route = lax.dot_general(
        stacked.astype(jnp.bfloat16),
        unit.astype(jnp.float32).astype(jnp.bfloat16),
        (((0,), (0,)), ((), ())),
        preferred_element_type=jnp.float32,
    ).astype(jnp.bfloat16)
    rows = out_refs[0].shape[0]
    for at, out_ref in enumerate(out_refs):
        out_ref[:, :width] = tokens_ref[pl.ds(at * rows, rows), :]
        out_ref[:, width:] = route[at * rows : (at + 1) * rows, :]


def pack_rows(tokens, expert_ids, gate_weights, pieces):
    rows, width = tokens.shape
    extra = -(-4 * expert_ids.shape[1] // LANES) * LANES
    piece = jax.ShapeDtypeStruct((rows // pieces, width + extra), jnp.bfloat16)
    return pl.pallas_call(
        pack_kernel,
        out_shape=[piece] * pieces,
        in_specs=[IN_VMEM] * 3,
        out_specs=[IN_VMEM] * pieces,
    )(tokens, expert_ids.T, gate_weights.T)


def expert_kernel(blocks, experts, with_prior, width, top_count, ids_ref, *refs):
    row_refs, refs = refs[:blocks], refs[blocks:]
    weight_refs, refs = refs[: 3 * experts], refs[3 * experts :]
    prior_refs, refs = (refs[:blocks], refs[blocks:]) if with_prior else ((), refs)
    out_refs, (rows_buf,) = refs[:blocks], refs[blocks:]
    block_rows = row_refs[0].shape[0]
    for at in range(blocks):
        rows_buf[pl.ds(at * block_rows, block_rows), :] = row_refs[at][...]
    route = rows_buf[:, width:].astype(jnp.float32)
    weight = sum(route[:, top_count * part : top_count * (part + 1)] for part in (1, 2, 3))
    rows = rows_buf[:, :width]
    for expert in range(experts):
        gate_ref, up_ref, down_ref = weight_refs[3 * expert : 3 * expert + 3]
        chosen = (route[:, :top_count] == ids_ref[expert].astype(jnp.float32)).astype(jnp.float32)
        scale = jnp.sum(chosen * weight, axis=1, keepdims=True)
        gate_part = jnp.dot(rows, gate_ref[0], preferred_element_type=jnp.float32)
        up_part = jnp.dot(rows, up_ref[0], preferred_element_type=jnp.float32)
        hidden = (gate_part / (1.0 + jnp.exp(-gate_part)) * up_part).astype(jnp.bfloat16)
        result = jnp.dot(hidden, down_ref[0], preferred_element_type=jnp.float32) * scale
        for at in range(blocks):
            value = result[at * block_rows : (at + 1) * block_rows]
            if expert:
                value += out_refs[at][...]
            elif with_prior:
                value += prior_refs[at][...]
            out_refs[at][...] = value


def run_experts(row_blocks, ids, weights, width, top_count, prior=()):
    blocks, experts = len(row_blocks), len(weights)
    block_rows, row_width = row_blocks[0].shape
    hidden_width = weights[0][0].shape[2]
    total = blocks * block_rows
    return pl.pallas_call(
        functools.partial(expert_kernel, blocks, experts, bool(prior), width, top_count),
        out_shape=[jax.ShapeDtypeStruct((block_rows, width), jnp.float32)] * blocks,
        in_specs=[IN_SMEM] + [IN_VMEM] * (blocks + 3 * experts + len(prior)),
        out_specs=[IN_VMEM] * blocks,
        scratch_shapes=[pltpu.VMEM((total, row_width), jnp.bfloat16)],
        compiler_params=pltpu.CompilerParams(vmem_limit_bytes=16 * 1024 * 1024),
        cost_estimate=pl.CostEstimate(
            flops=6 * total * width * hidden_width * experts,
            bytes_accessed=2 * (3 * width * hidden_width * experts + 2 * total * width),
            transcendentals=total * hidden_width * experts,
        ),
    )(ids, *row_blocks, *(array for weight in weights for array in weight), *prior)


def add_rounded(*terms):
    return sum(term.astype(jnp.float32) for term in terms).astype(jnp.bfloat16)


def shards(tokens, expert_ids, gate_weights, w_gate, w_up, w_down):
    width, top_count = tokens.shape[1], expert_ids.shape[1]
    devices = lax.axis_size("expert")
    ring = chip_ring(devices // 2)
    ways = (ring_pairs(ring, 1), ring_pairs(ring, -1))
    siblings = [(at, at ^ 1) for at in range(devices)]
    hops = len(ring) // 2
    last_is_shared = len(ring) % 2 == 0
    me = lax.axis_index("expert").astype(jnp.int32)
    one, other_one = me.reshape(1), (me ^ 1).reshape(1)
    own = (w_gate, w_up, w_down)
    run = functools.partial(run_experts, width=width, top_count=top_count)

    def chains_at(hop):
        if hop == 0:
            return [(0, 0), (1, 1)]
        if hop == hops and last_is_shared:
            return [(0, 0), (1, 1)]
        return [(way, piece) for way in (0, 1) for piece in (0, 1)]

    first = pack_rows(tokens, expert_ids, gate_weights, 2)
    rows = [{(0, 0): first[0], (0, 1): first[1], (1, 0): first[0], (1, 1): first[1]}]
    partial = []
    other = None
    for hop in range(1, hops + 1):
        moved = {
            chain: lax.ppermute(rows[-1][chain], "expert", ways[chain[0]])
            for chain in chains_at(hop)
        }
        if other is None:
            other = tuple(lax.ppermute(array, "expert", siblings) for array in own)
        keys = chains_at(hop - 1)
        results = run([rows[-1][key] for key in keys], one, [own])
        arrived, results = lax.optimization_barrier((moved, results))
        rows.append(arrived)
        partial.append(dict(zip(keys, results)))
    keys = chains_at(hops)
    late = [rows[-1][key] for key in keys]
    if hops:
        both = jnp.concatenate([one, other_one])
        results = run(late, both, [own, other])
    else:
        other = tuple(lax.ppermute(array, "expert", siblings) for array in own)
        results = run(late, jnp.concatenate([one, other_one]), [own, other])
    partial.append(dict(zip(keys, results)))

    moving = {key: value.astype(jnp.bfloat16) for key, value in partial[hops].items()}
    for hop in range(hops, 0, -1):
        moved = {
            chain: lax.ppermute(value, "expert", ways[1 - chain[0]])
            for chain, value in moving.items()
        }
        keys = chains_at(hop - 1)
        results = run(
            [rows[hop - 1][key] for key in keys],
            other_one,
            [other],
            prior=[partial[hop - 1][key] for key in keys],
        )
        moved, results = lax.optimization_barrier((moved, results))
        totals = dict(zip(keys, results))
        if hop == 1:
            pieces = [
                add_rounded(
                    totals[(piece, piece)],
                    *(value for chain, value in moved.items() if chain[1] == piece),
                )
                for piece in (0, 1)
            ]
            return jnp.concatenate(pieces, axis=0)
        moving = {
            key: add_rounded(totals[key], *([moved[key]] if key in moved else []))
            for key in keys
        }
    pieces = [value.astype(jnp.bfloat16) for value in partial[0].values()]
    return jnp.concatenate(pieces, axis=0)


def solution(mesh):
    placed = (
        P(("groups", "expert"), None),
        P(("groups", "expert"), None),
        P(("groups", "expert"), None),
        P("expert", None, None),
        P("expert", None, None),
        P("expert", None, None),
    )
    return jax.shard_map(
        shards, mesh=mesh, in_specs=placed, out_specs=P(("groups", "expert"), None), check_vma=False
    )
```

```python
import functools

import jax
import jax.numpy as jnp
from jax import lax
from jax.experimental import pallas as pl
from jax.experimental.pallas import tpu as pltpu
from jax.sharding import PartitionSpec as P

LANES = 128
IN_VMEM = pl.BlockSpec(memory_space=pltpu.VMEM)
IN_SMEM = pl.BlockSpec(memory_space=pltpu.SMEM)
IN_HBM = pl.BlockSpec(memory_space=pltpu.HBM)
DEPTH_STEP = 512
HIDDEN_STEP = 256
IN_FLIGHT = 3


def in_hbm(array):
    return pltpu.with_memory_space_constraint(array, pltpu.HBM)


def even_split(size, most):
    part = most
    while size % part:
        part //= 2
    return part


def chip_ring(chips):
    across = max(d for d in range(1, chips + 1) if chips % d == 0 and d * d <= chips)
    down = chips // across
    if across == 1 or down % 2:
        return list(range(chips))
    ring = []
    for row in range(down):
        columns = list(range(1, across))
        ring += [row * across + column for column in (columns if row % 2 == 0 else columns[::-1])]
    return [0] + ring + [row * across for row in range(down - 1, 0, -1)]


def ring_pairs(ring, way):
    count = len(ring)
    pairs = []
    for at, chip in enumerate(ring):
        for core in (0, 1):
            step = way if core == 0 else -way
            pairs.append((2 * chip + core, 2 * ring[(at + step) % count] + core))
    return pairs


def pack_kernel(tokens_ref, ids_ref, gates_ref, out_ref):
    width = tokens_ref.shape[1]
    rest = gates_ref[...]
    parts = [ids_ref[...].astype(jnp.float32)]
    for _ in range(3):
        parts.append(rest.astype(jnp.bfloat16).astype(jnp.float32))
        rest = rest - parts[-1]
    stacked = jnp.concatenate(parts, axis=0)
    shape = (stacked.shape[0], out_ref.shape[1] - width)
    unit = lax.broadcasted_iota(jnp.int32, shape, 0) == lax.broadcasted_iota(jnp.int32, shape, 1)
    route = lax.dot_general(
        stacked.astype(jnp.bfloat16),
        unit.astype(jnp.float32).astype(jnp.bfloat16),
        (((0,), (0,)), ((), ())),
        preferred_element_type=jnp.float32,
    )
    out_ref[:, :width] = tokens_ref[...]
    out_ref[:, width:] = route.astype(jnp.bfloat16)


def pack_rows(tokens, expert_ids, gate_weights):
    rows, width = tokens.shape
    extra = -(-4 * expert_ids.shape[1] // LANES) * LANES
    return pl.pallas_call(
        pack_kernel,
        out_shape=jax.ShapeDtypeStruct((rows, width + extra), jnp.bfloat16),
        in_specs=[IN_VMEM] * 3,
        out_specs=IN_VMEM,
    )(tokens, expert_ids.T, gate_weights.T)


def expert_kernel(blocks, experts, with_prior, width, top_count, ids_ref, *refs):
    row_refs, refs = refs[:blocks], refs[blocks:]
    weight_refs, refs = refs[: 3 * experts], refs[3 * experts :]
    prior_refs, refs = (refs[:blocks], refs[blocks:]) if with_prior else ((), refs)
    out_refs, refs = refs[:blocks], refs[blocks:]
    gate_buf, up_buf, down_buf, rows_buf, gate_part, up_part, total, sems = refs
    block_rows = row_refs[0].shape[0]
    hidden_width = gate_buf.shape[2]
    deep = even_split(width, DEPTH_STEP)
    wide = even_split(hidden_width, HIDDEN_STEP)
    stages = []
    for expert in range(experts):
        stages += [(expert, True, pl.ds(at, deep)) for at in range(0, width, deep)]
        stages += [(expert, False, pl.ds(at, wide)) for at in range(0, hidden_width, wide)]

    def copies(at):
        expert, is_input, span = stages[at]
        gate_ref, up_ref, down_ref = weight_refs[3 * expert : 3 * expert + 3]
        pairs = [(down_ref, down_buf)]
        if is_input:
            pairs = [(gate_ref, gate_buf), (up_ref, up_buf)]
        return [
            pltpu.make_async_copy(ref.at[0, span, :], buf.at[expert, span, :], sems.at[side, at])
            for side, (ref, buf) in enumerate(pairs)
        ]

    for at in range(min(IN_FLIGHT, len(stages))):
        for copy in copies(at):
            copy.start()
    for at in range(blocks):
        span = pl.ds(at * block_rows, block_rows)
        rows_buf[span, :] = row_refs[at][...]
        if with_prior:
            total[span, :] = prior_refs[at][...]
        else:
            total[span, :] = jnp.zeros((block_rows, width), jnp.float32)
    route = rows_buf[:, width:].astype(jnp.float32)
    weight = sum(route[:, top_count * part : top_count * (part + 1)] for part in (1, 2, 3))
    for at, (expert, is_input, span) in enumerate(stages):
        for copy in copies(at):
            copy.wait()
        if at + IN_FLIGHT < len(stages):
            for copy in copies(at + IN_FLIGHT):
                copy.start()
        if is_input:
            piece = rows_buf[:, span]
            gate_now = jnp.dot(piece, gate_buf[expert, span, :], preferred_element_type=jnp.float32)
            up_now = jnp.dot(piece, up_buf[expert, span, :], preferred_element_type=jnp.float32)
            if span.start == 0:
                gate_part[...] = gate_now
                up_part[...] = up_now
            else:
                gate_part[...] += gate_now
                up_part[...] += up_now
        else:
            expert_id = ids_ref[expert].astype(jnp.float32)
            chosen = (route[:, :top_count] == expert_id).astype(jnp.float32)
            scale = jnp.sum(chosen * weight, axis=1, keepdims=True)
            gate_now = gate_part[:, span]
            hidden = gate_now / (1.0 + jnp.exp(-gate_now)) * up_part[:, span]
            result = jnp.dot(
                hidden.astype(jnp.bfloat16),
                down_buf[expert, span, :],
                preferred_element_type=jnp.float32,
            )
            total[...] += result * scale
    for at in range(blocks):
        out_refs[at][...] = total[pl.ds(at * block_rows, block_rows), :]


def run_experts(row_blocks, ids, weights, width, top_count, prior=()):
    blocks, experts = len(row_blocks), len(weights)
    block_rows, row_width = row_blocks[0].shape
    hidden_width = weights[0][0].shape[2]
    total = blocks * block_rows
    stages = experts * (
        width // even_split(width, DEPTH_STEP) + hidden_width // even_split(hidden_width, HIDDEN_STEP)
    )
    return pl.pallas_call(
        functools.partial(expert_kernel, blocks, experts, bool(prior), width, top_count),
        out_shape=[jax.ShapeDtypeStruct((block_rows, width), jnp.float32)] * blocks,
        in_specs=[IN_SMEM]
        + [IN_VMEM] * blocks
        + [IN_HBM] * (3 * experts)
        + [IN_VMEM] * len(prior),
        out_specs=[IN_VMEM] * blocks,
        scratch_shapes=[
            pltpu.VMEM((experts, width, hidden_width), jnp.bfloat16),
            pltpu.VMEM((experts, width, hidden_width), jnp.bfloat16),
            pltpu.VMEM((experts, hidden_width, width), jnp.bfloat16),
            pltpu.VMEM((total, row_width), jnp.bfloat16),
            pltpu.VMEM((total, hidden_width), jnp.float32),
            pltpu.VMEM((total, hidden_width), jnp.float32),
            pltpu.VMEM((total, width), jnp.float32),
            pltpu.SemaphoreType.DMA((2, stages)),
        ],
        compiler_params=pltpu.CompilerParams(vmem_limit_bytes=(16 + 12 * experts) * 1024 * 1024),
        cost_estimate=pl.CostEstimate(
            flops=6 * total * width * hidden_width * experts,
            bytes_accessed=2 * (3 * width * hidden_width * experts + 2 * total * width),
            transcendentals=total * hidden_width * experts,
        ),
    )(ids, *row_blocks, *(in_hbm(array) for weight in weights for array in weight), *prior)


def add_rounded(*terms):
    return sum(term.astype(jnp.float32) for term in terms).astype(jnp.bfloat16)


def half_of(block, way):
    half = block.shape[0] // 2
    return block[way * half : (way + 1) * half]


def widened(half, way, rows):
    below = way * half.shape[0]
    return jnp.pad(half, ((below, rows - half.shape[0] - below), (0, 0)))


def shards(tokens, expert_ids, gate_weights, w_gate, w_up, w_down):
    width, top_count = tokens.shape[1], expert_ids.shape[1]
    devices = lax.axis_size("expert")
    ring = chip_ring(devices // 2)
    ways = (ring_pairs(ring, 1), ring_pairs(ring, -1))
    siblings = [(at, at ^ 1) for at in range(devices)]
    hops = len(ring) // 2
    shared_end = len(ring) % 2 == 0
    me = lax.axis_index("expert").astype(jnp.int32)
    one, other_one = me.reshape(1), (me ^ 1).reshape(1)
    own = (w_gate, w_up, w_down)
    run = functools.partial(run_experts, width=width, top_count=top_count)

    first = pack_rows(tokens, expert_ids, gate_weights)
    first, ready = lax.optimization_barrier((first, own))
    other = tuple(lax.ppermute(array, "expert", siblings) for array in ready)

    rows, partial = [[first]], []
    for hop in range(1, hops + 1):
        moved = []
        for way in (0, 1):
            block = rows[-1][way % len(rows[-1])]
            if hop == hops and shared_end:
                block = half_of(block, way)
            moved.append(lax.ppermute(block, "expert", ways[way]))
        results = run(rows[-1], one, [own])
        moved, results = lax.optimization_barrier((moved, results))
        rows.append(moved)
        partial.append(results)
    partial.append(run(rows[hops], jnp.concatenate([one, other_one]), [own, other]))

    moving = [value.astype(jnp.bfloat16) for value in partial[hops]]
    for hop in range(hops, 0, -1):
        moved = [lax.ppermute(moving[way], "expert", ways[1 - way]) for way in (0, 1)]
        results = run(rows[hop - 1], other_one, [other], prior=partial[hop - 1])
        moved, results = lax.optimization_barrier((moved, results))
        if hop == hops and shared_end:
            moved = [widened(moved[way], way, tokens.shape[0]) for way in (0, 1)]
        if hop == 1:
            return add_rounded(results[0], *moved)
        moving = [add_rounded(results[way], moved[way]) for way in (0, 1)]
    return moving[0]


def solution(mesh):
    placed = (
        P(("groups", "expert"), None),
        P(("groups", "expert"), None),
        P(("groups", "expert"), None),
        P("expert", None, None),
        P("expert", None, None),
        P("expert", None, None),
    )
    return jax.shard_map(
        shards, mesh=mesh, in_specs=placed, out_specs=P(("groups", "expert"), None), check_vma=False
    )
```

```python
import functools

import jax
import jax.numpy as jnp
from jax import lax
from jax.experimental import pallas as pl
from jax.experimental.pallas import tpu as pltpu
from jax.sharding import PartitionSpec as P

LANES = 128
IN_VMEM = pl.BlockSpec(memory_space=pltpu.VMEM)
IN_SMEM = pl.BlockSpec(memory_space=pltpu.SMEM)
IN_HBM = pl.BlockSpec(memory_space=pltpu.HBM)
DEPTH_STEP = 512
HIDDEN_STEP = 256
IN_FLIGHT = 5
SCOPED_BYTES = 24 * 1024 * 1024
KEPT_BYTES = 32 * 1024 * 1024


def in_hbm(array):
    return pltpu.with_memory_space_constraint(array, pltpu.HBM)


def even_split(size, most):
    part = most
    while size % part:
        part //= 2
    return part


def chip_ring(chips):
    across = max(d for d in range(1, chips + 1) if chips % d == 0 and d * d <= chips)
    down = chips // across
    if across == 1 or down % 2:
        return list(range(chips))
    ring = []
    for row in range(down):
        columns = list(range(1, across))
        ring += [row * across + column for column in (columns if row % 2 == 0 else columns[::-1])]
    return [0] + ring + [row * across for row in range(down - 1, 0, -1)]


def ring_pairs(ring, way):
    count = len(ring)
    pairs = []
    for at, chip in enumerate(ring):
        for core in (0, 1):
            step = way if core == 0 else -way
            pairs.append((2 * chip + core, 2 * ring[(at + step) % count] + core))
    return pairs


def pack_kernel(tokens_ref, ids_ref, gates_ref, out_ref):
    width = tokens_ref.shape[1]
    rest = gates_ref[...]
    parts = [ids_ref[...].astype(jnp.float32)]
    for _ in range(3):
        parts.append(rest.astype(jnp.bfloat16).astype(jnp.float32))
        rest = rest - parts[-1]
    stacked = jnp.concatenate(parts, axis=0)
    shape = (stacked.shape[0], out_ref.shape[1] - width)
    unit = lax.broadcasted_iota(jnp.int32, shape, 0) == lax.broadcasted_iota(jnp.int32, shape, 1)
    route = lax.dot_general(
        stacked.astype(jnp.bfloat16),
        unit.astype(jnp.float32).astype(jnp.bfloat16),
        (((0,), (0,)), ((), ())),
        preferred_element_type=jnp.float32,
    )
    out_ref[:, :width] = tokens_ref[...]
    out_ref[:, width:] = route.astype(jnp.bfloat16)


def pack_rows(tokens, expert_ids, gate_weights, made):
    rows, width = tokens.shape
    extra = -(-4 * expert_ids.shape[1] // LANES) * LANES
    return pl.pallas_call(
        pack_kernel,
        out_shape=made((rows, width + extra), jnp.bfloat16),
        in_specs=[IN_VMEM] * 3,
        out_specs=IN_VMEM,
    )(tokens, expert_ids.T, gate_weights.T)


def expert_kernel(blocks, streamed, with_prior, width, top_count, ids_ref, *refs):
    experts = len(streamed)
    row_refs, refs = refs[:blocks], refs[blocks:]
    weight_refs, refs = refs[: 3 * experts], refs[3 * experts :]
    prior_refs, refs = (refs[:blocks], refs[blocks:]) if with_prior else ((), refs)
    out_refs, refs = refs[:blocks], refs[blocks:]
    kept_refs, (rows_buf, gate_part, up_part, total, sems) = refs[:-5], refs[-5:]
    block_rows = row_refs[0].shape[0]
    hidden_width = gate_part.shape[1]
    deep = even_split(width, DEPTH_STEP)
    wide = even_split(hidden_width, HIDDEN_STEP)
    stages = [(True, pl.ds(at, deep)) for at in range(0, width, deep)]
    stages += [(False, pl.ds(at, wide)) for at in range(0, hidden_width, wide)]
    coming = [weight_refs[3 * at : 3 * at + 3] for at in range(experts) if streamed[at]]

    def copies(at):
        is_input, span = stages[at]
        sides = (0, 1) if is_input else (2,)
        return [
            pltpu.make_async_copy(
                coming[0][side].at[0, span, :], kept_refs[side].at[0, span, :], sems.at[side, at]
            )
            for side in sides
        ]

    def start(at):
        if coming and at < len(stages):
            for copy in copies(at):
                copy.start()

    for at in range(IN_FLIGHT):
        start(at)
    for at in range(blocks):
        span = pl.ds(at * block_rows, block_rows)
        rows_buf[span, :] = row_refs[at][...]
        if with_prior:
            total[span, :] = prior_refs[at][...]
    route = rows_buf[:, width:].astype(jnp.float32)
    weight = sum(route[:, top_count * part : top_count * (part + 1)] for part in (1, 2, 3))
    empty = not with_prior

    def add(gate_now, up_now, down, scale, empty):
        hidden = gate_now / (1.0 + jnp.exp(-gate_now)) * up_now
        result = jnp.dot(hidden.astype(jnp.bfloat16), down, preferred_element_type=jnp.float32)
        if empty:
            total[...] = result * scale
        else:
            total[...] += result * scale

    for expert in range(experts):
        chosen = route[:, :top_count] == ids_ref[expert].astype(jnp.float32)
        scale = jnp.sum(chosen.astype(jnp.float32) * weight, axis=1, keepdims=True)
        if not streamed[expert]:
            gate_ref, up_ref, down_ref = weight_refs[3 * expert : 3 * expert + 3]
            rows = rows_buf[:, :width]
            gate_now = jnp.dot(rows, gate_ref[0], preferred_element_type=jnp.float32)
            up_now = jnp.dot(rows, up_ref[0], preferred_element_type=jnp.float32)
            add(gate_now, up_now, down_ref[0], scale, empty)
            empty = False
            continue
        for at, (is_input, span) in enumerate(stages):
            for copy in copies(at):
                copy.wait()
            start(at + IN_FLIGHT)
            if not is_input:
                add(gate_part[:, span], up_part[:, span], kept_refs[2][0, span, :], scale, empty)
                empty = False
                continue
            for side, part in ((0, gate_part), (1, up_part)):
                now = jnp.dot(
                    rows_buf[:, span], kept_refs[side][0, span, :], preferred_element_type=jnp.float32
                )
                if at == 0:
                    part[...] = now
                else:
                    part[...] += now
    for at in range(blocks):
        out_refs[at][...] = total[pl.ds(at * block_rows, block_rows), :]


def run_experts(made, top_count, row_blocks, ids, weights, streamed, prior=()):
    blocks, experts = len(row_blocks), len(weights)
    block_rows, row_width = row_blocks[0].shape
    _, width, hidden_width = weights[0][0].shape
    total = blocks * block_rows
    stages = width // even_split(width, DEPTH_STEP) + hidden_width // even_split(
        hidden_width, HIDDEN_STEP
    )
    kept = [array for weight, coming in zip(weights, streamed) if coming for array in weight]
    results = pl.pallas_call(
        functools.partial(expert_kernel, blocks, streamed, bool(prior), width, top_count),
        out_shape=[made((block_rows, width), jnp.float32)] * blocks
        + [made(array.shape, array.dtype) for array in kept],
        in_specs=[IN_SMEM]
        + [IN_VMEM] * blocks
        + [IN_HBM if coming else IN_VMEM for coming in streamed for _ in range(3)]
        + [IN_VMEM] * len(prior),
        out_specs=[IN_VMEM] * (blocks + len(kept)),
        scratch_shapes=[
            pltpu.VMEM((total, row_width), jnp.bfloat16),
            pltpu.VMEM((total, hidden_width), jnp.float32),
            pltpu.VMEM((total, hidden_width), jnp.float32),
            pltpu.VMEM((total, width), jnp.float32),
            pltpu.SemaphoreType.DMA((3, stages)),
        ],
        compiler_params=pltpu.CompilerParams(vmem_limit_bytes=SCOPED_BYTES),
        cost_estimate=pl.CostEstimate(
            flops=6 * total * width * hidden_width * experts,
            bytes_accessed=2 * (3 * width * hidden_width * experts + 2 * total * width),
            transcendentals=total * hidden_width * experts,
        ),
    )(
        ids,
        *(made.pin(block) for block in row_blocks),
        *(
            in_hbm(array) if coming else made.pin(array)
            for weight, coming in zip(weights, streamed)
            for array in weight
        ),
        *(made.pin(block) for block in prior),
    )
    return results[:blocks], tuple(results[blocks:])


class InVmem:
    def __call__(self, shape, dtype):
        return pltpu.VMEM(shape, dtype)

    def pin(self, array):
        return pltpu.with_memory_space_constraint(array, pltpu.VMEM)


class Anywhere:
    def __call__(self, shape, dtype):
        return jax.ShapeDtypeStruct(shape, dtype)

    def pin(self, array):
        return array


def add_rounded(*terms):
    return sum(term.astype(jnp.float32) for term in terms).astype(jnp.bfloat16)


def half_of(block, way):
    half = block.shape[0] // 2
    return block[way * half : (way + 1) * half]


def widened(half, way, rows):
    below = way * half.shape[0]
    return jnp.pad(half, ((below, rows - half.shape[0] - below), (0, 0)))


def shards(tokens, expert_ids, gate_weights, w_gate, w_up, w_down):
    local, width = tokens.shape
    top_count = expert_ids.shape[1]
    devices = lax.axis_size("expert")
    ring = chip_ring(devices // 2)
    ways = (ring_pairs(ring, 1), ring_pairs(ring, -1))
    siblings = [(at, at ^ 1) for at in range(devices)]
    hops = len(ring) // 2
    shared_end = len(ring) % 2 == 0
    own = (w_gate, w_up, w_down)
    weight_bytes = 2 * sum(array.size * array.dtype.itemsize for array in own)
    kept_bytes = weight_bytes + len(ring) * local * width * 6
    made = InVmem() if kept_bytes <= KEPT_BYTES else Anywhere()
    run = functools.partial(run_experts, made, top_count)
    me = lax.axis_index("expert").astype(jnp.int32)
    one, other_one = me.reshape(1), (me ^ 1).reshape(1)
    both = jnp.concatenate([one, other_one])
    after = lax.optimization_barrier

    first = pack_rows(tokens, expert_ids, gate_weights, made)
    first, ready = after((first, own))
    other = tuple(lax.ppermute(array, "expert", siblings) for array in ready)

    def outward(block, way, hop):
        if hop == hops and shared_end:
            block = half_of(block, way)
        return lax.ppermute(block, "expert", ways[way])

    rows = {(way, 0): first for way in (0, 1)}
    partial = {}
    for way in (0, 1):
        rows[way, 1] = outward(first, way, 1)
    (start_sum,), own = run([first], one, [own], (True,))
    rows[0, 1], start_sum = after((rows[0, 1], start_sum))
    for hop in range(2, hops + 1):
        rows[0, hop] = outward(rows[0, hop - 1], 0, hop)
        keys = [(0, hop - 1)] + [(1, hop - 2)] * (hop > 2)
        results, _ = run([rows[key] for key in keys], one, [own], (False,))
        rows[1, hop - 1], results = after((rows[1, hop - 1], results))
        partial.update(zip(keys, results))
        rows[1, hop] = outward(rows[1, hop - 1], 1, hop)
    if hops > 1:
        results, other = run([rows[1, hops - 1]], both, [own, other], (False, True))
    else:
        results, other = run([first], other_one, [other], (True,), prior=[start_sum])
        (start_sum,) = results
    partial[1, hops - 1] = results[0]
    (long_end,), _ = run([rows[0, hops]], both, [own, other], (False, False))
    rows[1, hops], long_end = after((rows[1, hops], long_end))
    (short_end,), _ = run([rows[1, hops]], both, [own, other], (False, False))

    def homeward(block, way):
        return lax.ppermute(block.astype(jnp.bfloat16), "expert", ways[1 - way])

    def met(block, way, hop):
        if hop == hops and shared_end:
            block = widened(block, way, local)
        return add_rounded(block, partial[way, hop - 1])

    moving = [homeward(long_end, 0), homeward(short_end, 1)]
    if hops > 1:
        (value,), _ = run([rows[0, hops - 1]], other_one, [other], (False,), [partial[0, hops - 1]])
        moving[0], partial[0, hops - 1] = after((moving[0], value))
    partial[0, 0] = start_sum
    for hop in range(hops, 1, -1):
        long_sum = met(moving[0], 0, hop)
        moving[0] = homeward(long_sum, 0)
        keys = [(0, hop - 2), (1, hop - 2)] if hop > 2 else [(0, 0)]
        prior, _ = after(([partial[key] for key in keys], long_sum))
        results, _ = run([rows[key] for key in keys], other_one, [other], (False,), prior)
        moving[1], results = after((moving[1], results))
        partial.update(zip(keys, results))
        moving[1] = homeward(met(moving[1], 1, hop), 1)
    start_sum = partial[0, 0]
    if hops == 1 and shared_end:
        moving = [widened(moving[way], way, local) for way in (0, 1)]
    return add_rounded(start_sum, *moving)


def solution(mesh):
    placed = (
        P(("groups", "expert"), None),
        P(("groups", "expert"), None),
        P(("groups", "expert"), None),
        P("expert", None, None),
        P("expert", None, None),
        P("expert", None, None),
    )
    return jax.shard_map(
        shards, mesh=mesh, in_specs=placed, out_specs=P(("groups", "expert"), None), check_vma=False
    )
```

```python
import functools

import jax
import jax.numpy as jnp
from jax import lax
from jax.experimental import pallas as pl
from jax.experimental.pallas import tpu as pltpu
from jax.sharding import PartitionSpec as P

LANES = 128
IN_VMEM = pl.BlockSpec(memory_space=pltpu.VMEM)
IN_HBM = pl.BlockSpec(memory_space=pltpu.HBM)
DEPTH_STEP = 512
HIDDEN_STEP = 256
IN_FLIGHT = 5
SCOPED_BYTES = 8 * 1024 * 1024
KEPT_BYTES = 32 * 1024 * 1024


def in_hbm(array):
    return pltpu.with_memory_space_constraint(array, pltpu.HBM)


def even_split(size, most):
    part = most
    while size % part:
        part //= 2
    return part


def chip_ring(chips):
    across = max(d for d in range(1, chips + 1) if chips % d == 0 and d * d <= chips)
    down = chips // across
    if across == 1 or down % 2:
        return list(range(chips))
    ring = []
    for row in range(down):
        columns = list(range(1, across))
        ring += [row * across + column for column in (columns if row % 2 == 0 else columns[::-1])]
    return [0] + ring + [row * across for row in range(down - 1, 0, -1)]


def ring_pairs(ring, way):
    count = len(ring)
    pairs = []
    for at, chip in enumerate(ring):
        for core in (0, 1):
            step = way if core == 0 else -way
            pairs.append((2 * chip + core, 2 * ring[(at + step) % count] + core))
    return pairs


def pack_kernel(tokens_ref, ids_ref, gates_ref, out_ref):
    width = tokens_ref.shape[1]
    rest = gates_ref[...]
    parts = [ids_ref[...].astype(jnp.float32)]
    for _ in range(3):
        parts.append(rest.astype(jnp.bfloat16).astype(jnp.float32))
        rest = rest - parts[-1]
    stacked = jnp.concatenate(parts, axis=0)
    shape = (stacked.shape[0], out_ref.shape[1] - width)
    unit = lax.broadcasted_iota(jnp.int32, shape, 0) == lax.broadcasted_iota(jnp.int32, shape, 1)
    route = lax.dot_general(
        stacked.astype(jnp.bfloat16),
        unit.astype(jnp.float32).astype(jnp.bfloat16),
        (((0,), (0,)), ((), ())),
        preferred_element_type=jnp.float32,
    )
    out_ref[:, :width] = tokens_ref[...]
    out_ref[:, width:] = route.astype(jnp.bfloat16)


def pack_rows(tokens, expert_ids, gate_weights, made):
    rows, width = tokens.shape
    extra = -(-4 * expert_ids.shape[1] // LANES) * LANES
    return pl.pallas_call(
        pack_kernel,
        out_shape=made((rows, width + extra), jnp.bfloat16),
        in_specs=[IN_VMEM] * 3,
        out_specs=IN_VMEM,
        compiler_params=pltpu.CompilerParams(vmem_limit_bytes=SCOPED_BYTES),
    )(tokens, expert_ids.T, gate_weights.T)


def expert_kernel(blocks, flips, streamed, with_prior, width, top_count, *refs):
    experts = len(streamed)
    me = lax.axis_index("expert")
    row_refs, refs = refs[:blocks], refs[blocks:]
    weight_refs, refs = refs[: 3 * experts], refs[3 * experts :]
    prior_refs, refs = (refs[:blocks], refs[blocks:]) if with_prior else ((), refs)
    out_refs, refs = refs[:blocks], refs[blocks:]
    kept_refs, (rows_buf, gate_part, up_part, total, sems) = refs[:-5], refs[-5:]
    block_rows = row_refs[0].shape[0]
    hidden_width = gate_part.shape[1]
    deep = even_split(width, DEPTH_STEP)
    wide = even_split(hidden_width, HIDDEN_STEP)
    stages = [(True, pl.ds(at, deep)) for at in range(0, width, deep)]
    stages += [(False, pl.ds(at, wide)) for at in range(0, hidden_width, wide)]
    coming = [weight_refs[3 * at : 3 * at + 3] for at in range(experts) if streamed[at]]

    def copies(at):
        is_input, span = stages[at]
        sides = (0, 1) if is_input else (2,)
        return [
            pltpu.make_async_copy(
                coming[0][side].at[0, span, :], kept_refs[side].at[0, span, :], sems.at[side, at]
            )
            for side in sides
        ]

    def start(at):
        if coming and at < len(stages):
            for copy in copies(at):
                copy.start()

    for at in range(IN_FLIGHT):
        start(at)
    for at in range(blocks):
        span = pl.ds(at * block_rows, block_rows)
        rows_buf[span, :] = row_refs[at][...]
        if with_prior:
            total[span, :] = prior_refs[at][...]
    route = rows_buf[:, width:].astype(jnp.float32)
    weight = sum(route[:, top_count * part : top_count * (part + 1)] for part in (1, 2, 3))
    empty = not with_prior

    def add(gate_now, up_now, down, scale, empty):
        hidden = gate_now / (1.0 + jnp.exp(-gate_now)) * up_now
        result = jnp.dot(hidden.astype(jnp.bfloat16), down, preferred_element_type=jnp.float32)
        if empty:
            total[...] = result * scale
        else:
            total[...] += result * scale

    for expert in range(experts):
        chosen = route[:, :top_count] == (me ^ flips[expert]).astype(jnp.float32)
        scale = jnp.sum(chosen.astype(jnp.float32) * weight, axis=1, keepdims=True)
        if not streamed[expert]:
            gate_ref, up_ref, down_ref = weight_refs[3 * expert : 3 * expert + 3]
            rows = rows_buf[:, :width]
            gate_now = jnp.dot(rows, gate_ref[0], preferred_element_type=jnp.float32)
            up_now = jnp.dot(rows, up_ref[0], preferred_element_type=jnp.float32)
            add(gate_now, up_now, down_ref[0], scale, empty)
            empty = False
            continue
        for at, (is_input, span) in enumerate(stages):
            for copy in copies(at):
                copy.wait()
            start(at + IN_FLIGHT)
            if not is_input:
                add(gate_part[:, span], up_part[:, span], kept_refs[2][0, span, :], scale, empty)
                empty = False
                continue
            for side, part in ((0, gate_part), (1, up_part)):
                now = jnp.dot(
                    rows_buf[:, span], kept_refs[side][0, span, :], preferred_element_type=jnp.float32
                )
                if at == 0:
                    part[...] = now
                else:
                    part[...] += now
    for at in range(blocks):
        out_refs[at][...] = total[pl.ds(at * block_rows, block_rows), :]


def run_experts(made, top_count, row_blocks, flips, weights, streamed, prior=()):
    blocks, experts = len(row_blocks), len(weights)
    block_rows, row_width = row_blocks[0].shape
    _, width, hidden_width = weights[0][0].shape
    total = blocks * block_rows
    stages = width // even_split(width, DEPTH_STEP) + hidden_width // even_split(
        hidden_width, HIDDEN_STEP
    )
    kept = [array for weight, coming in zip(weights, streamed) if coming for array in weight]
    results = pl.pallas_call(
        functools.partial(expert_kernel, blocks, flips, streamed, bool(prior), width, top_count),
        out_shape=[made((block_rows, width), jnp.float32)] * blocks
        + [made(array.shape, array.dtype) for array in kept],
        in_specs=[IN_VMEM] * blocks
        + [IN_HBM if coming else IN_VMEM for coming in streamed for _ in range(3)]
        + [IN_VMEM] * len(prior),
        out_specs=[IN_VMEM] * (blocks + len(kept)),
        scratch_shapes=[
            pltpu.VMEM((total, row_width), jnp.bfloat16),
            pltpu.VMEM((total, hidden_width), jnp.float32),
            pltpu.VMEM((total, hidden_width), jnp.float32),
            pltpu.VMEM((total, width), jnp.float32),
            pltpu.SemaphoreType.DMA((3, stages)),
        ],
        compiler_params=pltpu.CompilerParams(vmem_limit_bytes=SCOPED_BYTES),
        cost_estimate=pl.CostEstimate(
            flops=6 * total * width * hidden_width * experts,
            bytes_accessed=2 * (3 * width * hidden_width * experts + 2 * total * width),
            transcendentals=total * hidden_width * experts,
        ),
    )(
        *(made.pin(block) for block in row_blocks),
        *(
            in_hbm(array) if coming else made.pin(array)
            for weight, coming in zip(weights, streamed)
            for array in weight
        ),
        *(made.pin(block) for block in prior),
    )
    return results[:blocks], tuple(results[blocks:])


class InVmem:
    def __call__(self, shape, dtype):
        return pltpu.VMEM(shape, dtype)

    def pin(self, array):
        return pltpu.with_memory_space_constraint(array, pltpu.VMEM)


class Anywhere:
    def __call__(self, shape, dtype):
        return jax.ShapeDtypeStruct(shape, dtype)

    def pin(self, array):
        return array


def add_rounded(*terms):
    return sum(term.astype(jnp.float32) for term in terms).astype(jnp.bfloat16)


def half_of(block, way):
    half = block.shape[0] // 2
    return block[way * half : (way + 1) * half]


def widened(half, way, rows):
    below = way * half.shape[0]
    return jnp.pad(half, ((below, rows - half.shape[0] - below), (0, 0)))


def shards(tokens, expert_ids, gate_weights, w_gate, w_up, w_down):
    local, width = tokens.shape
    top_count = expert_ids.shape[1]
    devices = lax.axis_size("expert")
    ring = chip_ring(devices // 2)
    ways = (ring_pairs(ring, 1), ring_pairs(ring, -1))
    siblings = [(at, at ^ 1) for at in range(devices)]
    hops = len(ring) // 2
    shared_end = len(ring) % 2 == 0
    own = (w_gate, w_up, w_down)
    weight_bytes = 2 * sum(array.size * array.dtype.itemsize for array in own)
    kept_bytes = weight_bytes + len(ring) * local * width * 6
    made = InVmem() if kept_bytes <= KEPT_BYTES else Anywhere()
    run = functools.partial(run_experts, made, top_count)
    one, other_one, both = (0,), (1,), (0, 1)
    after = lax.optimization_barrier

    first = pack_rows(tokens, expert_ids, gate_weights, made)
    first, ready = after((first, own))
    other = tuple(lax.ppermute(array, "expert", siblings) for array in ready)

    def outward(block, way, hop):
        if hop == hops and shared_end:
            block = half_of(block, way)
        return lax.ppermute(block, "expert", ways[way])

    rows = {(way, 0): first for way in (0, 1)}
    partial = {}
    for way in (0, 1):
        rows[way, 1] = outward(first, way, 1)
    (start_sum,), own = run([first], one, [own], (True,))
    rows[0, 1], start_sum = after((rows[0, 1], start_sum))
    for hop in range(2, hops + 1):
        rows[0, hop] = outward(rows[0, hop - 1], 0, hop)
        keys = [(0, hop - 1)] + [(1, hop - 2)] * (hop > 2)
        results, _ = run([rows[key] for key in keys], one, [own], (False,))
        rows[1, hop - 1], results = after((rows[1, hop - 1], results))
        partial.update(zip(keys, results))
        rows[1, hop] = outward(rows[1, hop - 1], 1, hop)
    if hops > 1:
        results, _ = run([rows[1, hops - 1]], both, [own, other], (False, False))
    else:
        results, _ = run([first], other_one, [other], (False,), prior=[start_sum])
        (start_sum,) = results
    partial[1, hops - 1] = results[0]
    ends, _ = run([rows[0, hops], rows[1, hops]], both, [own, other], (False, False))

    def homeward(block, way):
        return lax.ppermute(block.astype(jnp.bfloat16), "expert", ways[1 - way])

    def met(block, way, hop):
        if hop == hops and shared_end:
            block = widened(block, way, local)
        return add_rounded(block, partial[way, hop - 1])

    partial[0, 0] = start_sum
    moving = [homeward(ends[0], 0), None]
    short_end = ends[1]
    if hops > 1:
        keys = [(0, hops - 1)] + [(0, 0)] * (hops == 2)
        prior, short_end = after(([partial[key] for key in keys], short_end))
        results, _ = run([rows[key] for key in keys], other_one, [other], (False,), prior)
        short_end, results = after((short_end, results))
        partial.update(zip(keys, results))
    moving[1] = homeward(short_end, 1)
    for hop in range(hops, 1, -1):
        long_sum = met(moving[0], 0, hop)
        moving[0] = homeward(long_sum, 0)
        if hop > 2:
            keys = [(0, hop - 2), (1, hop - 2)] + [(0, 0)] * (hop == 3)
            prior, _ = after(([partial[key] for key in keys], long_sum))
            results, _ = run([rows[key] for key in keys], other_one, [other], (False,), prior)
            moving[1], results = after((moving[1], results))
            partial.update(zip(keys, results))
        moving[1] = homeward(met(moving[1], 1, hop), 1)
    start_sum = partial[0, 0]
    if hops == 1 and shared_end:
        moving = [widened(moving[way], way, local) for way in (0, 1)]
    return add_rounded(start_sum, *moving)


def solution(mesh):
    placed = (
        P(("groups", "expert"), None),
        P(("groups", "expert"), None),
        P(("groups", "expert"), None),
        P("expert", None, None),
        P("expert", None, None),
        P("expert", None, None),
    )
    return jax.shard_map(
        shards, mesh=mesh, in_specs=placed, out_specs=P(("groups", "expert"), None), check_vma=False
    )
```

```python
import functools

import jax
import jax.numpy as jnp
from jax import lax
from jax.experimental import pallas as pl
from jax.experimental.pallas import tpu as pltpu
from jax.sharding import PartitionSpec as P

LANES = 128
IN_VMEM = pl.BlockSpec(memory_space=pltpu.VMEM)
IN_HBM = pl.BlockSpec(memory_space=pltpu.HBM)
DEPTH_STEP = 512
HIDDEN_STEP = 256
IN_FLIGHT = 5
SCOPED_BYTES = 8 * 1024 * 1024
KEPT_BYTES = 32 * 1024 * 1024


def in_hbm(array):
    return pltpu.with_memory_space_constraint(array, pltpu.HBM)


def even_split(size, most):
    part = most
    while size % part:
        part //= 2
    return part


def chip_ring(chips):
    across = max(d for d in range(1, chips + 1) if chips % d == 0 and d * d <= chips)
    down = chips // across
    if across == 1 or down % 2:
        return list(range(chips))
    ring = []
    for row in range(down):
        columns = list(range(1, across))
        ring += [row * across + column for column in (columns if row % 2 == 0 else columns[::-1])]
    return [0] + ring + [row * across for row in range(down - 1, 0, -1)]


def ring_pairs(ring, way):
    count = len(ring)
    pairs = []
    for at, chip in enumerate(ring):
        for core in (0, 1):
            step = way if core == at % 2 else -way
            pairs.append((2 * chip + core, 2 * ring[(at + step) % count] + 1 - core))
    return pairs


def pack_kernel(tokens_ref, ids_ref, gates_ref, out_ref, ids_buf, gates_buf, sems):
    width = tokens_ref.shape[1]
    copies = [
        pltpu.make_async_copy(ids_ref, ids_buf, sems.at[0]),
        pltpu.make_async_copy(gates_ref, gates_buf, sems.at[1]),
        pltpu.make_async_copy(tokens_ref, out_ref.at[:, pl.ds(0, width)], sems.at[2]),
    ]
    for copy in copies:
        copy.start()
    for copy in copies[:2]:
        copy.wait()
    rest = gates_buf[...]
    parts = [ids_buf[...].astype(jnp.float32)]
    for _ in range(3):
        parts.append(rest.astype(jnp.bfloat16).astype(jnp.float32))
        rest = rest - parts[-1]
    stacked = jnp.concatenate(parts, axis=0)
    shape = (stacked.shape[0], out_ref.shape[1] - width)
    unit = lax.broadcasted_iota(jnp.int32, shape, 0) == lax.broadcasted_iota(jnp.int32, shape, 1)
    route = lax.dot_general(
        stacked.astype(jnp.bfloat16),
        unit.astype(jnp.float32).astype(jnp.bfloat16),
        (((0,), (0,)), ((), ())),
        preferred_element_type=jnp.float32,
    )
    out_ref[:, width:] = route.astype(jnp.bfloat16)
    copies[2].wait()


def pack_rows(tokens, expert_ids, gate_weights, made):
    rows, width = tokens.shape
    extra = -(-4 * expert_ids.shape[1] // LANES) * LANES
    ids, gates = expert_ids.T, gate_weights.T
    return pl.pallas_call(
        pack_kernel,
        out_shape=made((rows, width + extra), jnp.bfloat16),
        in_specs=[IN_HBM] * 3,
        out_specs=IN_VMEM,
        scratch_shapes=[
            pltpu.VMEM(ids.shape, ids.dtype),
            pltpu.VMEM(gates.shape, gates.dtype),
            pltpu.SemaphoreType.DMA((3,)),
        ],
        compiler_params=pltpu.CompilerParams(vmem_limit_bytes=SCOPED_BYTES),
    )(in_hbm(tokens), in_hbm(ids), in_hbm(gates))


def expert_kernel(blocks, flips, streamed, with_prior, width, top_count, *refs):
    experts = len(streamed)
    me = lax.axis_index("expert")
    row_refs, refs = refs[:blocks], refs[blocks:]
    weight_refs, refs = refs[: 3 * experts], refs[3 * experts :]
    prior_refs, refs = (refs[:blocks], refs[blocks:]) if with_prior else ((), refs)
    out_refs, refs = refs[:blocks], refs[blocks:]
    kept_refs, (rows_buf, gate_part, up_part, total, sems) = refs[:-5], refs[-5:]
    block_rows = row_refs[0].shape[0]
    hidden_width = gate_part.shape[1]
    deep = even_split(width, DEPTH_STEP)
    wide = even_split(hidden_width, HIDDEN_STEP)
    stages = [(True, pl.ds(at, deep)) for at in range(0, width, deep)]
    stages += [(False, pl.ds(at, wide)) for at in range(0, hidden_width, wide)]
    coming = [weight_refs[3 * at : 3 * at + 3] for at in range(experts) if streamed[at]]

    def copies(at):
        is_input, span = stages[at]
        sides = (0, 1) if is_input else (2,)
        return [
            pltpu.make_async_copy(
                coming[0][side].at[0, span, :], kept_refs[side].at[0, span, :], sems.at[side, at]
            )
            for side in sides
        ]

    def start(at):
        if coming and at < len(stages):
            for copy in copies(at):
                copy.start()

    for at in range(IN_FLIGHT):
        start(at)
    for at in range(blocks):
        span = pl.ds(at * block_rows, block_rows)
        rows_buf[span, :] = row_refs[at][...]
        if with_prior:
            total[span, :] = prior_refs[at][...]
    route = rows_buf[:, width:].astype(jnp.float32)
    weight = sum(route[:, top_count * part : top_count * (part + 1)] for part in (1, 2, 3))
    empty = not with_prior

    def add(gate_now, up_now, down, scale, empty):
        hidden = gate_now / (1.0 + jnp.exp(-gate_now)) * up_now
        result = jnp.dot(hidden.astype(jnp.bfloat16), down, preferred_element_type=jnp.float32)
        if empty:
            total[...] = result * scale
        else:
            total[...] += result * scale

    for expert in range(experts):
        chosen = route[:, :top_count] == (me ^ flips[expert]).astype(jnp.float32)
        scale = jnp.sum(chosen.astype(jnp.float32) * weight, axis=1, keepdims=True)
        if not streamed[expert]:
            gate_ref, up_ref, down_ref = weight_refs[3 * expert : 3 * expert + 3]
            rows = rows_buf[:, :width]
            gate_now = jnp.dot(rows, gate_ref[0], preferred_element_type=jnp.float32)
            up_now = jnp.dot(rows, up_ref[0], preferred_element_type=jnp.float32)
            add(gate_now, up_now, down_ref[0], scale, empty)
            empty = False
            continue
        for at, (is_input, span) in enumerate(stages):
            for copy in copies(at):
                copy.wait()
            start(at + IN_FLIGHT)
            if not is_input:
                add(gate_part[:, span], up_part[:, span], kept_refs[2][0, span, :], scale, empty)
                empty = False
                continue
            for side, part in ((0, gate_part), (1, up_part)):
                now = jnp.dot(
                    rows_buf[:, span], kept_refs[side][0, span, :], preferred_element_type=jnp.float32
                )
                if at == 0:
                    part[...] = now
                else:
                    part[...] += now
    for at in range(blocks):
        out_refs[at][...] = total[pl.ds(at * block_rows, block_rows), :]


def run_experts(made, top_count, row_blocks, flips, weights, streamed, prior=()):
    blocks, experts = len(row_blocks), len(weights)
    block_rows, row_width = row_blocks[0].shape
    _, width, hidden_width = weights[0][0].shape
    total = blocks * block_rows
    stages = width // even_split(width, DEPTH_STEP) + hidden_width // even_split(
        hidden_width, HIDDEN_STEP
    )
    kept = [array for weight, coming in zip(weights, streamed) if coming for array in weight]
    results = pl.pallas_call(
        functools.partial(expert_kernel, blocks, flips, streamed, bool(prior), width, top_count),
        out_shape=[made((block_rows, width), jnp.float32)] * blocks
        + [made(array.shape, array.dtype) for array in kept],
        in_specs=[IN_VMEM] * blocks
        + [IN_HBM if coming else IN_VMEM for coming in streamed for _ in range(3)]
        + [IN_VMEM] * len(prior),
        out_specs=[IN_VMEM] * (blocks + len(kept)),
        scratch_shapes=[
            pltpu.VMEM((total, row_width), jnp.bfloat16),
            pltpu.VMEM((total, hidden_width), jnp.float32),
            pltpu.VMEM((total, hidden_width), jnp.float32),
            pltpu.VMEM((total, width), jnp.float32),
            pltpu.SemaphoreType.DMA((3, stages)),
        ],
        compiler_params=pltpu.CompilerParams(vmem_limit_bytes=SCOPED_BYTES),
        cost_estimate=pl.CostEstimate(
            flops=6 * total * width * hidden_width * experts,
            bytes_accessed=2 * (3 * width * hidden_width * experts + 2 * total * width),
            transcendentals=total * hidden_width * experts,
        ),
    )(
        *(made.pin(block) for block in row_blocks),
        *(
            in_hbm(array) if coming else made.pin(array)
            for weight, coming in zip(weights, streamed)
            for array in weight
        ),
        *(made.pin(block) for block in prior),
    )
    return results[:blocks], tuple(results[blocks:])


class InVmem:
    def __call__(self, shape, dtype):
        return pltpu.VMEM(shape, dtype)

    def pin(self, array):
        return pltpu.with_memory_space_constraint(array, pltpu.VMEM)


class Anywhere:
    def __call__(self, shape, dtype):
        return jax.ShapeDtypeStruct(shape, dtype)

    def pin(self, array):
        return array


def add_rounded(*terms):
    return sum(term.astype(jnp.float32) for term in terms).astype(jnp.bfloat16)


def half_of(block, way):
    half = block.shape[0] // 2
    return block[way * half : (way + 1) * half]


def widened(half, way, rows):
    below = way * half.shape[0]
    return jnp.pad(half, ((below, rows - half.shape[0] - below), (0, 0)))


def shards(tokens, expert_ids, gate_weights, w_gate, w_up, w_down):
    local, width = tokens.shape
    top_count = expert_ids.shape[1]
    devices = lax.axis_size("expert")
    ring = chip_ring(devices // 2)
    ways = (ring_pairs(ring, 1), ring_pairs(ring, -1))
    siblings = [(at, at ^ 1) for at in range(devices)]
    hops = len(ring) // 2
    shared_end = len(ring) % 2 == 0
    own = (w_gate, w_up, w_down)
    weight_bytes = 2 * sum(array.size * array.dtype.itemsize for array in own)
    kept_bytes = weight_bytes + len(ring) * local * width * 6
    made = InVmem() if kept_bytes <= KEPT_BYTES else Anywhere()
    run = functools.partial(run_experts, made, top_count)
    one, other_one, both = (0,), (1,), (0, 1)
    after = lax.optimization_barrier

    first = pack_rows(tokens, expert_ids, gate_weights, made)
    first, ready = after((first, own))
    other = tuple(lax.ppermute(array, "expert", siblings) for array in ready)

    def outward(block, way, hop):
        if hop == hops and shared_end:
            block = half_of(block, way)
        return lax.ppermute(block, "expert", ways[way])

    rows = {(way, 0): first for way in (0, 1)}
    partial = {}
    for way in (0, 1):
        rows[way, 1] = outward(first, way, 1)
    (start_sum,), own = run([first], one, [own], (True,))
    rows[0, 1], start_sum = after((rows[0, 1], start_sum))
    for hop in range(2, hops + 1):
        rows[0, hop] = outward(rows[0, hop - 1], 0, hop)
        keys = [(0, hop - 1)] + [(1, hop - 2)] * (hop > 2)
        results, _ = run([rows[key] for key in keys], one, [own], (False,))
        rows[1, hop - 1], results = after((rows[1, hop - 1], results))
        partial.update(zip(keys, results))
        rows[1, hop] = outward(rows[1, hop - 1], 1, hop)
    if hops > 1:
        results, _ = run([rows[1, hops - 1]], both, [own, other], (False, False))
    else:
        results, _ = run([first], other_one, [other], (False,), prior=[start_sum])
        (start_sum,) = results
    partial[1, hops - 1] = results[0]
    ends, _ = run([rows[0, hops], rows[1, hops]], both, [own, other], (False, False))

    def homeward(block, way):
        return lax.ppermute(block.astype(jnp.bfloat16), "expert", ways[1 - way])

    def met(block, way, hop):
        if hop == hops and shared_end:
            block = widened(block, way, local)
        return add_rounded(block, partial[way, hop - 1])

    partial[0, 0] = start_sum
    moving = [homeward(ends[0], 0), None]
    short_end = ends[1]
    if hops > 1:
        keys = [(0, hops - 1)] + [(0, 0)] * (hops == 2)
        prior, short_end = after(([partial[key] for key in keys], short_end))
        results, _ = run([rows[key] for key in keys], other_one, [other], (False,), prior)
        short_end, results = after((short_end, results))
        partial.update(zip(keys, results))
    moving[1] = homeward(short_end, 1)
    for hop in range(hops, 1, -1):
        long_sum = met(moving[0], 0, hop)
        moving[0] = homeward(long_sum, 0)
        if hop > 2:
            keys = [(0, hop - 2), (1, hop - 2)] + [(0, 0)] * (hop == 3)
            prior, _ = after(([partial[key] for key in keys], long_sum))
            results, _ = run([rows[key] for key in keys], other_one, [other], (False,), prior)
            moving[1], results = after((moving[1], results))
            partial.update(zip(keys, results))
        moving[1] = homeward(met(moving[1], 1, hop), 1)
    start_sum = partial[0, 0]
    if hops == 1 and shared_end:
        moving = [widened(moving[way], way, local) for way in (0, 1)]
    return add_rounded(start_sum, *moving)


def solution(mesh):
    placed = (
        P(("groups", "expert"), None),
        P(("groups", "expert"), None),
        P(("groups", "expert"), None),
        P("expert", None, None),
        P("expert", None, None),
        P("expert", None, None),
    )
    return jax.shard_map(
        shards, mesh=mesh, in_specs=placed, out_specs=P(("groups", "expert"), None), check_vma=False
    )
```

```python
import functools

import jax
import jax.numpy as jnp
from jax import lax
from jax.experimental import pallas as pl
from jax.experimental.pallas import tpu as pltpu
from jax.sharding import PartitionSpec as P

LANES = 128
IN_VMEM = pl.BlockSpec(memory_space=pltpu.VMEM)
IN_HBM = pl.BlockSpec(memory_space=pltpu.HBM)
DEPTH_STEP = 512
HIDDEN_STEP = 256
IN_FLIGHT = 5
SCOPED_BYTES = 8 * 1024 * 1024
KEPT_BYTES = 32 * 1024 * 1024


def in_hbm(array):
    return pltpu.with_memory_space_constraint(array, pltpu.HBM)


def even_split(size, most):
    part = most
    while size % part:
        part //= 2
    return part


def chip_ring(chips):
    across = max(d for d in range(1, chips + 1) if chips % d == 0 and d * d <= chips)
    down = chips // across
    if across == 1 or down % 2:
        return list(range(chips))
    ring = []
    for row in range(down):
        columns = list(range(1, across))
        ring += [row * across + column for column in (columns if row % 2 == 0 else columns[::-1])]
    return [0] + ring + [row * across for row in range(down - 1, 0, -1)]


def ring_pairs(ring, way):
    count = len(ring)
    pairs = []
    for at, chip in enumerate(ring):
        for core in (0, 1):
            step = way if core == at % 2 else -way
            pairs.append((2 * chip + core, 2 * ring[(at + step) % count] + 1 - core))
    return pairs


def pack_kernel(tokens_ref, ids_ref, gates_ref, out_ref, ids_buf, gates_buf, sems):
    width = tokens_ref.shape[1]
    copies = [
        pltpu.make_async_copy(ids_ref, ids_buf, sems.at[0]),
        pltpu.make_async_copy(gates_ref, gates_buf, sems.at[1]),
        pltpu.make_async_copy(tokens_ref, out_ref.at[:, pl.ds(0, width)], sems.at[2]),
    ]
    for copy in copies:
        copy.start()
    for copy in copies[:2]:
        copy.wait()
    rest = gates_buf[...]
    parts = [ids_buf[...].astype(jnp.float32)]
    for _ in range(3):
        parts.append(rest.astype(jnp.bfloat16).astype(jnp.float32))
        rest = rest - parts[-1]
    stacked = jnp.concatenate(parts, axis=0)
    shape = (stacked.shape[0], out_ref.shape[1] - width)
    unit = lax.broadcasted_iota(jnp.int32, shape, 0) == lax.broadcasted_iota(jnp.int32, shape, 1)
    route = lax.dot_general(
        stacked.astype(jnp.bfloat16),
        unit.astype(jnp.float32).astype(jnp.bfloat16),
        (((0,), (0,)), ((), ())),
        preferred_element_type=jnp.float32,
    )
    out_ref[:, width:] = route.astype(jnp.bfloat16)
    copies[2].wait()


def pack_rows(tokens, expert_ids, gate_weights, made):
    rows, width = tokens.shape
    extra = -(-4 * expert_ids.shape[1] // LANES) * LANES
    ids, gates = expert_ids.T, gate_weights.T
    return pl.pallas_call(
        pack_kernel,
        out_shape=made((rows, width + extra), jnp.bfloat16),
        in_specs=[IN_HBM] * 3,
        out_specs=IN_VMEM,
        scratch_shapes=[
            pltpu.VMEM(ids.shape, ids.dtype),
            pltpu.VMEM(gates.shape, gates.dtype),
            pltpu.SemaphoreType.DMA((3,)),
        ],
        compiler_params=pltpu.CompilerParams(vmem_limit_bytes=SCOPED_BYTES),
    )(in_hbm(tokens), in_hbm(ids), in_hbm(gates))


def expert_kernel(blocks, flips, streamed, with_prior, width, top_count, *refs):
    experts = len(streamed)
    me = lax.axis_index("expert")
    row_refs, refs = refs[:blocks], refs[blocks:]
    weight_refs, refs = refs[: 3 * experts], refs[3 * experts :]
    prior_refs, refs = (refs[:blocks], refs[blocks:]) if with_prior else ((), refs)
    out_refs, refs = refs[:blocks], refs[blocks:]
    kept_refs, (rows_buf, gate_part, up_part, total, sems) = refs[:-5], refs[-5:]
    block_rows = row_refs[0].shape[0]
    hidden_width = gate_part.shape[1]
    deep = even_split(width, DEPTH_STEP)
    wide = even_split(hidden_width, HIDDEN_STEP)
    stages = [(True, pl.ds(at, deep)) for at in range(0, width, deep)]
    stages += [(False, pl.ds(at, wide)) for at in range(0, hidden_width, wide)]
    coming = [weight_refs[3 * at : 3 * at + 3] for at in range(experts) if streamed[at]]

    def copies(at):
        is_input, span = stages[at]
        sides = (0, 1) if is_input else (2,)
        return [
            pltpu.make_async_copy(
                coming[0][side].at[0, span, :], kept_refs[side].at[0, span, :], sems.at[side, at]
            )
            for side in sides
        ]

    def start(at):
        if coming and at < len(stages):
            for copy in copies(at):
                copy.start()

    for at in range(IN_FLIGHT):
        start(at)
    for at in range(blocks):
        span = pl.ds(at * block_rows, block_rows)
        rows_buf[span, :] = row_refs[at][...]
        if with_prior:
            total[span, :] = prior_refs[at][...]
    route = rows_buf[:, width:].astype(jnp.float32)
    weight = sum(route[:, top_count * part : top_count * (part + 1)] for part in (1, 2, 3))
    empty = not with_prior

    def add(gate_now, up_now, down, scale, empty):
        hidden = gate_now / (1.0 + jnp.exp(-gate_now)) * up_now
        result = jnp.dot(hidden.astype(jnp.bfloat16), down, preferred_element_type=jnp.float32)
        if empty:
            total[...] = result * scale
        else:
            total[...] += result * scale

    for expert in range(experts):
        chosen = route[:, :top_count] == (me ^ flips[expert]).astype(jnp.float32)
        scale = jnp.sum(chosen.astype(jnp.float32) * weight, axis=1, keepdims=True)
        if not streamed[expert]:
            gate_ref, up_ref, down_ref = weight_refs[3 * expert : 3 * expert + 3]
            rows = rows_buf[:, :width]
            gate_now = jnp.dot(rows, gate_ref[0], preferred_element_type=jnp.float32)
            up_now = jnp.dot(rows, up_ref[0], preferred_element_type=jnp.float32)
            add(gate_now, up_now, down_ref[0], scale, empty)
            empty = False
            continue
        for at, (is_input, span) in enumerate(stages):
            for copy in copies(at):
                copy.wait()
            start(at + IN_FLIGHT)
            if not is_input:
                add(gate_part[:, span], up_part[:, span], kept_refs[2][0, span, :], scale, empty)
                empty = False
                continue
            for side, part in ((0, gate_part), (1, up_part)):
                now = jnp.dot(
                    rows_buf[:, span], kept_refs[side][0, span, :], preferred_element_type=jnp.float32
                )
                if at == 0:
                    part[...] = now
                else:
                    part[...] += now
    for at in range(blocks):
        out_refs[at][...] = total[pl.ds(at * block_rows, block_rows), :]


def run_experts(made, top_count, row_blocks, flips, weights, streamed, prior=()):
    blocks, experts = len(row_blocks), len(weights)
    block_rows, row_width = row_blocks[0].shape
    _, width, hidden_width = weights[0][0].shape
    total = blocks * block_rows
    stages = width // even_split(width, DEPTH_STEP) + hidden_width // even_split(
        hidden_width, HIDDEN_STEP
    )
    kept = [array for weight, coming in zip(weights, streamed) if coming for array in weight]
    results = pl.pallas_call(
        functools.partial(expert_kernel, blocks, flips, streamed, bool(prior), width, top_count),
        out_shape=[made((block_rows, width), jnp.float32)] * blocks
        + [made(array.shape, array.dtype) for array in kept],
        in_specs=[IN_VMEM] * blocks
        + [IN_HBM if coming else IN_VMEM for coming in streamed for _ in range(3)]
        + [IN_VMEM] * len(prior),
        out_specs=[IN_VMEM] * (blocks + len(kept)),
        scratch_shapes=[
            pltpu.VMEM((total, row_width), jnp.bfloat16),
            pltpu.VMEM((total, hidden_width), jnp.float32),
            pltpu.VMEM((total, hidden_width), jnp.float32),
            pltpu.VMEM((total, width), jnp.float32),
            pltpu.SemaphoreType.DMA((3, stages)),
        ],
        compiler_params=pltpu.CompilerParams(vmem_limit_bytes=SCOPED_BYTES),
        cost_estimate=pl.CostEstimate(
            flops=6 * total * width * hidden_width * experts,
            bytes_accessed=2 * (3 * width * hidden_width * experts + 2 * total * width),
            transcendentals=total * hidden_width * experts,
        ),
    )(
        *(made.pin(block) for block in row_blocks),
        *(
            in_hbm(array) if coming else made.pin(array)
            for weight, coming in zip(weights, streamed)
            for array in weight
        ),
        *(made.pin(block) for block in prior),
    )
    return results[:blocks], tuple(results[blocks:])


class InVmem:
    def __call__(self, shape, dtype):
        return pltpu.VMEM(shape, dtype)

    def pin(self, array):
        return pltpu.with_memory_space_constraint(array, pltpu.VMEM)


class Anywhere:
    def __call__(self, shape, dtype):
        return jax.ShapeDtypeStruct(shape, dtype)

    def pin(self, array):
        return array


def add_rounded(*terms):
    return sum(term.astype(jnp.float32) for term in terms).astype(jnp.bfloat16)


def shards(tokens, expert_ids, gate_weights, w_gate, w_up, w_down):
    local, width = tokens.shape
    top_count = expert_ids.shape[1]
    devices = lax.axis_size("expert")
    ring = chip_ring(devices // 2)
    ways = (ring_pairs(ring, 1), ring_pairs(ring, -1))
    siblings = [(at, at ^ 1) for at in range(devices)]
    hops = (len(ring) // 2, (len(ring) - 1) // 2)
    own = (w_gate, w_up, w_down)
    weight_bytes = 2 * sum(array.size * array.dtype.itemsize for array in own)
    kept_bytes = weight_bytes + len(ring) * local * width * 6
    made = InVmem() if kept_bytes <= KEPT_BYTES else Anywhere()
    run = functools.partial(run_experts, made, top_count)
    after = lax.optimization_barrier

    def outward(block, way):
        return lax.ppermute(block, "expert", ways[way])

    def homeward(block, way):
        return lax.ppermute(block, "expert", ways[1 - way])

    first = pack_rows(tokens, expert_ids, gate_weights, made)
    first, ready = after((first, own))
    other = tuple(lax.ppermute(array, "expert", siblings) for array in ready)

    rows = {(0, 0): first}
    partial = {}
    if hops[0]:
        rows[0, 1] = outward(first, 0)
    (partial[0, 0],), own = run([first], (0,), [own], (True,))
    if hops[1]:
        later, partial[0, 0] = after((first, partial[0, 0]))
        rows[1, 1] = outward(later, 1)
    if hops[0]:
        rows[0, 1], partial[0, 0] = after((rows[0, 1], partial[0, 0]))
    for hop in range(2, hops[0] + 1):
        rows[0, hop] = outward(rows[0, hop - 1], 0)
        keys = [(0, hop - 1)] + [(1, hop - 2)] * (hop > 2)
        results, _ = run([rows[key] for key in keys], (0,), [own], (False,))
        rows[1, hop - 1], results = after((rows[1, hop - 1], results))
        partial.update(zip(keys, results))
        if hop <= hops[1]:
            rows[1, hop] = outward(rows[1, hop - 1], 1)
    keys = [key for key in rows if key not in partial]
    if keys:
        results, _ = run([rows[key] for key in keys], (0, 1), [own, other], (False, False))
        partial.update(zip(keys, results))

    def sibling_sums(keys, prior):
        results, _ = run([rows[key] for key in keys], (1,), [other], (False,), prior)
        return results

    if hops[0] < 2:
        partial[0, 0] = sibling_sums([(0, 0)], [partial[0, 0]])[0]
    arrived = [None, None]
    level = list(hops)
    while level[0]:
        values = [None, None]
        values[0] = add_rounded(partial[0, level[0]], *[x for x in arrived[:1] if x is not None])
        arrived[0] = homeward(values[0], 0)
        keys = [(way, at - 1) for way, at in enumerate(level) if at > 1]
        keys = [key for key in keys if key in partial and key != (1, hops[0] - 1)]
        keys += [(0, 0)] * (level[0] == 2)
        waiting = arrived[1] if arrived[1] is not None else partial.get((1, level[1]))
        if keys:
            prior, _ = after(([partial[key] for key in keys], values[0]))
            waiting, results = after((waiting, sibling_sums(keys, prior)))
            partial.update(zip(keys, results))
        if level[1]:
            values[1] = add_rounded(*([waiting] if arrived[1] is None else [waiting, partial[1, level[1]]]))
            arrived[1] = homeward(values[1], 1)
        elif arrived[1] is not None:
            arrived[1] = waiting
        level = [max(at - 1, 0) for at in level]
    return add_rounded(partial[0, 0], *[value for value in arrived if value is not None])


def solution(mesh):
    placed = (
        P(("groups", "expert"), None),
        P(("groups", "expert"), None),
        P(("groups", "expert"), None),
        P("expert", None, None),
        P("expert", None, None),
        P("expert", None, None),
    )
    return jax.shard_map(
        shards, mesh=mesh, in_specs=placed, out_specs=P(("groups", "expert"), None), check_vma=False
    )
```

```python
import functools

import jax
import jax.numpy as jnp
from jax import lax
from jax.experimental import pallas as pl
from jax.experimental.pallas import tpu as pltpu
from jax.sharding import PartitionSpec as P

LANES = 128
IN_VMEM = pl.BlockSpec(memory_space=pltpu.VMEM)
IN_HBM = pl.BlockSpec(memory_space=pltpu.HBM)
DEPTH_STEP = 512
HIDDEN_STEP = 256
SCOPED_BYTES = 8 * 1024 * 1024
KEPT_BYTES = 32 * 1024 * 1024


def in_hbm(array):
    return pltpu.with_memory_space_constraint(array, pltpu.HBM)


def even_split(size, most):
    part = most
    while size % part:
        part //= 2
    return part


def chip_ring(chips):
    across = max(d for d in range(1, chips + 1) if chips % d == 0 and d * d <= chips)
    down = chips // across
    if across == 1 or down % 2:
        return list(range(chips))
    ring = []
    for row in range(down):
        columns = list(range(1, across))
        ring += [row * across + column for column in (columns if row % 2 == 0 else columns[::-1])]
    return [0] + ring + [row * across for row in range(down - 1, 0, -1)]


def ring_pairs(ring, way):
    count = len(ring)
    pairs = []
    for at, chip in enumerate(ring):
        for core in (0, 1):
            step = way if core == at % 2 else -way
            pairs.append((2 * chip + core, 2 * ring[(at + step) % count] + 1 - core))
    return pairs


def pack_kernel(tokens_ref, ids_ref, gates_ref, out_ref, ids_buf, gates_buf, sems):
    width = tokens_ref.shape[1]
    copies = [
        pltpu.make_async_copy(ids_ref, ids_buf, sems.at[0]),
        pltpu.make_async_copy(gates_ref, gates_buf, sems.at[1]),
        pltpu.make_async_copy(tokens_ref, out_ref.at[:, pl.ds(0, width)], sems.at[2]),
    ]
    for copy in copies:
        copy.start()
    for copy in copies[:2]:
        copy.wait()
    rest = gates_buf[...]
    parts = [ids_buf[...].astype(jnp.float32)]
    for _ in range(3):
        parts.append(rest.astype(jnp.bfloat16).astype(jnp.float32))
        rest = rest - parts[-1]
    stacked = jnp.concatenate(parts, axis=0)
    shape = (stacked.shape[0], out_ref.shape[1] - width)
    unit = lax.broadcasted_iota(jnp.int32, shape, 0) == lax.broadcasted_iota(jnp.int32, shape, 1)
    route = lax.dot_general(
        stacked.astype(jnp.bfloat16),
        unit.astype(jnp.float32).astype(jnp.bfloat16),
        (((0,), (0,)), ((), ())),
        preferred_element_type=jnp.float32,
    )
    out_ref[:, width:] = route.astype(jnp.bfloat16)
    copies[2].wait()


def pack_rows(tokens, expert_ids, gate_weights, made):
    rows, width = tokens.shape
    extra = -(-4 * expert_ids.shape[1] // LANES) * LANES
    ids, gates = expert_ids.T, gate_weights.T
    return pl.pallas_call(
        pack_kernel,
        out_shape=made((rows, width + extra), jnp.bfloat16),
        in_specs=[IN_HBM] * 3,
        out_specs=IN_VMEM,
        scratch_shapes=[
            pltpu.VMEM(ids.shape, ids.dtype),
            pltpu.VMEM(gates.shape, gates.dtype),
            pltpu.SemaphoreType.DMA((3,)),
        ],
        compiler_params=pltpu.CompilerParams(vmem_limit_bytes=SCOPED_BYTES),
    )(in_hbm(tokens), in_hbm(ids), in_hbm(gates))


def row_scale(route, expert, top_count):
    route = route.astype(jnp.float32)
    chosen = (route[:, :top_count] == expert.astype(jnp.float32)).astype(jnp.float32)
    weight = sum(route[:, top_count * part : top_count * (part + 1)] for part in (1, 2, 3))
    return jnp.sum(chosen * weight, axis=1, keepdims=True)


def expert_kernel(blocks, flips, with_prior, top_count, *refs):
    row_refs, refs = refs[:blocks], refs[blocks:]
    weight_refs, refs = refs[: 3 * len(flips)], refs[3 * len(flips) :]
    prior_refs, refs = (refs[:blocks], refs[blocks:]) if with_prior else ((), refs)
    out_refs, (rows_buf, total) = refs[:blocks], refs[blocks:]
    block_rows, width = out_refs[0].shape
    me = lax.axis_index("expert")
    for at in range(blocks):
        span = pl.ds(at * block_rows, block_rows)
        rows_buf[span, :] = row_refs[at][...]
        if with_prior:
            total[span, :] = prior_refs[at][...]
    rows = rows_buf[:, :width]
    for at, flip in enumerate(flips):
        gate_ref, up_ref, down_ref = weight_refs[3 * at : 3 * at + 3]
        scale = row_scale(rows_buf[:, width:], me ^ flip, top_count)
        gate_part = jnp.dot(rows, gate_ref[0], preferred_element_type=jnp.float32)
        up_part = jnp.dot(rows, up_ref[0], preferred_element_type=jnp.float32)
        hidden = (gate_part / (1.0 + jnp.exp(-gate_part)) * up_part).astype(jnp.bfloat16)
        result = jnp.dot(hidden, down_ref[0], preferred_element_type=jnp.float32) * scale
        if at or with_prior:
            total[...] += result
        else:
            total[...] = result
    for at in range(blocks):
        out_refs[at][...] = total[pl.ds(at * block_rows, block_rows), :]


def run_experts(made, top_count, row_blocks, flips, weights, prior=()):
    blocks, experts = len(row_blocks), len(weights)
    block_rows, row_width = row_blocks[0].shape
    _, width, hidden_width = weights[0][0].shape
    total = blocks * block_rows
    return pl.pallas_call(
        functools.partial(expert_kernel, blocks, flips, bool(prior), top_count),
        out_shape=[made((block_rows, width), jnp.float32)] * blocks,
        in_specs=[IN_VMEM] * (blocks + 3 * experts + len(prior)),
        out_specs=[IN_VMEM] * blocks,
        scratch_shapes=[
            pltpu.VMEM((total, row_width), jnp.bfloat16),
            pltpu.VMEM((total, width), jnp.float32),
        ],
        compiler_params=pltpu.CompilerParams(vmem_limit_bytes=SCOPED_BYTES),
        cost_estimate=pl.CostEstimate(
            flops=6 * total * width * hidden_width * experts,
            bytes_accessed=2 * (3 * width * hidden_width * experts + 2 * total * width),
            transcendentals=total * hidden_width * experts,
        ),
    )(
        *(made.pin(block) for block in row_blocks),
        *(made.pin(array) for weight in weights for array in weight),
        *(made.pin(block) for block in prior),
    )


def first_kernel(rows_ref, gate_in, up_in, hidden_ref, gate_ref, up_ref, parts, sems):
    width = gate_ref.shape[1]
    deep = even_split(width, DEPTH_STEP)
    sides = ((gate_in, gate_ref), (up_in, up_ref))

    def copies(at):
        span = pl.ds(at * deep, deep)
        return [
            pltpu.make_async_copy(source.at[0, span, :], kept.at[0, span, :], sems.at[side, at])
            for side, (source, kept) in enumerate(sides)
        ]

    steps = width // deep
    for at in range(steps):
        for copy in copies(at):
            copy.start()
    for at in range(steps):
        for copy in copies(at):
            copy.wait()
        span = pl.ds(at * deep, deep)
        for side, (_, kept) in enumerate(sides):
            now = jnp.dot(rows_ref[:, span], kept[0, span, :], preferred_element_type=jnp.float32)
            if at == 0:
                parts[side] = now
            else:
                parts[side] += now
    gate_part, up_part = parts[0], parts[1]
    hidden_ref[...] = (gate_part / (1.0 + jnp.exp(-gate_part)) * up_part).astype(jnp.bfloat16)


def second_kernel(top_count, rows_ref, hidden_ref, down_in, out_ref, down_ref, sems):
    hidden_width, width = down_ref.shape[1:]
    wide = even_split(hidden_width, HIDDEN_STEP)

    def copy(at):
        span = pl.ds(at * wide, wide)
        return pltpu.make_async_copy(down_in.at[0, span, :], down_ref.at[0, span, :], sems.at[at])

    steps = hidden_width // wide
    for at in range(steps):
        copy(at).start()
    scale = row_scale(rows_ref[:, width:], lax.axis_index("expert"), top_count)
    for at in range(steps):
        copy(at).wait()
        span = pl.ds(at * wide, wide)
        now = jnp.dot(hidden_ref[:, span], down_ref[0, span, :], preferred_element_type=jnp.float32)
        if at == 0:
            out_ref[...] = now
        else:
            out_ref[...] += now
    out_ref[...] = out_ref[...] * scale


def take_inputs_in(made, block, gate, up):
    _, width, hidden_width = gate.shape
    rows = block.shape[0]
    hidden, gate, up = pl.pallas_call(
        first_kernel,
        out_shape=[made((rows, hidden_width), jnp.bfloat16)] + [made(gate.shape, gate.dtype)] * 2,
        in_specs=[IN_VMEM] + [IN_HBM] * 2,
        out_specs=[IN_VMEM] * 3,
        scratch_shapes=[
            pltpu.VMEM((2, rows, hidden_width), jnp.float32),
            pltpu.SemaphoreType.DMA((2, width // even_split(width, DEPTH_STEP))),
        ],
        compiler_params=pltpu.CompilerParams(vmem_limit_bytes=SCOPED_BYTES),
        cost_estimate=pl.CostEstimate(
            flops=4 * rows * width * hidden_width,
            bytes_accessed=4 * width * hidden_width,
            transcendentals=rows * hidden_width,
        ),
    )(made.pin(block), in_hbm(gate), in_hbm(up))
    return hidden, gate, up


def take_output_in(made, top_count, block, hidden, down):
    _, hidden_width, width = down.shape
    rows = block.shape[0]
    return pl.pallas_call(
        functools.partial(second_kernel, top_count),
        out_shape=[made((rows, width), jnp.float32), made(down.shape, down.dtype)],
        in_specs=[IN_VMEM] * 2 + [IN_HBM],
        out_specs=[IN_VMEM] * 2,
        scratch_shapes=[
            pltpu.SemaphoreType.DMA((hidden_width // even_split(hidden_width, HIDDEN_STEP),))
        ],
        compiler_params=pltpu.CompilerParams(vmem_limit_bytes=SCOPED_BYTES),
        cost_estimate=pl.CostEstimate(
            flops=2 * rows * width * hidden_width,
            bytes_accessed=2 * width * hidden_width,
            transcendentals=0,
        ),
    )(made.pin(block), made.pin(hidden), in_hbm(down))


class InVmem:
    def __call__(self, shape, dtype):
        return pltpu.VMEM(shape, dtype)

    def pin(self, array):
        return pltpu.with_memory_space_constraint(array, pltpu.VMEM)


class Anywhere:
    def __call__(self, shape, dtype):
        return jax.ShapeDtypeStruct(shape, dtype)

    def pin(self, array):
        return array


def add_rounded(*terms):
    return sum(term.astype(jnp.float32) for term in terms).astype(jnp.bfloat16)


def shards(tokens, expert_ids, gate_weights, w_gate, w_up, w_down):
    local, width = tokens.shape
    top_count = expert_ids.shape[1]
    devices = lax.axis_size("expert")
    ring = chip_ring(devices // 2)
    ways = (ring_pairs(ring, 1), ring_pairs(ring, -1))
    siblings = [(at, at ^ 1) for at in range(devices)]
    hops = (len(ring) // 2, (len(ring) - 1) // 2)
    own = (w_gate, w_up, w_down)
    weight_bytes = 2 * sum(array.size * array.dtype.itemsize for array in own)
    kept_bytes = weight_bytes + len(ring) * local * width * 6
    made = InVmem() if kept_bytes <= KEPT_BYTES else Anywhere()
    run = functools.partial(run_experts, made, top_count)
    after = lax.optimization_barrier

    def outward(block, way):
        return lax.ppermute(block, "expert", ways[way])

    def homeward(block, way):
        return lax.ppermute(block, "expert", ways[1 - way])

    first = pack_rows(tokens, expert_ids, gate_weights, made)
    first, ready = after((first, own))
    other = tuple(lax.ppermute(array, "expert", siblings) for array in ready)

    rows = {(0, 0): first}
    partial = {}
    if hops[0]:
        rows[0, 1] = outward(first, 0)
    hidden, gate, up = take_inputs_in(made, first, w_gate, w_up)
    if hops[1]:
        later, hidden = after((first, hidden))
        rows[1, 1] = outward(later, 1)
    partial[0, 0], down = take_output_in(made, top_count, first, hidden, w_down)
    own = (gate, up, down)
    if hops[0]:
        rows[0, 1], partial[0, 0] = after((rows[0, 1], partial[0, 0]))
    for hop in range(2, hops[0] + 1):
        rows[0, hop] = outward(rows[0, hop - 1], 0)
        keys = [(0, hop - 1)] + [(1, hop - 2)] * (hop > 2)
        results = run([rows[key] for key in keys], (0,), [own])
        rows[1, hop - 1], results = after((rows[1, hop - 1], results))
        partial.update(zip(keys, results))
        if hop <= hops[1]:
            rows[1, hop] = outward(rows[1, hop - 1], 1)
    keys = [key for key in rows if key not in partial]
    if keys:
        results = run([rows[key] for key in keys], (0, 1), [own, other])
        partial.update(zip(keys, results))

    def sibling_sums(keys, prior):
        return run([rows[key] for key in keys], (1,), [other], prior)

    if hops[0] < 2:
        partial[0, 0] = sibling_sums([(0, 0)], [partial[0, 0]])[0]
    arrived = [None, None]
    level = list(hops)
    while level[0]:
        values = [None, None]
        values[0] = add_rounded(partial[0, level[0]], *[x for x in arrived[:1] if x is not None])
        arrived[0] = homeward(values[0], 0)
        keys = [(way, at - 1) for way, at in enumerate(level) if at > 1]
        keys = [key for key in keys if key in partial and key != (1, hops[0] - 1)]
        keys += [(0, 0)] * (level[0] == 2)
        waiting = arrived[1] if arrived[1] is not None else partial.get((1, level[1]))
        if keys:
            prior, _ = after(([partial[key] for key in keys], values[0]))
            waiting, results = after((waiting, sibling_sums(keys, prior)))
            partial.update(zip(keys, results))
        if level[1]:
            values[1] = add_rounded(*([waiting] if arrived[1] is None else [waiting, partial[1, level[1]]]))
            arrived[1] = homeward(values[1], 1)
        elif arrived[1] is not None:
            arrived[1] = waiting
        level = [max(at - 1, 0) for at in level]
    return add_rounded(partial[0, 0], *[value for value in arrived if value is not None])


def solution(mesh):
    placed = (
        P(("groups", "expert"), None),
        P(("groups", "expert"), None),
        P(("groups", "expert"), None),
        P("expert", None, None),
        P("expert", None, None),
        P("expert", None, None),
    )
    return jax.shard_map(
        shards, mesh=mesh, in_specs=placed, out_specs=P(("groups", "expert"), None), check_vma=False
    )
```

```python
import functools

import jax
import jax.numpy as jnp
from jax import lax
from jax.experimental import pallas as pl
from jax.experimental.pallas import tpu as pltpu
from jax.sharding import PartitionSpec as P

LANES = 128
IN_VMEM = pl.BlockSpec(memory_space=pltpu.VMEM)
IN_HBM = pl.BlockSpec(memory_space=pltpu.HBM)
DEPTH_STEP = 512
HIDDEN_STEP = 256
SCOPED_BYTES = 8 * 1024 * 1024
KEPT_BYTES = 32 * 1024 * 1024


def in_hbm(array):
    return pltpu.with_memory_space_constraint(array, pltpu.HBM)


def even_split(size, most):
    part = most
    while size % part:
        part //= 2
    return part


def chip_ring(chips):
    across = max(d for d in range(1, chips + 1) if chips % d == 0 and d * d <= chips)
    down = chips // across
    if across == 1 or down % 2:
        return list(range(chips))
    ring = []
    for row in range(down):
        columns = list(range(1, across))
        ring += [row * across + column for column in (columns if row % 2 == 0 else columns[::-1])]
    return [0] + ring + [row * across for row in range(down - 1, 0, -1)]


def ring_pairs(ring, way):
    count = len(ring)
    pairs = []
    for at, chip in enumerate(ring):
        for core in (0, 1):
            step = way if core == at % 2 else -way
            pairs.append((2 * chip + core, 2 * ring[(at + step) % count] + 1 - core))
    return pairs


def pack_kernel(tokens_ref, ids_ref, gates_ref, out_ref, ids_buf, gates_buf, sems):
    width = tokens_ref.shape[1]
    copies = [
        pltpu.make_async_copy(ids_ref, ids_buf, sems.at[0]),
        pltpu.make_async_copy(gates_ref, gates_buf, sems.at[1]),
        pltpu.make_async_copy(tokens_ref, out_ref.at[:, pl.ds(0, width)], sems.at[2]),
    ]
    for copy in copies:
        copy.start()
    for copy in copies[:2]:
        copy.wait()
    rest = gates_buf[...]
    parts = [ids_buf[...].astype(jnp.float32)]
    for _ in range(3):
        parts.append(rest.astype(jnp.bfloat16).astype(jnp.float32))
        rest = rest - parts[-1]
    stacked = jnp.concatenate(parts, axis=0)
    shape = (stacked.shape[0], out_ref.shape[1] - width)
    unit = lax.broadcasted_iota(jnp.int32, shape, 0) == lax.broadcasted_iota(jnp.int32, shape, 1)
    route = lax.dot_general(
        stacked.astype(jnp.bfloat16),
        unit.astype(jnp.float32).astype(jnp.bfloat16),
        (((0,), (0,)), ((), ())),
        preferred_element_type=jnp.float32,
    )
    out_ref[:, width:] = route.astype(jnp.bfloat16)
    copies[2].wait()


def pack_rows(tokens, expert_ids, gate_weights, made):
    rows, width = tokens.shape
    extra = -(-4 * expert_ids.shape[1] // LANES) * LANES
    ids, gates = expert_ids.T, gate_weights.T
    return pl.pallas_call(
        pack_kernel,
        out_shape=made((rows, width + extra), jnp.bfloat16),
        in_specs=[IN_HBM] * 3,
        out_specs=IN_VMEM,
        scratch_shapes=[
            pltpu.VMEM(ids.shape, ids.dtype),
            pltpu.VMEM(gates.shape, gates.dtype),
            pltpu.SemaphoreType.DMA((3,)),
        ],
        compiler_params=pltpu.CompilerParams(vmem_limit_bytes=SCOPED_BYTES),
    )(in_hbm(tokens), in_hbm(ids), in_hbm(gates))


def row_scale(route, expert, top_count):
    route = route.astype(jnp.float32)
    chosen = (route[:, :top_count] == expert.astype(jnp.float32)).astype(jnp.float32)
    weight = sum(route[:, top_count * part : top_count * (part + 1)] for part in (1, 2, 3))
    return jnp.sum(chosen * weight, axis=1, keepdims=True)


def expert_kernel(blocks, flips, with_prior, top_count, *refs):
    row_refs, refs = refs[:blocks], refs[blocks:]
    weight_refs, refs = refs[: 3 * len(flips)], refs[3 * len(flips) :]
    prior_refs, refs = (refs[:blocks], refs[blocks:]) if with_prior else ((), refs)
    out_refs, (rows_buf, total) = refs[:blocks], refs[blocks:]
    block_rows, width = out_refs[0].shape
    me = lax.axis_index("expert")
    for at in range(blocks):
        span = pl.ds(at * block_rows, block_rows)
        rows_buf[span, :] = row_refs[at][...]
        if with_prior:
            total[span, :] = prior_refs[at][...]
    rows = rows_buf[:, :width]
    for at, flip in enumerate(flips):
        gate_ref, up_ref, down_ref = weight_refs[3 * at : 3 * at + 3]
        scale = row_scale(rows_buf[:, width:], me ^ flip, top_count)
        gate_part = jnp.dot(rows, gate_ref[0], preferred_element_type=jnp.float32)
        up_part = jnp.dot(rows, up_ref[0], preferred_element_type=jnp.float32)
        hidden = (gate_part / (1.0 + jnp.exp(-gate_part)) * up_part).astype(jnp.bfloat16)
        result = jnp.dot(hidden, down_ref[0], preferred_element_type=jnp.float32) * scale
        if at or with_prior:
            total[...] += result
        else:
            total[...] = result
    for at in range(blocks):
        out_refs[at][...] = total[pl.ds(at * block_rows, block_rows), :]


def run_experts(made, top_count, row_blocks, flips, weights, prior=()):
    blocks, experts = len(row_blocks), len(weights)
    block_rows, row_width = row_blocks[0].shape
    _, width, hidden_width = weights[0][0].shape
    total = blocks * block_rows
    return pl.pallas_call(
        functools.partial(expert_kernel, blocks, flips, bool(prior), top_count),
        out_shape=[made((block_rows, width), jnp.float32)] * blocks,
        in_specs=[IN_VMEM] * (blocks + 3 * experts + len(prior)),
        out_specs=[IN_VMEM] * blocks,
        scratch_shapes=[
            pltpu.VMEM((total, row_width), jnp.bfloat16),
            pltpu.VMEM((total, width), jnp.float32),
        ],
        compiler_params=pltpu.CompilerParams(vmem_limit_bytes=SCOPED_BYTES),
        cost_estimate=pl.CostEstimate(
            flops=6 * total * width * hidden_width * experts,
            bytes_accessed=2 * (3 * width * hidden_width * experts + 2 * total * width),
            transcendentals=total * hidden_width * experts,
        ),
    )(
        *(made.pin(block) for block in row_blocks),
        *(made.pin(array) for weight in weights for array in weight),
        *(made.pin(block) for block in prior),
    )


def first_kernel(rows_ref, gate_in, up_in, hidden_ref, gate_ref, up_ref, parts, sems):
    width = gate_ref.shape[1]
    deep = even_split(width, DEPTH_STEP)
    sides = ((gate_in, gate_ref), (up_in, up_ref))

    def copies(at):
        span = pl.ds(at * deep, deep)
        return [
            pltpu.make_async_copy(source.at[0, span, :], kept.at[0, span, :], sems.at[side, at])
            for side, (source, kept) in enumerate(sides)
        ]

    steps = width // deep
    for at in range(steps):
        for copy in copies(at):
            copy.start()
    for at in range(steps):
        for copy in copies(at):
            copy.wait()
        span = pl.ds(at * deep, deep)
        for side, (_, kept) in enumerate(sides):
            now = jnp.dot(rows_ref[:, span], kept[0, span, :], preferred_element_type=jnp.float32)
            if at == 0:
                parts[side] = now
            else:
                parts[side] += now
    gate_part, up_part = parts[0], parts[1]
    hidden_ref[...] = (gate_part / (1.0 + jnp.exp(-gate_part)) * up_part).astype(jnp.bfloat16)


def second_kernel(top_count, rows_ref, hidden_ref, down_in, out_ref, down_ref, sems):
    hidden_width, width = down_ref.shape[1:]
    wide = even_split(hidden_width, HIDDEN_STEP)

    def copy(at):
        span = pl.ds(at * wide, wide)
        return pltpu.make_async_copy(down_in.at[0, span, :], down_ref.at[0, span, :], sems.at[at])

    steps = hidden_width // wide
    for at in range(steps):
        copy(at).start()
    scale = row_scale(rows_ref[:, width:], lax.axis_index("expert"), top_count)
    for at in range(steps):
        copy(at).wait()
        span = pl.ds(at * wide, wide)
        now = jnp.dot(hidden_ref[:, span], down_ref[0, span, :], preferred_element_type=jnp.float32)
        if at == 0:
            out_ref[...] = now
        else:
            out_ref[...] += now
    out_ref[...] = out_ref[...] * scale


def take_inputs_in(made, block, gate, up):
    _, width, hidden_width = gate.shape
    rows = block.shape[0]
    hidden, gate, up = pl.pallas_call(
        first_kernel,
        out_shape=[made((rows, hidden_width), jnp.bfloat16)] + [made(gate.shape, gate.dtype)] * 2,
        in_specs=[IN_VMEM] + [IN_HBM] * 2,
        out_specs=[IN_VMEM] * 3,
        scratch_shapes=[
            pltpu.VMEM((2, rows, hidden_width), jnp.float32),
            pltpu.SemaphoreType.DMA((2, width // even_split(width, DEPTH_STEP))),
        ],
        compiler_params=pltpu.CompilerParams(vmem_limit_bytes=SCOPED_BYTES),
        cost_estimate=pl.CostEstimate(
            flops=4 * rows * width * hidden_width,
            bytes_accessed=4 * width * hidden_width,
            transcendentals=rows * hidden_width,
        ),
    )(made.pin(block), in_hbm(gate), in_hbm(up))
    return hidden, gate, up


def take_output_in(made, top_count, block, hidden, down):
    _, hidden_width, width = down.shape
    rows = block.shape[0]
    return pl.pallas_call(
        functools.partial(second_kernel, top_count),
        out_shape=[made((rows, width), jnp.float32), made(down.shape, down.dtype)],
        in_specs=[IN_VMEM] * 2 + [IN_HBM],
        out_specs=[IN_VMEM] * 2,
        scratch_shapes=[
            pltpu.SemaphoreType.DMA((hidden_width // even_split(hidden_width, HIDDEN_STEP),))
        ],
        compiler_params=pltpu.CompilerParams(vmem_limit_bytes=SCOPED_BYTES),
        cost_estimate=pl.CostEstimate(
            flops=2 * rows * width * hidden_width,
            bytes_accessed=2 * width * hidden_width,
            transcendentals=0,
        ),
    )(made.pin(block), made.pin(hidden), in_hbm(down))


class InVmem:
    def __call__(self, shape, dtype):
        return pltpu.VMEM(shape, dtype)

    def pin(self, array):
        return pltpu.with_memory_space_constraint(array, pltpu.VMEM)


class Anywhere:
    def __call__(self, shape, dtype):
        return jax.ShapeDtypeStruct(shape, dtype)

    def pin(self, array):
        return array


def add_rounded(*terms):
    return sum(term.astype(jnp.float32) for term in terms).astype(jnp.bfloat16)


def shards(tokens, expert_ids, gate_weights, w_gate, w_up, w_down):
    local, width = tokens.shape
    top_count = expert_ids.shape[1]
    devices = lax.axis_size("expert")
    ring = chip_ring(devices // 2)
    ways = (ring_pairs(ring, 1), ring_pairs(ring, -1))
    siblings = [(at, at ^ 1) for at in range(devices)]
    hops = (len(ring) // 2, (len(ring) - 1) // 2)
    own = (w_gate, w_up, w_down)
    weight_bytes = 2 * sum(array.size * array.dtype.itemsize for array in own)
    kept_bytes = weight_bytes + len(ring) * local * width * 6
    made = InVmem() if kept_bytes <= KEPT_BYTES else Anywhere()
    run = functools.partial(run_experts, made, top_count)
    after = lax.optimization_barrier

    def outward(block, way):
        return lax.ppermute(block, "expert", ways[way])

    def homeward(block, way):
        return lax.ppermute(block, "expert", ways[1 - way])

    first = pack_rows(tokens, expert_ids, gate_weights, made)
    first, ready = after((first, own))
    other = tuple(lax.ppermute(array, "expert", siblings) for array in ready)

    rows = {(0, 0): first}
    partial = {}
    if hops[0]:
        rows[0, 1] = outward(first, 0)
    hidden, gate, up = take_inputs_in(made, first, w_gate, w_up)
    if hops[1]:
        later, hidden = after((first, hidden))
        rows[1, 1] = outward(later, 1)
    partial[0, 0], down = take_output_in(made, top_count, first, hidden, w_down)
    own = (gate, up, down)
    if hops[0]:
        rows[0, 1], partial[0, 0] = after((rows[0, 1], partial[0, 0]))
    for hop in range(2, hops[0] + 1):
        rows[0, hop] = outward(rows[0, hop - 1], 0)
        keys = [(0, hop - 1)] + [(1, hop - 2)] * (hop > 2)
        results = [run([rows[key]], (0,), [own])[0] for key in keys]
        rows[1, hop - 1], results = after((rows[1, hop - 1], results))
        partial.update(zip(keys, results))
        if hop <= hops[1]:
            rows[1, hop] = outward(rows[1, hop - 1], 1)
    keys = [key for key in rows if key not in partial]
    if keys:
        results = run([rows[key] for key in keys], (0, 1), [own, other])
        partial.update(zip(keys, results))

    def sibling_sums(keys, prior):
        return [run([rows[key]], (1,), [other], [value])[0] for key, value in zip(keys, prior)]

    if hops[0] < 2:
        partial[0, 0] = sibling_sums([(0, 0)], [partial[0, 0]])[0]
    arrived = [None, None]
    level = list(hops)
    while level[0]:
        values = [None, None]
        values[0] = add_rounded(partial[0, level[0]], *[x for x in arrived[:1] if x is not None])
        arrived[0] = homeward(values[0], 0)
        keys = [(way, at - 1) for way, at in enumerate(level) if at > 1]
        keys = [key for key in keys if key in partial and key != (1, hops[0] - 1)]
        keys += [(0, 0)] * (level[0] == 2)
        waiting = arrived[1] if arrived[1] is not None else partial.get((1, level[1]))
        if keys:
            prior, _ = after(([partial[key] for key in keys], values[0]))
            waiting, results = after((waiting, sibling_sums(keys, prior)))
            partial.update(zip(keys, results))
        if level[1]:
            values[1] = add_rounded(*([waiting] if arrived[1] is None else [waiting, partial[1, level[1]]]))
            arrived[1] = homeward(values[1], 1)
        elif arrived[1] is not None:
            arrived[1] = waiting
        level = [max(at - 1, 0) for at in level]
    return add_rounded(partial[0, 0], *[value for value in arrived if value is not None])


def solution(mesh):
    placed = (
        P(("groups", "expert"), None),
        P(("groups", "expert"), None),
        P(("groups", "expert"), None),
        P("expert", None, None),
        P("expert", None, None),
        P("expert", None, None),
    )
    return jax.shard_map(
        shards, mesh=mesh, in_specs=placed, out_specs=P(("groups", "expert"), None), check_vma=False
    )
```

```python
import functools

import jax
import jax.numpy as jnp
from jax import lax
from jax.experimental import pallas as pl
from jax.experimental.pallas import tpu as pltpu
from jax.sharding import PartitionSpec as P

LANES = 128
IN_VMEM = pl.BlockSpec(memory_space=pltpu.VMEM)
IN_HBM = pl.BlockSpec(memory_space=pltpu.HBM)
DEPTH_STEP = 512
HIDDEN_STEP = 256
PASS_ROWS = 128
SCOPED_BYTES = 8 * 1024 * 1024
KEPT_BYTES = 32 * 1024 * 1024


def in_hbm(array):
    return pltpu.with_memory_space_constraint(array, pltpu.HBM)


def even_split(size, most):
    part = most
    while size % part:
        part //= 2
    return part


def chip_ring(chips):
    across = max(d for d in range(1, chips + 1) if chips % d == 0 and d * d <= chips)
    down = chips // across
    if across == 1 or down % 2:
        return list(range(chips))
    ring = []
    for row in range(down):
        columns = list(range(1, across))
        ring += [row * across + column for column in (columns if row % 2 == 0 else columns[::-1])]
    return [0] + ring + [row * across for row in range(down - 1, 0, -1)]


def ring_pairs(ring, way):
    count = len(ring)
    pairs = []
    for at, chip in enumerate(ring):
        for core in (0, 1):
            step = way if core == at % 2 else -way
            pairs.append((2 * chip + core, 2 * ring[(at + step) % count] + 1 - core))
    return pairs


def pack_kernel(tokens_ref, ids_ref, gates_ref, out_ref, ids_buf, gates_buf, sems):
    width = tokens_ref.shape[1]
    copies = [
        pltpu.make_async_copy(ids_ref, ids_buf, sems.at[0]),
        pltpu.make_async_copy(gates_ref, gates_buf, sems.at[1]),
        pltpu.make_async_copy(tokens_ref, out_ref.at[:, pl.ds(0, width)], sems.at[2]),
    ]
    for copy in copies:
        copy.start()
    for copy in copies[:2]:
        copy.wait()
    rest = gates_buf[...]
    parts = [ids_buf[...].astype(jnp.float32)]
    for _ in range(3):
        parts.append(rest.astype(jnp.bfloat16).astype(jnp.float32))
        rest = rest - parts[-1]
    stacked = jnp.concatenate(parts, axis=0)
    shape = (stacked.shape[0], out_ref.shape[1] - width)
    unit = lax.broadcasted_iota(jnp.int32, shape, 0) == lax.broadcasted_iota(jnp.int32, shape, 1)
    route = lax.dot_general(
        stacked.astype(jnp.bfloat16),
        unit.astype(jnp.float32).astype(jnp.bfloat16),
        (((0,), (0,)), ((), ())),
        preferred_element_type=jnp.float32,
    )
    out_ref[:, width:] = route.astype(jnp.bfloat16)
    copies[2].wait()


def pack_rows(tokens, expert_ids, gate_weights, made):
    rows, width = tokens.shape
    extra = -(-4 * expert_ids.shape[1] // LANES) * LANES
    ids, gates = expert_ids.T, gate_weights.T
    return pl.pallas_call(
        pack_kernel,
        out_shape=made((rows, width + extra), jnp.bfloat16),
        in_specs=[IN_HBM] * 3,
        out_specs=IN_VMEM,
        scratch_shapes=[
            pltpu.VMEM(ids.shape, ids.dtype),
            pltpu.VMEM(gates.shape, gates.dtype),
            pltpu.SemaphoreType.DMA((3,)),
        ],
        compiler_params=pltpu.CompilerParams(vmem_limit_bytes=SCOPED_BYTES),
    )(in_hbm(tokens), in_hbm(ids), in_hbm(gates))


def row_scale(route, expert, top_count):
    route = route.astype(jnp.float32)
    chosen = (route[:, :top_count] == expert.astype(jnp.float32)).astype(jnp.float32)
    weight = sum(route[:, top_count * part : top_count * (part + 1)] for part in (1, 2, 3))
    return jnp.sum(chosen * weight, axis=1, keepdims=True)


def expert_kernel(blocks, flips, with_prior, top_count, *refs):
    row_refs, refs = refs[:blocks], refs[blocks:]
    weight_refs, refs = refs[: 3 * len(flips)], refs[3 * len(flips) :]
    prior_refs, refs = (refs[:blocks], refs[blocks:]) if with_prior else ((), refs)
    out_refs, (rows_buf, total) = refs[:blocks], refs[blocks:]
    block_rows, width = out_refs[0].shape
    real = blocks * block_rows
    me = lax.axis_index("expert")
    for at in range(rows_buf.shape[0] // block_rows):
        rows_buf[pl.ds(at * block_rows, block_rows), :] = row_refs[at % blocks][...]
    for at in range(blocks if with_prior else 0):
        total[pl.ds(at * block_rows, block_rows), :] = prior_refs[at][...]
    rows = rows_buf[:, :width]
    for at, flip in enumerate(flips):
        gate_ref, up_ref, down_ref = weight_refs[3 * at : 3 * at + 3]
        scale = row_scale(rows_buf[:real, width:], me ^ flip, top_count)
        gate_part = jnp.dot(rows, gate_ref[0], preferred_element_type=jnp.float32)
        up_part = jnp.dot(rows, up_ref[0], preferred_element_type=jnp.float32)
        hidden = (gate_part / (1.0 + jnp.exp(-gate_part)) * up_part).astype(jnp.bfloat16)
        result = jnp.dot(hidden, down_ref[0], preferred_element_type=jnp.float32)[:real] * scale
        if at or with_prior:
            total[...] += result
        else:
            total[...] = result
    for at in range(blocks):
        out_refs[at][...] = total[pl.ds(at * block_rows, block_rows), :]


def run_experts(made, top_count, row_blocks, flips, weights, prior=()):
    blocks, experts = len(row_blocks), len(weights)
    block_rows, row_width = row_blocks[0].shape
    _, width, hidden_width = weights[0][0].shape
    total = blocks * block_rows
    padded = max(total, PASS_ROWS // block_rows * block_rows)
    return pl.pallas_call(
        functools.partial(expert_kernel, blocks, flips, bool(prior), top_count),
        out_shape=[made((block_rows, width), jnp.float32)] * blocks,
        in_specs=[IN_VMEM] * (blocks + 3 * experts + len(prior)),
        out_specs=[IN_VMEM] * blocks,
        scratch_shapes=[
            pltpu.VMEM((padded, row_width), jnp.bfloat16),
            pltpu.VMEM((total, width), jnp.float32),
        ],
        compiler_params=pltpu.CompilerParams(vmem_limit_bytes=SCOPED_BYTES),
        cost_estimate=pl.CostEstimate(
            flops=6 * total * width * hidden_width * experts,
            bytes_accessed=2 * (3 * width * hidden_width * experts + 2 * total * width),
            transcendentals=total * hidden_width * experts,
        ),
    )(
        *(made.pin(block) for block in row_blocks),
        *(made.pin(array) for weight in weights for array in weight),
        *(made.pin(block) for block in prior),
    )


def first_kernel(rows_ref, gate_in, up_in, hidden_ref, gate_ref, up_ref, parts, sems):
    width = gate_ref.shape[1]
    deep = even_split(width, DEPTH_STEP)
    sides = ((gate_in, gate_ref), (up_in, up_ref))

    def copies(at):
        span = pl.ds(at * deep, deep)
        return [
            pltpu.make_async_copy(source.at[0, span, :], kept.at[0, span, :], sems.at[side, at])
            for side, (source, kept) in enumerate(sides)
        ]

    steps = width // deep
    for at in range(steps):
        for copy in copies(at):
            copy.start()
    for at in range(steps):
        for copy in copies(at):
            copy.wait()
        span = pl.ds(at * deep, deep)
        for side, (_, kept) in enumerate(sides):
            now = jnp.dot(rows_ref[:, span], kept[0, span, :], preferred_element_type=jnp.float32)
            if at == 0:
                parts[side] = now
            else:
                parts[side] += now
    gate_part, up_part = parts[0], parts[1]
    hidden_ref[...] = (gate_part / (1.0 + jnp.exp(-gate_part)) * up_part).astype(jnp.bfloat16)


def second_kernel(top_count, rows_ref, hidden_ref, down_in, out_ref, down_ref, sems):
    hidden_width, width = down_ref.shape[1:]
    wide = even_split(hidden_width, HIDDEN_STEP)

    def copy(at):
        span = pl.ds(at * wide, wide)
        return pltpu.make_async_copy(down_in.at[0, span, :], down_ref.at[0, span, :], sems.at[at])

    steps = hidden_width // wide
    for at in range(steps):
        copy(at).start()
    scale = row_scale(rows_ref[:, width:], lax.axis_index("expert"), top_count)
    for at in range(steps):
        copy(at).wait()
        span = pl.ds(at * wide, wide)
        now = jnp.dot(hidden_ref[:, span], down_ref[0, span, :], preferred_element_type=jnp.float32)
        if at == 0:
            out_ref[...] = now
        else:
            out_ref[...] += now
    out_ref[...] = out_ref[...] * scale


def take_inputs_in(made, block, gate, up):
    _, width, hidden_width = gate.shape
    rows = block.shape[0]
    hidden, gate, up = pl.pallas_call(
        first_kernel,
        out_shape=[made((rows, hidden_width), jnp.bfloat16)] + [made(gate.shape, gate.dtype)] * 2,
        in_specs=[IN_VMEM] + [IN_HBM] * 2,
        out_specs=[IN_VMEM] * 3,
        scratch_shapes=[
            pltpu.VMEM((2, rows, hidden_width), jnp.float32),
            pltpu.SemaphoreType.DMA((2, width // even_split(width, DEPTH_STEP))),
        ],
        compiler_params=pltpu.CompilerParams(vmem_limit_bytes=SCOPED_BYTES),
        cost_estimate=pl.CostEstimate(
            flops=4 * rows * width * hidden_width,
            bytes_accessed=4 * width * hidden_width,
            transcendentals=rows * hidden_width,
        ),
    )(made.pin(block), in_hbm(gate), in_hbm(up))
    return hidden, gate, up


def take_output_in(made, top_count, block, hidden, down):
    _, hidden_width, width = down.shape
    rows = block.shape[0]
    return pl.pallas_call(
        functools.partial(second_kernel, top_count),
        out_shape=[made((rows, width), jnp.float32), made(down.shape, down.dtype)],
        in_specs=[IN_VMEM] * 2 + [IN_HBM],
        out_specs=[IN_VMEM] * 2,
        scratch_shapes=[
            pltpu.SemaphoreType.DMA((hidden_width // even_split(hidden_width, HIDDEN_STEP),))
        ],
        compiler_params=pltpu.CompilerParams(vmem_limit_bytes=SCOPED_BYTES),
        cost_estimate=pl.CostEstimate(
            flops=2 * rows * width * hidden_width,
            bytes_accessed=2 * width * hidden_width,
            transcendentals=0,
        ),
    )(made.pin(block), made.pin(hidden), in_hbm(down))


class InVmem:
    def __call__(self, shape, dtype):
        return pltpu.VMEM(shape, dtype)

    def pin(self, array):
        return pltpu.with_memory_space_constraint(array, pltpu.VMEM)


class Anywhere:
    def __call__(self, shape, dtype):
        return jax.ShapeDtypeStruct(shape, dtype)

    def pin(self, array):
        return array


def add_rounded(*terms):
    return sum(term.astype(jnp.float32) for term in terms).astype(jnp.bfloat16)


def shards(tokens, expert_ids, gate_weights, w_gate, w_up, w_down):
    local, width = tokens.shape
    top_count = expert_ids.shape[1]
    devices = lax.axis_size("expert")
    ring = chip_ring(devices // 2)
    ways = (ring_pairs(ring, 1), ring_pairs(ring, -1))
    siblings = [(at, at ^ 1) for at in range(devices)]
    hops = (len(ring) // 2, (len(ring) - 1) // 2)
    own = (w_gate, w_up, w_down)
    weight_bytes = 2 * sum(array.size * array.dtype.itemsize for array in own)
    kept_bytes = weight_bytes + len(ring) * local * width * 6
    made = InVmem() if kept_bytes <= KEPT_BYTES else Anywhere()
    run = functools.partial(run_experts, made, top_count)
    after = lax.optimization_barrier

    def outward(block, way):
        return lax.ppermute(block, "expert", ways[way])

    def homeward(block, way):
        return lax.ppermute(block, "expert", ways[1 - way])

    first = pack_rows(tokens, expert_ids, gate_weights, made)
    first, ready = after((first, own))
    other = tuple(lax.ppermute(array, "expert", siblings) for array in ready)

    rows = {(0, 0): first}
    partial = {}
    if hops[0]:
        rows[0, 1] = outward(first, 0)
    hidden, gate, up = take_inputs_in(made, first, w_gate, w_up)
    if hops[1]:
        later, hidden = after((first, hidden))
        rows[1, 1] = outward(later, 1)
    partial[0, 0], down = take_output_in(made, top_count, first, hidden, w_down)
    own = (gate, up, down)
    if hops[0]:
        rows[0, 1], partial[0, 0] = after((rows[0, 1], partial[0, 0]))
    for hop in range(2, hops[0] + 1):
        rows[0, hop] = outward(rows[0, hop - 1], 0)
        keys = [(0, hop - 1)] + [(1, hop - 2)] * (hop > 2)
        results = run([rows[key] for key in keys], (0,), [own])
        rows[1, hop - 1], results = after((rows[1, hop - 1], results))
        partial.update(zip(keys, results))
        if hop <= hops[1]:
            rows[1, hop] = outward(rows[1, hop - 1], 1)
    ends = [[key for key in rows if key not in partial and key[0] == way] for way in (1, 0)]
    complete = ends[0] + ends[1]
    for keys in ends:
        if keys:
            results = run([rows[key] for key in keys], (0, 1), [own, other])
            partial.update(zip(keys, results))

    def sibling_sums(keys, prior):
        return run([rows[key] for key in keys], (1,), [other], prior)

    if hops[0] < 2:
        partial[0, 0] = sibling_sums([(0, 0)], [partial[0, 0]])[0]
    arrived = [None, None]
    level = list(hops)
    if level[1]:
        arrived[1] = homeward(partial[1, level[1]].astype(jnp.bfloat16), 1)
        level[1] -= 1
    while level[0]:
        value = add_rounded(partial[0, level[0]], *[x for x in arrived[:1] if x is not None])
        arrived[0] = homeward(value, 0)
        level[0] -= 1
        keys = [key for key in [(0, level[0]), (1, level[1])] if key[1] and key not in complete]
        keys += [(0, 0)] * (level[0] == 1)
        if keys:
            prior, _ = after(([partial[key] for key in keys], value))
            results = sibling_sums(keys, prior)
            if arrived[1] is not None:
                arrived[1], results = after((arrived[1], results))
            partial.update(zip(keys, results))
        if level[1]:
            arrived[1] = homeward(add_rounded(arrived[1], partial[1, level[1]]), 1)
            level[1] -= 1
    return add_rounded(partial[0, 0], *[value for value in arrived if value is not None])


def solution(mesh):
    placed = (
        P(("groups", "expert"), None),
        P(("groups", "expert"), None),
        P(("groups", "expert"), None),
        P("expert", None, None),
        P("expert", None, None),
        P("expert", None, None),
    )
    return jax.shard_map(
        shards, mesh=mesh, in_specs=placed, out_specs=P(("groups", "expert"), None), check_vma=False
    )
```

```python
import functools

import jax
import jax.numpy as jnp
from jax import lax
from jax.experimental import pallas as pl
from jax.experimental.pallas import tpu as pltpu
from jax.sharding import PartitionSpec as P

LANES = 128
IN_VMEM = pl.BlockSpec(memory_space=pltpu.VMEM)
IN_HBM = pl.BlockSpec(memory_space=pltpu.HBM)
DEPTH_STEP = 512
HIDDEN_STEP = 256
PASS_ROWS = 192
SCOPED_BYTES = 8 * 1024 * 1024
KEPT_BYTES = 32 * 1024 * 1024


def in_hbm(array):
    return pltpu.with_memory_space_constraint(array, pltpu.HBM)


def even_split(size, most):
    part = most
    while size % part:
        part //= 2
    return part


def chip_ring(chips):
    across = max(d for d in range(1, chips + 1) if chips % d == 0 and d * d <= chips)
    down = chips // across
    if across == 1 or down % 2:
        return list(range(chips))
    ring = []
    for row in range(down):
        columns = list(range(1, across))
        ring += [row * across + column for column in (columns if row % 2 == 0 else columns[::-1])]
    return [0] + ring + [row * across for row in range(down - 1, 0, -1)]


def ring_pairs(ring, way):
    count = len(ring)
    pairs = []
    for at, chip in enumerate(ring):
        for core in (0, 1):
            step = way if core == at % 2 else -way
            pairs.append((2 * chip + core, 2 * ring[(at + step) % count] + 1 - core))
    return pairs


def pack_kernel(tokens_ref, ids_ref, gates_ref, out_ref, ids_buf, gates_buf, sems):
    width = tokens_ref.shape[1]
    copies = [
        pltpu.make_async_copy(ids_ref, ids_buf, sems.at[0]),
        pltpu.make_async_copy(gates_ref, gates_buf, sems.at[1]),
        pltpu.make_async_copy(tokens_ref, out_ref.at[:, pl.ds(0, width)], sems.at[2]),
    ]
    for copy in copies:
        copy.start()
    for copy in copies[:2]:
        copy.wait()
    rest = gates_buf[...]
    parts = [ids_buf[...].astype(jnp.float32)]
    for _ in range(3):
        parts.append(rest.astype(jnp.bfloat16).astype(jnp.float32))
        rest = rest - parts[-1]
    stacked = jnp.concatenate(parts, axis=0)
    shape = (stacked.shape[0], out_ref.shape[1] - width)
    unit = lax.broadcasted_iota(jnp.int32, shape, 0) == lax.broadcasted_iota(jnp.int32, shape, 1)
    route = lax.dot_general(
        stacked.astype(jnp.bfloat16),
        unit.astype(jnp.float32).astype(jnp.bfloat16),
        (((0,), (0,)), ((), ())),
        preferred_element_type=jnp.float32,
    )
    out_ref[:, width:] = route.astype(jnp.bfloat16)
    copies[2].wait()


def pack_rows(tokens, expert_ids, gate_weights, made):
    rows, width = tokens.shape
    extra = -(-4 * expert_ids.shape[1] // LANES) * LANES
    ids, gates = expert_ids.T, gate_weights.T
    return pl.pallas_call(
        pack_kernel,
        out_shape=made((rows, width + extra), jnp.bfloat16),
        in_specs=[IN_HBM] * 3,
        out_specs=IN_VMEM,
        scratch_shapes=[
            pltpu.VMEM(ids.shape, ids.dtype),
            pltpu.VMEM(gates.shape, gates.dtype),
            pltpu.SemaphoreType.DMA((3,)),
        ],
        compiler_params=pltpu.CompilerParams(vmem_limit_bytes=SCOPED_BYTES),
    )(in_hbm(tokens), in_hbm(ids), in_hbm(gates))


def row_scale(route, expert, top_count):
    route = route.astype(jnp.float32)
    chosen = (route[:, :top_count] == expert.astype(jnp.float32)).astype(jnp.float32)
    weight = sum(route[:, top_count * part : top_count * (part + 1)] for part in (1, 2, 3))
    return jnp.sum(chosen * weight, axis=1, keepdims=True)


def expert_kernel(blocks, flips, with_prior, top_count, *refs):
    row_refs, refs = refs[:blocks], refs[blocks:]
    weight_refs, refs = refs[: 3 * len(flips)], refs[3 * len(flips) :]
    prior_refs, refs = (refs[:blocks], refs[blocks:]) if with_prior else ((), refs)
    out_refs, (rows_buf, total) = refs[:blocks], refs[blocks:]
    block_rows, width = out_refs[0].shape
    real = blocks * block_rows
    me = lax.axis_index("expert")
    for at in range(rows_buf.shape[0] // block_rows):
        rows_buf[pl.ds(at * block_rows, block_rows), :] = row_refs[at % blocks][...]
    for at in range(blocks if with_prior else 0):
        total[pl.ds(at * block_rows, block_rows), :] = prior_refs[at][...]
    rows = rows_buf[:, :width]
    for at, flip in enumerate(flips):
        gate_ref, up_ref, down_ref = weight_refs[3 * at : 3 * at + 3]
        scale = row_scale(rows_buf[:real, width:], me ^ flip, top_count)
        gate_part = jnp.dot(rows, gate_ref[0], preferred_element_type=jnp.float32)
        up_part = jnp.dot(rows, up_ref[0], preferred_element_type=jnp.float32)
        hidden = (gate_part / (1.0 + jnp.exp(-gate_part)) * up_part).astype(jnp.bfloat16)
        result = jnp.dot(hidden, down_ref[0], preferred_element_type=jnp.float32)[:real] * scale
        if at or with_prior:
            total[...] += result
        else:
            total[...] = result
    for at in range(blocks):
        out_refs[at][...] = total[pl.ds(at * block_rows, block_rows), :]


def run_experts(made, top_count, row_blocks, flips, weights, prior=()):
    blocks, experts = len(row_blocks), len(weights)
    block_rows, row_width = row_blocks[0].shape
    _, width, hidden_width = weights[0][0].shape
    total = blocks * block_rows
    padded = max(total, PASS_ROWS // block_rows * block_rows) if experts == 1 else total
    return pl.pallas_call(
        functools.partial(expert_kernel, blocks, flips, bool(prior), top_count),
        out_shape=[made((block_rows, width), jnp.float32)] * blocks,
        in_specs=[IN_VMEM] * (blocks + 3 * experts + len(prior)),
        out_specs=[IN_VMEM] * blocks,
        scratch_shapes=[
            pltpu.VMEM((padded, row_width), jnp.bfloat16),
            pltpu.VMEM((total, width), jnp.float32),
        ],
        compiler_params=pltpu.CompilerParams(vmem_limit_bytes=SCOPED_BYTES),
        cost_estimate=pl.CostEstimate(
            flops=6 * total * width * hidden_width * experts,
            bytes_accessed=2 * (3 * width * hidden_width * experts + 2 * total * width),
            transcendentals=total * hidden_width * experts,
        ),
    )(
        *(made.pin(block) for block in row_blocks),
        *(made.pin(array) for weight in weights for array in weight),
        *(made.pin(block) for block in prior),
    )


def first_kernel(rows_ref, gate_in, up_in, hidden_ref, gate_ref, up_ref, parts, sems):
    width = gate_ref.shape[1]
    deep = even_split(width, DEPTH_STEP)
    sides = ((gate_in, gate_ref), (up_in, up_ref))

    def copies(at):
        span = pl.ds(at * deep, deep)
        return [
            pltpu.make_async_copy(source.at[0, span, :], kept.at[0, span, :], sems.at[side, at])
            for side, (source, kept) in enumerate(sides)
        ]

    steps = width // deep
    for at in range(steps):
        for copy in copies(at):
            copy.start()
    for at in range(steps):
        for copy in copies(at):
            copy.wait()
        span = pl.ds(at * deep, deep)
        for side, (_, kept) in enumerate(sides):
            now = jnp.dot(rows_ref[:, span], kept[0, span, :], preferred_element_type=jnp.float32)
            if at == 0:
                parts[side] = now
            else:
                parts[side] += now
    gate_part, up_part = parts[0], parts[1]
    hidden_ref[...] = (gate_part / (1.0 + jnp.exp(-gate_part)) * up_part).astype(jnp.bfloat16)


def second_kernel(top_count, rows_ref, hidden_ref, down_in, out_ref, down_ref, sems):
    hidden_width, width = down_ref.shape[1:]
    wide = even_split(hidden_width, HIDDEN_STEP)

    def copy(at):
        span = pl.ds(at * wide, wide)
        return pltpu.make_async_copy(down_in.at[0, span, :], down_ref.at[0, span, :], sems.at[at])

    steps = hidden_width // wide
    for at in range(steps):
        copy(at).start()
    scale = row_scale(rows_ref[:, width:], lax.axis_index("expert"), top_count)
    for at in range(steps):
        copy(at).wait()
        span = pl.ds(at * wide, wide)
        now = jnp.dot(hidden_ref[:, span], down_ref[0, span, :], preferred_element_type=jnp.float32)
        if at == 0:
            out_ref[...] = now
        else:
            out_ref[...] += now
    out_ref[...] = out_ref[...] * scale


def take_inputs_in(made, block, gate, up):
    _, width, hidden_width = gate.shape
    rows = block.shape[0]
    hidden, gate, up = pl.pallas_call(
        first_kernel,
        out_shape=[made((rows, hidden_width), jnp.bfloat16)] + [made(gate.shape, gate.dtype)] * 2,
        in_specs=[IN_VMEM] + [IN_HBM] * 2,
        out_specs=[IN_VMEM] * 3,
        scratch_shapes=[
            pltpu.VMEM((2, rows, hidden_width), jnp.float32),
            pltpu.SemaphoreType.DMA((2, width // even_split(width, DEPTH_STEP))),
        ],
        compiler_params=pltpu.CompilerParams(vmem_limit_bytes=SCOPED_BYTES),
        cost_estimate=pl.CostEstimate(
            flops=4 * rows * width * hidden_width,
            bytes_accessed=4 * width * hidden_width,
            transcendentals=rows * hidden_width,
        ),
    )(made.pin(block), in_hbm(gate), in_hbm(up))
    return hidden, gate, up


def take_output_in(made, top_count, block, hidden, down):
    _, hidden_width, width = down.shape
    rows = block.shape[0]
    return pl.pallas_call(
        functools.partial(second_kernel, top_count),
        out_shape=[made((rows, width), jnp.float32), made(down.shape, down.dtype)],
        in_specs=[IN_VMEM] * 2 + [IN_HBM],
        out_specs=[IN_VMEM] * 2,
        scratch_shapes=[
            pltpu.SemaphoreType.DMA((hidden_width // even_split(hidden_width, HIDDEN_STEP),))
        ],
        compiler_params=pltpu.CompilerParams(vmem_limit_bytes=SCOPED_BYTES),
        cost_estimate=pl.CostEstimate(
            flops=2 * rows * width * hidden_width,
            bytes_accessed=2 * width * hidden_width,
            transcendentals=0,
        ),
    )(made.pin(block), made.pin(hidden), in_hbm(down))


class InVmem:
    def __call__(self, shape, dtype):
        return pltpu.VMEM(shape, dtype)

    def pin(self, array):
        return pltpu.with_memory_space_constraint(array, pltpu.VMEM)


class Anywhere:
    def __call__(self, shape, dtype):
        return jax.ShapeDtypeStruct(shape, dtype)

    def pin(self, array):
        return array


def add_rounded(*terms):
    return sum(term.astype(jnp.float32) for term in terms).astype(jnp.bfloat16)


def shards(tokens, expert_ids, gate_weights, w_gate, w_up, w_down):
    local, width = tokens.shape
    top_count = expert_ids.shape[1]
    devices = lax.axis_size("expert")
    ring = chip_ring(devices // 2)
    ways = (ring_pairs(ring, 1), ring_pairs(ring, -1))
    siblings = [(at, at ^ 1) for at in range(devices)]
    hops = (len(ring) // 2, (len(ring) - 1) // 2)
    own = (w_gate, w_up, w_down)
    weight_bytes = 2 * sum(array.size * array.dtype.itemsize for array in own)
    kept_bytes = weight_bytes + len(ring) * local * width * 6
    made = InVmem() if kept_bytes <= KEPT_BYTES else Anywhere()
    run = functools.partial(run_experts, made, top_count)
    after = lax.optimization_barrier

    def outward(block, way):
        return lax.ppermute(block, "expert", ways[way])

    def homeward(block, way):
        return lax.ppermute(block, "expert", ways[1 - way])

    first = pack_rows(tokens, expert_ids, gate_weights, made)
    first, ready = after((first, own))
    other = tuple(lax.ppermute(array, "expert", siblings) for array in ready)

    rows = {(0, 0): first}
    partial = {}
    if hops[0]:
        rows[0, 1] = outward(first, 0)
    hidden, gate, up = take_inputs_in(made, first, w_gate, w_up)
    if hops[1]:
        later, hidden = after((first, hidden))
        rows[1, 1] = outward(later, 1)
    partial[0, 0], down = take_output_in(made, top_count, first, hidden, w_down)
    own = (gate, up, down)
    if hops[0]:
        rows[0, 1], partial[0, 0] = after((rows[0, 1], partial[0, 0]))
    for hop in range(2, hops[0] + 1):
        rows[0, hop] = outward(rows[0, hop - 1], 0)
        keys = [(0, hop - 1)] + [(1, hop - 2)] * (hop > 2)
        results = run([rows[key] for key in keys], (0,), [own])
        rows[1, hop - 1], results = after((rows[1, hop - 1], results))
        partial.update(zip(keys, results))
        if hop <= hops[1]:
            rows[1, hop] = outward(rows[1, hop - 1], 1)
    keys = [key for key in rows if key not in partial]
    if keys:
        results = run([rows[key] for key in keys], (0, 1), [own, other])
        partial.update(zip(keys, results))

    def sibling_sums(keys, prior):
        return run([rows[key] for key in keys], (1,), [other], prior)

    if hops[0] < 2:
        partial[0, 0] = sibling_sums([(0, 0)], [partial[0, 0]])[0]
    arrived = [None, None]
    level = list(hops)
    while level[0]:
        values = [None, None]
        values[0] = add_rounded(partial[0, level[0]], *[x for x in arrived[:1] if x is not None])
        arrived[0] = homeward(values[0], 0)
        keys = [(way, at - 1) for way, at in enumerate(level) if at > 1]
        keys = [key for key in keys if key in partial and key != (1, hops[0] - 1)]
        keys += [(0, 0)] * (level[0] == 2)
        waiting = arrived[1] if arrived[1] is not None else partial.get((1, level[1]))
        if keys:
            prior, _ = after(([partial[key] for key in keys], values[0]))
            waiting, results = after((waiting, sibling_sums(keys, prior)))
            partial.update(zip(keys, results))
        if level[1]:
            values[1] = add_rounded(*([waiting] if arrived[1] is None else [waiting, partial[1, level[1]]]))
            arrived[1] = homeward(values[1], 1)
        elif arrived[1] is not None:
            arrived[1] = waiting
        level = [max(at - 1, 0) for at in level]
    return add_rounded(partial[0, 0], *[value for value in arrived if value is not None])


def solution(mesh):
    placed = (
        P(("groups", "expert"), None),
        P(("groups", "expert"), None),
        P(("groups", "expert"), None),
        P("expert", None, None),
        P("expert", None, None),
        P("expert", None, None),
    )
    return jax.shard_map(
        shards, mesh=mesh, in_specs=placed, out_specs=P(("groups", "expert"), None), check_vma=False
    )
```

```python
import functools

import jax
import jax.numpy as jnp
from jax import lax
from jax.experimental import pallas as pl
from jax.experimental.pallas import tpu as pltpu
from jax.sharding import PartitionSpec as P

LANES = 128
IN_VMEM = pl.BlockSpec(memory_space=pltpu.VMEM)
IN_HBM = pl.BlockSpec(memory_space=pltpu.HBM)
DEPTH_STEP = 512
HIDDEN_STEP = 256
PASS_ROWS = 192
HINT = 12
KEPT_BYTES = 32 * 1024 * 1024


def in_hbm(array):
    return pltpu.with_memory_space_constraint(array, pltpu.HBM)


def even_split(size, most):
    part = most
    while size % part:
        part //= 2
    return part


def chip_ring(chips):
    across = max(d for d in range(1, chips + 1) if chips % d == 0 and d * d <= chips)
    down = chips // across
    if across == 1 or down % 2:
        return list(range(chips))
    ring = []
    for row in range(down):
        columns = list(range(1, across))
        ring += [row * across + column for column in (columns if row % 2 == 0 else columns[::-1])]
    return [0] + ring + [row * across for row in range(down - 1, 0, -1)]


def ring_pairs(ring, way):
    count = len(ring)
    pairs = []
    for at, chip in enumerate(ring):
        for core in (0, 1):
            step = way if core == at % 2 else -way
            pairs.append((2 * chip + core, 2 * ring[(at + step) % count] + 1 - core))
    return pairs


def pack_kernel(tokens_ref, ids_ref, gates_ref, out_ref, ids_buf, gates_buf, sems):
    width = tokens_ref.shape[1]
    copies = [
        pltpu.make_async_copy(ids_ref, ids_buf, sems.at[0]),
        pltpu.make_async_copy(gates_ref, gates_buf, sems.at[1]),
        pltpu.make_async_copy(tokens_ref, out_ref.at[:, pl.ds(0, width)], sems.at[2]),
    ]
    for copy in copies:
        copy.start()
    for copy in copies[:2]:
        copy.wait()
    rest = gates_buf[...]
    parts = [ids_buf[...].astype(jnp.float32)]
    for _ in range(3):
        parts.append(rest.astype(jnp.bfloat16).astype(jnp.float32))
        rest = rest - parts[-1]
    stacked = jnp.concatenate(parts, axis=0)
    shape = (stacked.shape[0], out_ref.shape[1] - width)
    unit = lax.broadcasted_iota(jnp.int32, shape, 0) == lax.broadcasted_iota(jnp.int32, shape, 1)
    route = lax.dot_general(
        stacked.astype(jnp.bfloat16),
        unit.astype(jnp.float32).astype(jnp.bfloat16),
        (((0,), (0,)), ((), ())),
        preferred_element_type=jnp.float32,
    )
    out_ref[:, width:] = route.astype(jnp.bfloat16)
    copies[2].wait()


def pack_rows(tokens, expert_ids, gate_weights, made):
    rows, width = tokens.shape
    extra = -(-4 * expert_ids.shape[1] // LANES) * LANES
    ids, gates = expert_ids.T, gate_weights.T
    return pl.pallas_call(
        pack_kernel,
        out_shape=made((rows, width + extra), jnp.bfloat16),
        in_specs=[IN_HBM] * 3,
        out_specs=IN_VMEM,
        scratch_shapes=[
            pltpu.VMEM(ids.shape, ids.dtype),
            pltpu.VMEM(gates.shape, gates.dtype),
            pltpu.SemaphoreType.DMA((3,)),
        ],
        compiler_params=pltpu.CompilerParams(vmem_limit_bytes=made.scoped_bytes),
    )(in_hbm(tokens), in_hbm(ids), in_hbm(gates))


def row_scale(route, expert, top_count):
    route = route.astype(jnp.float32)
    chosen = (route[:, :top_count] == expert.astype(jnp.float32)).astype(jnp.float32)
    weight = sum(route[:, top_count * part : top_count * (part + 1)] for part in (1, 2, 3))
    return jnp.sum(chosen * weight, axis=1, keepdims=True)


def expert_kernel(blocks, flips, with_prior, top_count, *refs):
    row_refs, refs = refs[:blocks], refs[blocks:]
    weight_refs, refs = refs[: 3 * len(flips)], refs[3 * len(flips) :]
    prior_refs, refs = (refs[:blocks], refs[blocks:]) if with_prior else ((), refs)
    out_refs, (rows_buf, total) = refs[:blocks], refs[blocks:]
    block_rows, width = out_refs[0].shape
    real = blocks * block_rows
    me = lax.axis_index("expert")
    for at in range(rows_buf.shape[0] // block_rows):
        rows_buf[pl.ds(at * block_rows, block_rows), :] = row_refs[at % blocks][...]
    for at in range(blocks if with_prior else 0):
        total[pl.ds(at * block_rows, block_rows), :] = prior_refs[at][...]
    rows = rows_buf[:, :width]
    for at, flip in enumerate(flips):
        gate_ref, up_ref, down_ref = weight_refs[3 * at : 3 * at + 3]
        scale = row_scale(rows_buf[:real, width:], me ^ flip, top_count)
        gate_part = jnp.dot(rows, gate_ref[0], preferred_element_type=jnp.float32)
        up_part = jnp.dot(rows, up_ref[0], preferred_element_type=jnp.float32)
        hidden = (gate_part / (1.0 + jnp.exp(-gate_part)) * up_part).astype(jnp.bfloat16)
        result = jnp.dot(hidden, down_ref[0], preferred_element_type=jnp.float32)[:real] * scale
        if at or with_prior:
            total[...] += result
        else:
            total[...] = result
    for at in range(blocks):
        out_refs[at][...] = total[pl.ds(at * block_rows, block_rows), :]


def run_experts(made, top_count, row_blocks, flips, weights, prior=()):
    blocks, experts = len(row_blocks), len(weights)
    block_rows, row_width = row_blocks[0].shape
    _, width, hidden_width = weights[0][0].shape
    total = blocks * block_rows
    padded = max(total, PASS_ROWS // block_rows * block_rows) if experts == 1 else total
    return pl.pallas_call(
        functools.partial(expert_kernel, blocks, flips, bool(prior), top_count),
        out_shape=[made((block_rows, width), jnp.float32)] * blocks,
        in_specs=[IN_VMEM] * (blocks + 3 * experts + len(prior)),
        out_specs=[IN_VMEM] * blocks,
        scratch_shapes=[
            pltpu.VMEM((padded, row_width), jnp.bfloat16),
            pltpu.VMEM((total, width), jnp.float32),
        ],
        compiler_params=pltpu.CompilerParams(vmem_limit_bytes=made.scoped_bytes),
        cost_estimate=pl.CostEstimate(
            flops=HINT * 6 * total * width * hidden_width * experts,
            bytes_accessed=2 * (3 * width * hidden_width * experts + 2 * total * width),
            transcendentals=total * hidden_width * experts,
        ),
    )(
        *(made.pin(block) for block in row_blocks),
        *(made.pin(array) for weight in weights for array in weight),
        *(made.pin(block) for block in prior),
    )


def first_kernel(rows_ref, gate_in, up_in, hidden_ref, gate_ref, up_ref, parts, sems):
    width = gate_ref.shape[1]
    deep = even_split(width, DEPTH_STEP)
    sides = ((gate_in, gate_ref), (up_in, up_ref))

    def copies(at):
        span = pl.ds(at * deep, deep)
        return [
            pltpu.make_async_copy(source.at[0, span, :], kept.at[0, span, :], sems.at[side, at])
            for side, (source, kept) in enumerate(sides)
        ]

    steps = width // deep
    for at in range(steps):
        for copy in copies(at):
            copy.start()
    for at in range(steps):
        for copy in copies(at):
            copy.wait()
        span = pl.ds(at * deep, deep)
        for side, (_, kept) in enumerate(sides):
            now = jnp.dot(rows_ref[:, span], kept[0, span, :], preferred_element_type=jnp.float32)
            if at == 0:
                parts[side] = now
            else:
                parts[side] += now
    gate_part, up_part = parts[0], parts[1]
    hidden_ref[...] = (gate_part / (1.0 + jnp.exp(-gate_part)) * up_part).astype(jnp.bfloat16)


def second_kernel(top_count, rows_ref, hidden_ref, down_in, out_ref, down_ref, sems):
    hidden_width, width = down_ref.shape[1:]
    wide = even_split(hidden_width, HIDDEN_STEP)

    def copy(at):
        span = pl.ds(at * wide, wide)
        return pltpu.make_async_copy(down_in.at[0, span, :], down_ref.at[0, span, :], sems.at[at])

    steps = hidden_width // wide
    for at in range(steps):
        copy(at).start()
    scale = row_scale(rows_ref[:, width:], lax.axis_index("expert"), top_count)
    for at in range(steps):
        copy(at).wait()
        span = pl.ds(at * wide, wide)
        now = jnp.dot(hidden_ref[:, span], down_ref[0, span, :], preferred_element_type=jnp.float32)
        if at == 0:
            out_ref[...] = now
        else:
            out_ref[...] += now
    out_ref[...] = out_ref[...] * scale


def take_inputs_in(made, block, gate, up):
    _, width, hidden_width = gate.shape
    rows = block.shape[0]
    hidden, gate, up = pl.pallas_call(
        first_kernel,
        out_shape=[made((rows, hidden_width), jnp.bfloat16)] + [made(gate.shape, gate.dtype)] * 2,
        in_specs=[IN_VMEM] + [IN_HBM] * 2,
        out_specs=[IN_VMEM] * 3,
        scratch_shapes=[
            pltpu.VMEM((2, rows, hidden_width), jnp.float32),
            pltpu.SemaphoreType.DMA((2, width // even_split(width, DEPTH_STEP))),
        ],
        compiler_params=pltpu.CompilerParams(vmem_limit_bytes=made.scoped_bytes),
        cost_estimate=pl.CostEstimate(
            flops=HINT * 4 * rows * width * hidden_width,
            bytes_accessed=4 * width * hidden_width,
            transcendentals=rows * hidden_width,
        ),
    )(made.pin(block), in_hbm(gate), in_hbm(up))
    return hidden, gate, up


def take_output_in(made, top_count, block, hidden, down):
    _, hidden_width, width = down.shape
    rows = block.shape[0]
    return pl.pallas_call(
        functools.partial(second_kernel, top_count),
        out_shape=[made((rows, width), jnp.float32), made(down.shape, down.dtype)],
        in_specs=[IN_VMEM] * 2 + [IN_HBM],
        out_specs=[IN_VMEM] * 2,
        scratch_shapes=[
            pltpu.SemaphoreType.DMA((hidden_width // even_split(hidden_width, HIDDEN_STEP),))
        ],
        compiler_params=pltpu.CompilerParams(vmem_limit_bytes=made.scoped_bytes),
        cost_estimate=pl.CostEstimate(
            flops=HINT * 2 * rows * width * hidden_width,
            bytes_accessed=2 * width * hidden_width,
            transcendentals=0,
        ),
    )(made.pin(block), made.pin(hidden), in_hbm(down))


class InVmem:
    scoped_bytes = 8 * 1024 * 1024

    def __call__(self, shape, dtype):
        return pltpu.VMEM(shape, dtype)

    def pin(self, array):
        return pltpu.with_memory_space_constraint(array, pltpu.VMEM)


class Anywhere:
    scoped_bytes = 48 * 1024 * 1024

    def __call__(self, shape, dtype):
        return jax.ShapeDtypeStruct(shape, dtype)

    def pin(self, array):
        return array


def add_rounded(*terms):
    return sum(term.astype(jnp.float32) for term in terms).astype(jnp.bfloat16)


def shards(tokens, expert_ids, gate_weights, w_gate, w_up, w_down):
    local, width = tokens.shape
    top_count = expert_ids.shape[1]
    devices = lax.axis_size("expert")
    ring = chip_ring(devices // 2)
    ways = (ring_pairs(ring, 1), ring_pairs(ring, -1))
    siblings = [(at, at ^ 1) for at in range(devices)]
    hops = (len(ring) // 2, (len(ring) - 1) // 2)
    own = (w_gate, w_up, w_down)
    weight_bytes = 2 * sum(array.size * array.dtype.itemsize for array in own)
    kept_bytes = weight_bytes + len(ring) * local * width * 6
    made = InVmem() if kept_bytes <= KEPT_BYTES else Anywhere()
    run = functools.partial(run_experts, made, top_count)
    after = lax.optimization_barrier

    def outward(block, way):
        return lax.ppermute(block, "expert", ways[way])

    def homeward(block, way):
        return lax.ppermute(block, "expert", ways[1 - way])

    first = pack_rows(tokens, expert_ids, gate_weights, made)

    rows = {(0, 0): first}
    partial = {}
    if hops[0]:
        rows[0, 1] = outward(first, 0)
    hidden, gate, up = take_inputs_in(made, first, w_gate, w_up)
    if hops[1]:
        later, hidden = after((first, hidden))
        rows[1, 1] = outward(later, 1)
    hidden, ready = after((hidden, (gate, up)))
    other = tuple(lax.ppermute(array, "expert", siblings) for array in ready)
    partial[0, 0], down = take_output_in(made, top_count, first, hidden, w_down)
    own = (gate, up, down)
    other += (lax.ppermute(down, "expert", siblings),)
    if hops[0]:
        rows[0, 1], partial[0, 0] = after((rows[0, 1], partial[0, 0]))
    for hop in range(2, hops[0] + 1):
        rows[0, hop] = outward(rows[0, hop - 1], 0)
        keys = [(0, hop - 1)] + [(1, hop - 2)] * (hop > 2)
        results = run([rows[key] for key in keys], (0,), [own])
        rows[1, hop - 1], results = after((rows[1, hop - 1], results))
        partial.update(zip(keys, results))
        if hop <= hops[1]:
            rows[1, hop] = outward(rows[1, hop - 1], 1)
    keys = [key for key in rows if key not in partial]
    if keys:
        results = run([rows[key] for key in keys], (0, 1), [own, other])
        partial.update(zip(keys, results))

    def sibling_sums(keys, prior):
        return run([rows[key] for key in keys], (1,), [other], prior)

    if hops[0] < 2:
        partial[0, 0] = sibling_sums([(0, 0)], [partial[0, 0]])[0]
    arrived = [None, None]
    level = list(hops)
    while level[0]:
        values = [None, None]
        values[0] = add_rounded(partial[0, level[0]], *[x for x in arrived[:1] if x is not None])
        arrived[0] = homeward(values[0], 0)
        keys = [(way, at - 1) for way, at in enumerate(level) if at > 1]
        keys = [key for key in keys if key in partial and key != (1, hops[0] - 1)]
        keys += [(0, 0)] * (level[0] == 2)
        waiting = arrived[1] if arrived[1] is not None else partial.get((1, level[1]))
        if keys:
            prior, _ = after(([partial[key] for key in keys], values[0]))
            waiting, results = after((waiting, sibling_sums(keys, prior)))
            partial.update(zip(keys, results))
        if level[1]:
            values[1] = add_rounded(*([waiting] if arrived[1] is None else [waiting, partial[1, level[1]]]))
            arrived[1] = homeward(values[1], 1)
        elif arrived[1] is not None:
            arrived[1] = waiting
        level = [max(at - 1, 0) for at in level]
    return add_rounded(partial[0, 0], *[value for value in arrived if value is not None])


def solution(mesh):
    placed = (
        P(("groups", "expert"), None),
        P(("groups", "expert"), None),
        P(("groups", "expert"), None),
        P("expert", None, None),
        P("expert", None, None),
        P("expert", None, None),
    )
    return jax.shard_map(
        shards, mesh=mesh, in_specs=placed, out_specs=P(("groups", "expert"), None), check_vma=False
    )
```

```python
import functools

import jax
import jax.numpy as jnp
from jax import lax
from jax.experimental import pallas as pl
from jax.experimental.pallas import tpu as pltpu
from jax.sharding import PartitionSpec as P

LANES = 128
IN_VMEM = pl.BlockSpec(memory_space=pltpu.VMEM)
IN_HBM = pl.BlockSpec(memory_space=pltpu.HBM)
DEPTH_STEP = 512
HIDDEN_STEP = 256
PASS_ROWS = 192
SCOPED_BYTES = 8 * 1024 * 1024
KEPT_BYTES = 32 * 1024 * 1024


def in_hbm(array):
    return pltpu.with_memory_space_constraint(array, pltpu.HBM)


def even_split(size, most):
    part = most
    while size % part:
        part //= 2
    return part


def chip_ring(chips):
    across = max(d for d in range(1, chips + 1) if chips % d == 0 and d * d <= chips)
    down = chips // across
    if across == 1 or down % 2:
        return list(range(chips))
    ring = []
    for row in range(down):
        columns = list(range(1, across))
        ring += [row * across + column for column in (columns if row % 2 == 0 else columns[::-1])]
    return [0] + ring + [row * across for row in range(down - 1, 0, -1)]


def ring_pairs(ring, way):
    count = len(ring)
    pairs = []
    for at, chip in enumerate(ring):
        for core in (0, 1):
            step = way if core == at % 2 else -way
            pairs.append((2 * chip + core, 2 * ring[(at + step) % count] + 1 - core))
    return pairs


def pack_kernel(tokens_ref, ids_ref, gates_ref, out_ref, ids_buf, gates_buf, sems):
    width = tokens_ref.shape[1]
    copies = [
        pltpu.make_async_copy(ids_ref, ids_buf, sems.at[0]),
        pltpu.make_async_copy(gates_ref, gates_buf, sems.at[1]),
        pltpu.make_async_copy(tokens_ref, out_ref.at[:, pl.ds(0, width)], sems.at[2]),
    ]
    for copy in copies:
        copy.start()
    for copy in copies[:2]:
        copy.wait()
    rest = gates_buf[...]
    parts = [ids_buf[...].astype(jnp.float32)]
    for _ in range(3):
        parts.append(rest.astype(jnp.bfloat16).astype(jnp.float32))
        rest = rest - parts[-1]
    stacked = jnp.concatenate(parts, axis=0)
    shape = (stacked.shape[0], out_ref.shape[1] - width)
    unit = lax.broadcasted_iota(jnp.int32, shape, 0) == lax.broadcasted_iota(jnp.int32, shape, 1)
    route = lax.dot_general(
        stacked.astype(jnp.bfloat16),
        unit.astype(jnp.float32).astype(jnp.bfloat16),
        (((0,), (0,)), ((), ())),
        preferred_element_type=jnp.float32,
    )
    out_ref[:, width:] = route.astype(jnp.bfloat16)
    copies[2].wait()


def pack_rows(tokens, expert_ids, gate_weights, made):
    rows, width = tokens.shape
    extra = -(-4 * expert_ids.shape[1] // LANES) * LANES
    ids, gates = expert_ids.T, gate_weights.T
    return pl.pallas_call(
        pack_kernel,
        out_shape=made((rows, width + extra), jnp.bfloat16),
        in_specs=[IN_HBM] * 3,
        out_specs=IN_VMEM,
        scratch_shapes=[
            pltpu.VMEM(ids.shape, ids.dtype),
            pltpu.VMEM(gates.shape, gates.dtype),
            pltpu.SemaphoreType.DMA((3,)),
        ],
        compiler_params=pltpu.CompilerParams(vmem_limit_bytes=SCOPED_BYTES),
    )(in_hbm(tokens), in_hbm(ids), in_hbm(gates))


def row_scale(route, expert, top_count):
    route = route.astype(jnp.float32)
    chosen = (route[:, :top_count] == expert.astype(jnp.float32)).astype(jnp.float32)
    weight = sum(route[:, top_count * part : top_count * (part + 1)] for part in (1, 2, 3))
    return jnp.sum(chosen * weight, axis=1, keepdims=True)


def expert_kernel(blocks, flips, with_prior, top_count, *refs):
    row_refs, refs = refs[:blocks], refs[blocks:]
    weight_refs, refs = refs[: 3 * len(flips)], refs[3 * len(flips) :]
    prior_refs, refs = (refs[:blocks], refs[blocks:]) if with_prior else ((), refs)
    out_refs, (rows_buf, total) = refs[:blocks], refs[blocks:]
    block_rows, width = out_refs[0].shape
    real = blocks * block_rows
    me = lax.axis_index("expert")
    for at in range(rows_buf.shape[0] // block_rows):
        rows_buf[pl.ds(at * block_rows, block_rows), :] = row_refs[at % blocks][...]
    for at in range(blocks if with_prior else 0):
        total[pl.ds(at * block_rows, block_rows), :] = prior_refs[at][...]
    rows = rows_buf[:, :width]
    for at, flip in enumerate(flips):
        gate_ref, up_ref, down_ref = weight_refs[3 * at : 3 * at + 3]
        scale = row_scale(rows_buf[:real, width:], me ^ flip, top_count)
        gate_part = jnp.dot(rows, gate_ref[0], preferred_element_type=jnp.float32)
        up_part = jnp.dot(rows, up_ref[0], preferred_element_type=jnp.float32)
        hidden = (gate_part / (1.0 + jnp.exp(-gate_part)) * up_part).astype(jnp.bfloat16)
        result = jnp.dot(hidden, down_ref[0], preferred_element_type=jnp.float32)[:real] * scale
        if at or with_prior:
            total[...] += result
        else:
            total[...] = result
    for at in range(blocks):
        out_refs[at][...] = total[pl.ds(at * block_rows, block_rows), :]


def run_experts(made, top_count, row_blocks, flips, weights, prior=()):
    blocks, experts = len(row_blocks), len(weights)
    block_rows, row_width = row_blocks[0].shape
    _, width, hidden_width = weights[0][0].shape
    total = blocks * block_rows
    padded = max(total, PASS_ROWS // block_rows * block_rows) if experts == 1 else total
    return pl.pallas_call(
        functools.partial(expert_kernel, blocks, flips, bool(prior), top_count),
        out_shape=[made((block_rows, width), jnp.float32)] * blocks,
        in_specs=[IN_VMEM] * (blocks + 3 * experts + len(prior)),
        out_specs=[IN_VMEM] * blocks,
        scratch_shapes=[
            pltpu.VMEM((padded, row_width), jnp.bfloat16),
            pltpu.VMEM((total, width), jnp.float32),
        ],
        compiler_params=pltpu.CompilerParams(vmem_limit_bytes=SCOPED_BYTES),
        cost_estimate=pl.CostEstimate(
            flops=6 * total * width * hidden_width * experts,
            bytes_accessed=2 * (3 * width * hidden_width * experts + 2 * total * width),
            transcendentals=total * hidden_width * experts,
        ),
    )(
        *(made.pin(block) for block in row_blocks),
        *(made.pin(array) for weight in weights for array in weight),
        *(made.pin(block) for block in prior),
    )


def first_kernel(rows_ref, gate_in, up_in, hidden_ref, gate_ref, up_ref, parts, sems):
    width = gate_ref.shape[1]
    deep = even_split(width, DEPTH_STEP)
    sides = ((gate_in, gate_ref), (up_in, up_ref))

    def copies(at):
        span = pl.ds(at * deep, deep)
        return [
            pltpu.make_async_copy(source.at[0, span, :], kept.at[0, span, :], sems.at[side, at])
            for side, (source, kept) in enumerate(sides)
        ]

    steps = width // deep
    for at in range(steps):
        for copy in copies(at):
            copy.start()
    for at in range(steps):
        for copy in copies(at):
            copy.wait()
        span = pl.ds(at * deep, deep)
        for side, (_, kept) in enumerate(sides):
            now = jnp.dot(rows_ref[:, span], kept[0, span, :], preferred_element_type=jnp.float32)
            if at == 0:
                parts[side] = now
            else:
                parts[side] += now
    gate_part, up_part = parts[0], parts[1]
    hidden_ref[...] = (gate_part / (1.0 + jnp.exp(-gate_part)) * up_part).astype(jnp.bfloat16)


def second_kernel(top_count, rows_ref, hidden_ref, down_in, out_ref, down_ref, sems):
    hidden_width, width = down_ref.shape[1:]
    wide = even_split(hidden_width, HIDDEN_STEP)

    def copy(at):
        span = pl.ds(at * wide, wide)
        return pltpu.make_async_copy(down_in.at[0, span, :], down_ref.at[0, span, :], sems.at[at])

    steps = hidden_width // wide
    for at in range(steps):
        copy(at).start()
    scale = row_scale(rows_ref[:, width:], lax.axis_index("expert"), top_count)
    for at in range(steps):
        copy(at).wait()
        span = pl.ds(at * wide, wide)
        now = jnp.dot(hidden_ref[:, span], down_ref[0, span, :], preferred_element_type=jnp.float32)
        if at == 0:
            out_ref[...] = now
        else:
            out_ref[...] += now
    out_ref[...] = out_ref[...] * scale


def take_inputs_in(made, block, gate, up):
    _, width, hidden_width = gate.shape
    rows = block.shape[0]
    hidden, gate, up = pl.pallas_call(
        first_kernel,
        out_shape=[made((rows, hidden_width), jnp.bfloat16)] + [made(gate.shape, gate.dtype)] * 2,
        in_specs=[IN_VMEM] + [IN_HBM] * 2,
        out_specs=[IN_VMEM] * 3,
        scratch_shapes=[
            pltpu.VMEM((2, rows, hidden_width), jnp.float32),
            pltpu.SemaphoreType.DMA((2, width // even_split(width, DEPTH_STEP))),
        ],
        compiler_params=pltpu.CompilerParams(vmem_limit_bytes=SCOPED_BYTES),
        cost_estimate=pl.CostEstimate(
            flops=4 * rows * width * hidden_width,
            bytes_accessed=4 * width * hidden_width,
            transcendentals=rows * hidden_width,
        ),
    )(made.pin(block), in_hbm(gate), in_hbm(up))
    return hidden, gate, up


def take_output_in(made, top_count, block, hidden, down):
    _, hidden_width, width = down.shape
    rows = block.shape[0]
    return pl.pallas_call(
        functools.partial(second_kernel, top_count),
        out_shape=[made((rows, width), jnp.float32), made(down.shape, down.dtype)],
        in_specs=[IN_VMEM] * 2 + [IN_HBM],
        out_specs=[IN_VMEM] * 2,
        scratch_shapes=[
            pltpu.SemaphoreType.DMA((hidden_width // even_split(hidden_width, HIDDEN_STEP),))
        ],
        compiler_params=pltpu.CompilerParams(vmem_limit_bytes=SCOPED_BYTES),
        cost_estimate=pl.CostEstimate(
            flops=2 * rows * width * hidden_width,
            bytes_accessed=2 * width * hidden_width,
            transcendentals=0,
        ),
    )(made.pin(block), made.pin(hidden), in_hbm(down))


class InVmem:
    def __call__(self, shape, dtype):
        return pltpu.VMEM(shape, dtype)

    def pin(self, array):
        return pltpu.with_memory_space_constraint(array, pltpu.VMEM)


class Anywhere:
    def __call__(self, shape, dtype):
        return jax.ShapeDtypeStruct(shape, dtype)

    def pin(self, array):
        return array


def add_rounded(*terms):
    return sum(term.astype(jnp.float32) for term in terms).astype(jnp.bfloat16)


def shards(tokens, expert_ids, gate_weights, w_gate, w_up, w_down):
    local, width = tokens.shape
    top_count = expert_ids.shape[1]
    devices = lax.axis_size("expert")
    ring = chip_ring(devices // 2)
    ways = (ring_pairs(ring, 1), ring_pairs(ring, -1))
    siblings = [(at, at ^ 1) for at in range(devices)]
    hops = (len(ring) // 2, (len(ring) - 1) // 2)
    own = (w_gate, w_up, w_down)
    weight_bytes = 2 * sum(array.size * array.dtype.itemsize for array in own)
    kept_bytes = weight_bytes + len(ring) * local * width * 6
    made = InVmem() if kept_bytes <= KEPT_BYTES else Anywhere()
    run = functools.partial(run_experts, made, top_count)
    after = lax.optimization_barrier

    def outward(block, way):
        return lax.ppermute(block, "expert", ways[way])

    def homeward(block, way):
        return lax.ppermute(block, "expert", ways[1 - way])

    first = pack_rows(tokens, expert_ids, gate_weights, made)
    other = tuple(lax.ppermute(array, "expert", siblings) for array in own)

    rows = {(0, 0): first}
    partial = {}
    if hops[0]:
        rows[0, 1] = outward(first, 0)
    hidden, gate, up = take_inputs_in(made, first, w_gate, w_up)
    if hops[1]:
        later, hidden = after((first, hidden))
        rows[1, 1] = outward(later, 1)
    partial[0, 0], down = take_output_in(made, top_count, first, hidden, w_down)
    own = (gate, up, down)
    if hops[0]:
        rows[0, 1], partial[0, 0] = after((rows[0, 1], partial[0, 0]))
    for hop in range(2, hops[0] + 1):
        rows[0, hop] = outward(rows[0, hop - 1], 0)
        keys = [(0, hop - 1)] + [(1, hop - 2)] * (hop > 2)
        results = run([rows[key] for key in keys], (0,), [own])
        rows[1, hop - 1], results = after((rows[1, hop - 1], results))
        partial.update(zip(keys, results))
        if hop <= hops[1]:
            rows[1, hop] = outward(rows[1, hop - 1], 1)
    keys = [key for key in rows if key not in partial]
    if keys:
        results = run([rows[key] for key in keys], (0, 1), [own, other])
        partial.update(zip(keys, results))

    def sibling_sums(keys, prior):
        return run([rows[key] for key in keys], (1,), [other], prior)

    if hops[0] < 2:
        partial[0, 0] = sibling_sums([(0, 0)], [partial[0, 0]])[0]
    arrived = [None, None]
    level = list(hops)
    while level[0]:
        values = [None, None]
        values[0] = add_rounded(partial[0, level[0]], *[x for x in arrived[:1] if x is not None])
        arrived[0] = homeward(values[0], 0)
        keys = [(way, at - 1) for way, at in enumerate(level) if at > 1]
        keys = [key for key in keys if key in partial and key != (1, hops[0] - 1)]
        keys += [(0, 0)] * (level[0] == 2)
        waiting = arrived[1] if arrived[1] is not None else partial.get((1, level[1]))
        if keys:
            prior, _ = after(([partial[key] for key in keys], values[0]))
            waiting, results = after((waiting, sibling_sums(keys, prior)))
            partial.update(zip(keys, results))
        if level[1]:
            values[1] = add_rounded(*([waiting] if arrived[1] is None else [waiting, partial[1, level[1]]]))
            arrived[1] = homeward(values[1], 1)
        elif arrived[1] is not None:
            arrived[1] = waiting
        level = [max(at - 1, 0) for at in level]
    total = partial[0, 0]
    if arrived[1] is not None:
        total, arrived[0] = after((total + arrived[1].astype(jnp.float32), arrived[0]))
    return add_rounded(total, *[value for value in arrived[:1] if value is not None])


def solution(mesh):
    placed = (
        P(("groups", "expert"), None),
        P(("groups", "expert"), None),
        P(("groups", "expert"), None),
        P("expert", None, None),
        P("expert", None, None),
        P("expert", None, None),
    )
    return jax.shard_map(
        shards, mesh=mesh, in_specs=placed, out_specs=P(("groups", "expert"), None), check_vma=False
    )
```

```python
import functools

import jax
import jax.numpy as jnp
from jax import lax
from jax.experimental import pallas as pl
from jax.experimental.pallas import tpu as pltpu
from jax.sharding import PartitionSpec as P

LANES = 128
IN_VMEM = pl.BlockSpec(memory_space=pltpu.VMEM)
IN_HBM = pl.BlockSpec(memory_space=pltpu.HBM)
DEPTH_STEP = 512
HIDDEN_STEP = 256
PASS_ROWS = 192
SCOPED_BYTES = 8 * 1024 * 1024
KEPT_BYTES = 32 * 1024 * 1024


def in_hbm(array):
    return pltpu.with_memory_space_constraint(array, pltpu.HBM)


def even_split(size, most):
    part = most
    while size % part:
        part //= 2
    return part


def chip_ring(chips):
    across = max(d for d in range(1, chips + 1) if chips % d == 0 and d * d <= chips)
    down = chips // across
    if across == 1 or down % 2:
        return list(range(chips))
    ring = []
    for row in range(down):
        columns = list(range(1, across))
        ring += [row * across + column for column in (columns if row % 2 == 0 else columns[::-1])]
    return [0] + ring + [row * across for row in range(down - 1, 0, -1)]


def ring_pairs(ring, way, hop):
    count = len(ring)
    step = 1 if way == 0 else -1
    pairs = []
    for at, chip in enumerate(ring):
        for core in (0, 1):
            if 2 * hop == count and core == 0 and hop > 1:
                continue
            arrival = 1 - core if way == 0 and hop == 1 else core
            if 2 * hop == count and arrival == 0:
                continue
            pairs.append((2 * chip + core, 2 * ring[(at + step) % count] + arrival))
    return pairs


def pack_kernel(tokens_ref, ids_ref, gates_ref, out_ref, ids_buf, gates_buf, sems):
    width = tokens_ref.shape[1]
    copies = [
        pltpu.make_async_copy(ids_ref, ids_buf, sems.at[0]),
        pltpu.make_async_copy(gates_ref, gates_buf, sems.at[1]),
        pltpu.make_async_copy(tokens_ref, out_ref.at[:, pl.ds(0, width)], sems.at[2]),
    ]
    for copy in copies:
        copy.start()
    for copy in copies[:2]:
        copy.wait()
    rest = gates_buf[...]
    parts = [ids_buf[...].astype(jnp.float32)]
    for _ in range(3):
        parts.append(rest.astype(jnp.bfloat16).astype(jnp.float32))
        rest = rest - parts[-1]
    stacked = jnp.concatenate(parts, axis=0)
    shape = (stacked.shape[0], out_ref.shape[1] - width)
    unit = lax.broadcasted_iota(jnp.int32, shape, 0) == lax.broadcasted_iota(jnp.int32, shape, 1)
    route = lax.dot_general(
        stacked.astype(jnp.bfloat16),
        unit.astype(jnp.float32).astype(jnp.bfloat16),
        (((0,), (0,)), ((), ())),
        preferred_element_type=jnp.float32,
    )
    out_ref[:, width:] = route.astype(jnp.bfloat16)
    copies[2].wait()


def pack_rows(tokens, expert_ids, gate_weights, made):
    rows, width = tokens.shape
    extra = -(-4 * expert_ids.shape[1] // LANES) * LANES
    ids, gates = expert_ids.T, gate_weights.T
    return pl.pallas_call(
        pack_kernel,
        out_shape=made((rows, width + extra), jnp.bfloat16),
        in_specs=[IN_HBM] * 3,
        out_specs=IN_VMEM,
        scratch_shapes=[
            pltpu.VMEM(ids.shape, ids.dtype),
            pltpu.VMEM(gates.shape, gates.dtype),
            pltpu.SemaphoreType.DMA((3,)),
        ],
        compiler_params=pltpu.CompilerParams(vmem_limit_bytes=SCOPED_BYTES),
    )(in_hbm(tokens), in_hbm(ids), in_hbm(gates))


def row_scale(route, expert, top_count):
    route = route.astype(jnp.float32)
    chosen = (route[:, :top_count] == expert.astype(jnp.float32)).astype(jnp.float32)
    weight = sum(route[:, top_count * part : top_count * (part + 1)] for part in (1, 2, 3))
    return jnp.sum(chosen * weight, axis=1, keepdims=True)


def expert_kernel(blocks, flips, with_prior, top_count, *refs):
    row_refs, refs = refs[:blocks], refs[blocks:]
    weight_refs, refs = refs[: 3 * len(flips)], refs[3 * len(flips) :]
    prior_refs, refs = (refs[:blocks], refs[blocks:]) if with_prior else ((), refs)
    out_refs, (rows_buf, total) = refs[:blocks], refs[blocks:]
    block_rows, width = out_refs[0].shape
    real = blocks * block_rows
    me = lax.axis_index("expert")
    for at in range(rows_buf.shape[0] // block_rows):
        rows_buf[pl.ds(at * block_rows, block_rows), :] = row_refs[at % blocks][...]
    for at in range(blocks if with_prior else 0):
        total[pl.ds(at * block_rows, block_rows), :] = prior_refs[at][...]
    rows = rows_buf[:, :width]
    for at, flip in enumerate(flips):
        gate_ref, up_ref, down_ref = weight_refs[3 * at : 3 * at + 3]
        scale = row_scale(rows_buf[:real, width:], me ^ flip, top_count)
        gate_part = jnp.dot(rows, gate_ref[0], preferred_element_type=jnp.float32)
        up_part = jnp.dot(rows, up_ref[0], preferred_element_type=jnp.float32)
        hidden = (gate_part / (1.0 + jnp.exp(-gate_part)) * up_part).astype(jnp.bfloat16)
        result = jnp.dot(hidden, down_ref[0], preferred_element_type=jnp.float32)[:real] * scale
        if at or with_prior:
            total[...] += result
        else:
            total[...] = result
    for at in range(blocks):
        out_refs[at][...] = total[pl.ds(at * block_rows, block_rows), :]


def run_experts(made, top_count, row_blocks, flips, weights, prior=()):
    blocks, experts = len(row_blocks), len(weights)
    block_rows, row_width = row_blocks[0].shape
    _, width, hidden_width = weights[0][0].shape
    total = blocks * block_rows
    padded = max(total, PASS_ROWS // block_rows * block_rows) if experts == 1 else total
    return pl.pallas_call(
        functools.partial(expert_kernel, blocks, flips, bool(prior), top_count),
        out_shape=[made((block_rows, width), jnp.float32)] * blocks,
        in_specs=[IN_VMEM] * (blocks + 3 * experts + len(prior)),
        out_specs=[IN_VMEM] * blocks,
        scratch_shapes=[
            pltpu.VMEM((padded, row_width), jnp.bfloat16),
            pltpu.VMEM((total, width), jnp.float32),
        ],
        compiler_params=pltpu.CompilerParams(vmem_limit_bytes=SCOPED_BYTES),
        cost_estimate=pl.CostEstimate(
            flops=6 * total * width * hidden_width * experts,
            bytes_accessed=2 * (3 * width * hidden_width * experts + 2 * total * width),
            transcendentals=total * hidden_width * experts,
        ),
    )(
        *(made.pin(block) for block in row_blocks),
        *(made.pin(array) for weight in weights for array in weight),
        *(made.pin(block) for block in prior),
    )


def first_kernel(rows_ref, gate_in, up_in, hidden_ref, gate_ref, up_ref, parts, sems):
    width = gate_ref.shape[1]
    deep = even_split(width, DEPTH_STEP)
    sides = ((gate_in, gate_ref), (up_in, up_ref))

    def copies(at):
        span = pl.ds(at * deep, deep)
        return [
            pltpu.make_async_copy(source.at[0, span, :], kept.at[0, span, :], sems.at[side, at])
            for side, (source, kept) in enumerate(sides)
        ]

    steps = width // deep
    for at in range(steps):
        for copy in copies(at):
            copy.start()
    for at in range(steps):
        for copy in copies(at):
            copy.wait()
        span = pl.ds(at * deep, deep)
        for side, (_, kept) in enumerate(sides):
            now = jnp.dot(rows_ref[:, span], kept[0, span, :], preferred_element_type=jnp.float32)
            if at == 0:
                parts[side] = now
            else:
                parts[side] += now
    gate_part, up_part = parts[0], parts[1]
    hidden_ref[...] = (gate_part / (1.0 + jnp.exp(-gate_part)) * up_part).astype(jnp.bfloat16)


def second_kernel(top_count, rows_ref, hidden_ref, down_in, out_ref, down_ref, sems):
    hidden_width, width = down_ref.shape[1:]
    wide = even_split(hidden_width, HIDDEN_STEP)

    def copy(at):
        span = pl.ds(at * wide, wide)
        return pltpu.make_async_copy(down_in.at[0, span, :], down_ref.at[0, span, :], sems.at[at])

    steps = hidden_width // wide
    for at in range(steps):
        copy(at).start()
    scale = row_scale(rows_ref[:, width:], lax.axis_index("expert"), top_count)
    for at in range(steps):
        copy(at).wait()
        span = pl.ds(at * wide, wide)
        now = jnp.dot(hidden_ref[:, span], down_ref[0, span, :], preferred_element_type=jnp.float32)
        if at == 0:
            out_ref[...] = now
        else:
            out_ref[...] += now
    out_ref[...] = out_ref[...] * scale


def take_inputs_in(made, block, gate, up):
    _, width, hidden_width = gate.shape
    rows = block.shape[0]
    hidden, gate, up = pl.pallas_call(
        first_kernel,
        out_shape=[made((rows, hidden_width), jnp.bfloat16)] + [made(gate.shape, gate.dtype)] * 2,
        in_specs=[IN_VMEM] + [IN_HBM] * 2,
        out_specs=[IN_VMEM] * 3,
        scratch_shapes=[
            pltpu.VMEM((2, rows, hidden_width), jnp.float32),
            pltpu.SemaphoreType.DMA((2, width // even_split(width, DEPTH_STEP))),
        ],
        compiler_params=pltpu.CompilerParams(vmem_limit_bytes=SCOPED_BYTES),
        cost_estimate=pl.CostEstimate(
            flops=4 * rows * width * hidden_width,
            bytes_accessed=4 * width * hidden_width,
            transcendentals=rows * hidden_width,
        ),
    )(made.pin(block), in_hbm(gate), in_hbm(up))
    return hidden, gate, up


def take_output_in(made, top_count, block, hidden, down):
    _, hidden_width, width = down.shape
    rows = block.shape[0]
    return pl.pallas_call(
        functools.partial(second_kernel, top_count),
        out_shape=[made((rows, width), jnp.float32), made(down.shape, down.dtype)],
        in_specs=[IN_VMEM] * 2 + [IN_HBM],
        out_specs=[IN_VMEM] * 2,
        scratch_shapes=[
            pltpu.SemaphoreType.DMA((hidden_width // even_split(hidden_width, HIDDEN_STEP),))
        ],
        compiler_params=pltpu.CompilerParams(vmem_limit_bytes=SCOPED_BYTES),
        cost_estimate=pl.CostEstimate(
            flops=2 * rows * width * hidden_width,
            bytes_accessed=2 * width * hidden_width,
            transcendentals=0,
        ),
    )(made.pin(block), made.pin(hidden), in_hbm(down))


class InVmem:
    def __call__(self, shape, dtype):
        return pltpu.VMEM(shape, dtype)

    def pin(self, array):
        return pltpu.with_memory_space_constraint(array, pltpu.VMEM)


class Anywhere:
    def __call__(self, shape, dtype):
        return jax.ShapeDtypeStruct(shape, dtype)

    def pin(self, array):
        return array


def add_rounded(*terms):
    return sum(term.astype(jnp.float32) for term in terms).astype(jnp.bfloat16)


def shards(tokens, expert_ids, gate_weights, w_gate, w_up, w_down):
    local, width = tokens.shape
    top_count = expert_ids.shape[1]
    devices = lax.axis_size("expert")
    ring = chip_ring(devices // 2)
    siblings = [(at, at ^ 1) for at in range(devices)]
    hops = (len(ring) // 2, len(ring) // 2)
    own = (w_gate, w_up, w_down)
    weight_bytes = 2 * sum(array.size * array.dtype.itemsize for array in own)
    kept_bytes = weight_bytes + len(ring) * local * width * 6
    made = InVmem() if kept_bytes <= KEPT_BYTES else Anywhere()
    run = functools.partial(run_experts, made, top_count)
    after = lax.optimization_barrier

    def outward(block, way, hop):
        return lax.ppermute(block, "expert", ring_pairs(ring, way, hop))

    def homeward(block, way, hop):
        back = [(target, source) for source, target in ring_pairs(ring, way, hop)]
        return lax.ppermute(block, "expert", back)

    first = pack_rows(tokens, expert_ids, gate_weights, made)
    other = tuple(lax.ppermute(array, "expert", siblings) for array in own)

    rows = {(0, 0): first}
    partial = {}
    if hops[0]:
        rows[0, 1] = outward(first, 0, 1)
    hidden, gate, up = take_inputs_in(made, first, w_gate, w_up)
    if hops[1]:
        later, hidden = after((first, hidden))
        rows[1, 1] = outward(later, 1, 1)
    partial[0, 0], down = take_output_in(made, top_count, first, hidden, w_down)
    own = (gate, up, down)
    if hops[0]:
        rows[0, 1], partial[0, 0] = after((rows[0, 1], partial[0, 0]))
    for hop in range(2, hops[0] + 1):
        rows[0, hop] = outward(rows[0, hop - 1], 0, hop)
        keys = [(0, hop - 1)] + [(1, hop - 2)] * (hop > 2)
        results = run([rows[key] for key in keys], (0,), [own])
        rows[1, hop - 1], results = after((rows[1, hop - 1], results))
        partial.update(zip(keys, results))
        if hop <= hops[1]:
            rows[1, hop] = outward(rows[1, hop - 1], 1, hop)
    keys = [key for key in rows if key not in partial]
    if keys:
        results = run([rows[key] for key in keys], (0, 1), [own, other])
        partial.update(zip(keys, results))

    def sibling_sums(keys, prior):
        return run([rows[key] for key in keys], (1,), [other], prior)

    if hops[0] < 2:
        partial[0, 0] = sibling_sums([(0, 0)], [partial[0, 0]])[0]
    arrived = [None, None]
    level = list(hops)
    while level[0]:
        values = [None, None]
        values[0] = add_rounded(partial[0, level[0]], *[x for x in arrived[:1] if x is not None])
        arrived[0] = homeward(values[0], 0, level[0])
        keys = [(way, at - 1) for way, at in enumerate(level) if at > 1]
        keys = [key for key in keys if key in partial and key != (1, hops[0] - 1)]
        keys += [(0, 0)] * (level[0] == 2)
        waiting = arrived[1] if arrived[1] is not None else partial.get((1, level[1]))
        if keys:
            prior, _ = after(([partial[key] for key in keys], values[0]))
            waiting, results = after((waiting, sibling_sums(keys, prior)))
            partial.update(zip(keys, results))
        if level[1]:
            values[1] = add_rounded(*([waiting] if arrived[1] is None else [waiting, partial[1, level[1]]]))
            arrived[1] = homeward(values[1], 1, level[1])
        elif arrived[1] is not None:
            arrived[1] = waiting
        level = [max(at - 1, 0) for at in level]
    total = partial[0, 0]
    if arrived[1] is not None:
        total, arrived[0] = after((total + arrived[1].astype(jnp.float32), arrived[0]))
    return add_rounded(total, *[value for value in arrived[:1] if value is not None])


def solution(mesh):
    placed = (
        P(("groups", "expert"), None),
        P(("groups", "expert"), None),
        P(("groups", "expert"), None),
        P("expert", None, None),
        P("expert", None, None),
        P("expert", None, None),
    )
    return jax.shard_map(
        shards, mesh=mesh, in_specs=placed, out_specs=P(("groups", "expert"), None), check_vma=False
    )
```

```python
import functools

import jax
import jax.numpy as jnp
from jax import lax
from jax.experimental import pallas as pl
from jax.experimental.pallas import tpu as pltpu
from jax.sharding import PartitionSpec as P

LANES = 128
IN_VMEM = pl.BlockSpec(memory_space=pltpu.VMEM)
IN_HBM = pl.BlockSpec(memory_space=pltpu.HBM)
DEPTH_STEP = 512
HIDDEN_STEP = 256
PASS_ROWS = 128
FIRST_ROWS = 256
SCOPED_BYTES = 8 * 1024 * 1024
KEPT_BYTES = 32 * 1024 * 1024


def in_hbm(array):
    return pltpu.with_memory_space_constraint(array, pltpu.HBM)


def even_split(size, most):
    part = most
    while size % part:
        part //= 2
    return part


def chip_ring(chips):
    across = max(d for d in range(1, chips + 1) if chips % d == 0 and d * d <= chips)
    down = chips // across
    if across == 1 or down % 2:
        return list(range(chips))
    ring = []
    for row in range(down):
        columns = list(range(1, across))
        ring += [row * across + column for column in (columns if row % 2 == 0 else columns[::-1])]
    return [0] + ring + [row * across for row in range(down - 1, 0, -1)]


def ring_pairs(ring, way):
    count = len(ring)
    pairs = []
    for at, chip in enumerate(ring):
        for core in (0, 1):
            step = way if core == at % 2 else -way
            pairs.append((2 * chip + core, 2 * ring[(at + step) % count] + 1 - core))
    return pairs


def pack_kernel(tokens_ref, ids_ref, gates_ref, out_ref, ids_buf, gates_buf, sems):
    width = tokens_ref.shape[1]
    copies = [
        pltpu.make_async_copy(ids_ref, ids_buf, sems.at[0]),
        pltpu.make_async_copy(gates_ref, gates_buf, sems.at[1]),
        pltpu.make_async_copy(tokens_ref, out_ref.at[:, pl.ds(0, width)], sems.at[2]),
    ]
    for copy in copies:
        copy.start()
    for copy in copies[:2]:
        copy.wait()
    rest = gates_buf[...]
    parts = [ids_buf[...].astype(jnp.float32)]
    for _ in range(3):
        parts.append(rest.astype(jnp.bfloat16).astype(jnp.float32))
        rest = rest - parts[-1]
    stacked = jnp.concatenate(parts, axis=0)
    shape = (stacked.shape[0], out_ref.shape[1] - width)
    unit = lax.broadcasted_iota(jnp.int32, shape, 0) == lax.broadcasted_iota(jnp.int32, shape, 1)
    route = lax.dot_general(
        stacked.astype(jnp.bfloat16),
        unit.astype(jnp.float32).astype(jnp.bfloat16),
        (((0,), (0,)), ((), ())),
        preferred_element_type=jnp.float32,
    )
    out_ref[:, width:] = route.astype(jnp.bfloat16)
    copies[2].wait()


def pack_rows(tokens, expert_ids, gate_weights, made):
    rows, width = tokens.shape
    extra = -(-4 * expert_ids.shape[1] // LANES) * LANES
    ids, gates = expert_ids.T, gate_weights.T
    return pl.pallas_call(
        pack_kernel,
        out_shape=made((rows, width + extra), jnp.bfloat16),
        in_specs=[IN_HBM] * 3,
        out_specs=IN_VMEM,
        scratch_shapes=[
            pltpu.VMEM(ids.shape, ids.dtype),
            pltpu.VMEM(gates.shape, gates.dtype),
            pltpu.SemaphoreType.DMA((3,)),
        ],
        compiler_params=pltpu.CompilerParams(vmem_limit_bytes=SCOPED_BYTES),
    )(in_hbm(tokens), in_hbm(ids), in_hbm(gates))


def row_scale(route, expert, top_count):
    route = route.astype(jnp.float32)
    chosen = (route[:, :top_count] == expert.astype(jnp.float32)).astype(jnp.float32)
    weight = sum(route[:, top_count * part : top_count * (part + 1)] for part in (1, 2, 3))
    return jnp.sum(chosen * weight, axis=1, keepdims=True)


def expert_kernel(blocks, flips, with_prior, top_count, *refs):
    row_refs, refs = refs[:blocks], refs[blocks:]
    weight_refs, refs = refs[: 3 * len(flips)], refs[3 * len(flips) :]
    prior_refs, refs = (refs[:blocks], refs[blocks:]) if with_prior else ((), refs)
    out_refs, (rows_buf, total) = refs[:blocks], refs[blocks:]
    block_rows, width = out_refs[0].shape
    real = blocks * block_rows
    me = lax.axis_index("expert")
    for at in range(rows_buf.shape[0] // block_rows):
        rows_buf[pl.ds(at * block_rows, block_rows), :] = row_refs[at % blocks][...]
    for at in range(blocks if with_prior else 0):
        total[pl.ds(at * block_rows, block_rows), :] = prior_refs[at][...]
    rows = rows_buf[:, :width]
    for at, flip in enumerate(flips):
        gate_ref, up_ref, down_ref = weight_refs[3 * at : 3 * at + 3]
        scale = row_scale(rows_buf[:real, width:], me ^ flip, top_count)
        gate_part = jnp.dot(rows, gate_ref[0], preferred_element_type=jnp.float32)
        up_part = jnp.dot(rows, up_ref[0], preferred_element_type=jnp.float32)
        hidden = (gate_part / (1.0 + jnp.exp(-gate_part)) * up_part).astype(jnp.bfloat16)
        result = jnp.dot(hidden, down_ref[0], preferred_element_type=jnp.float32)[:real] * scale
        if at or with_prior:
            total[...] += result
        else:
            total[...] = result
    for at in range(blocks):
        out_refs[at][...] = total[pl.ds(at * block_rows, block_rows), :]


def run_experts(made, top_count, row_blocks, flips, weights, prior=(), least=PASS_ROWS):
    blocks, experts = len(row_blocks), len(weights)
    block_rows, row_width = row_blocks[0].shape
    _, width, hidden_width = weights[0][0].shape
    total = blocks * block_rows
    padded = max(total, least // block_rows * block_rows) if experts == 1 else total
    return pl.pallas_call(
        functools.partial(expert_kernel, blocks, flips, bool(prior), top_count),
        out_shape=[made((block_rows, width), jnp.float32)] * blocks,
        in_specs=[IN_VMEM] * (blocks + 3 * experts + len(prior)),
        out_specs=[IN_VMEM] * blocks,
        scratch_shapes=[
            pltpu.VMEM((padded, row_width), jnp.bfloat16),
            pltpu.VMEM((total, width), jnp.float32),
        ],
        compiler_params=pltpu.CompilerParams(vmem_limit_bytes=SCOPED_BYTES),
        cost_estimate=pl.CostEstimate(
            flops=6 * total * width * hidden_width * experts,
            bytes_accessed=2 * (3 * width * hidden_width * experts + 2 * total * width),
            transcendentals=total * hidden_width * experts,
        ),
    )(
        *(made.pin(block) for block in row_blocks),
        *(made.pin(array) for weight in weights for array in weight),
        *(made.pin(block) for block in prior),
    )


def first_kernel(rows_ref, gate_in, up_in, hidden_ref, gate_ref, up_ref, parts, sems):
    width = gate_ref.shape[1]
    deep = even_split(width, DEPTH_STEP)
    sides = ((gate_in, gate_ref), (up_in, up_ref))

    def copies(at):
        span = pl.ds(at * deep, deep)
        return [
            pltpu.make_async_copy(source.at[0, span, :], kept.at[0, span, :], sems.at[side, at])
            for side, (source, kept) in enumerate(sides)
        ]

    steps = width // deep
    for at in range(steps):
        for copy in copies(at):
            copy.start()
    for at in range(steps):
        for copy in copies(at):
            copy.wait()
        span = pl.ds(at * deep, deep)
        for side, (_, kept) in enumerate(sides):
            now = jnp.dot(rows_ref[:, span], kept[0, span, :], preferred_element_type=jnp.float32)
            if at == 0:
                parts[side] = now
            else:
                parts[side] += now
    gate_part, up_part = parts[0], parts[1]
    hidden_ref[...] = (gate_part / (1.0 + jnp.exp(-gate_part)) * up_part).astype(jnp.bfloat16)


def second_kernel(top_count, rows_ref, hidden_ref, down_in, out_ref, down_ref, sems):
    hidden_width, width = down_ref.shape[1:]
    wide = even_split(hidden_width, HIDDEN_STEP)

    def copy(at):
        span = pl.ds(at * wide, wide)
        return pltpu.make_async_copy(down_in.at[0, span, :], down_ref.at[0, span, :], sems.at[at])

    steps = hidden_width // wide
    for at in range(steps):
        copy(at).start()
    scale = row_scale(rows_ref[:, width:], lax.axis_index("expert"), top_count)
    for at in range(steps):
        copy(at).wait()
        span = pl.ds(at * wide, wide)
        now = jnp.dot(hidden_ref[:, span], down_ref[0, span, :], preferred_element_type=jnp.float32)
        if at == 0:
            out_ref[...] = now
        else:
            out_ref[...] += now
    out_ref[...] = out_ref[...] * scale


def take_inputs_in(made, block, gate, up):
    _, width, hidden_width = gate.shape
    rows = block.shape[0]
    hidden, gate, up = pl.pallas_call(
        first_kernel,
        out_shape=[made((rows, hidden_width), jnp.bfloat16)] + [made(gate.shape, gate.dtype)] * 2,
        in_specs=[IN_VMEM] + [IN_HBM] * 2,
        out_specs=[IN_VMEM] * 3,
        scratch_shapes=[
            pltpu.VMEM((2, rows, hidden_width), jnp.float32),
            pltpu.SemaphoreType.DMA((2, width // even_split(width, DEPTH_STEP))),
        ],
        compiler_params=pltpu.CompilerParams(vmem_limit_bytes=SCOPED_BYTES),
        cost_estimate=pl.CostEstimate(
            flops=4 * rows * width * hidden_width,
            bytes_accessed=4 * width * hidden_width,
            transcendentals=rows * hidden_width,
        ),
    )(made.pin(block), in_hbm(gate), in_hbm(up))
    return hidden, gate, up


def take_output_in(made, top_count, block, hidden, down):
    _, hidden_width, width = down.shape
    rows = block.shape[0]
    return pl.pallas_call(
        functools.partial(second_kernel, top_count),
        out_shape=[made((rows, width), jnp.float32), made(down.shape, down.dtype)],
        in_specs=[IN_VMEM] * 2 + [IN_HBM],
        out_specs=[IN_VMEM] * 2,
        scratch_shapes=[
            pltpu.SemaphoreType.DMA((hidden_width // even_split(hidden_width, HIDDEN_STEP),))
        ],
        compiler_params=pltpu.CompilerParams(vmem_limit_bytes=SCOPED_BYTES),
        cost_estimate=pl.CostEstimate(
            flops=2 * rows * width * hidden_width,
            bytes_accessed=2 * width * hidden_width,
            transcendentals=0,
        ),
    )(made.pin(block), made.pin(hidden), in_hbm(down))


class InVmem:
    def __call__(self, shape, dtype):
        return pltpu.VMEM(shape, dtype)

    def pin(self, array):
        return pltpu.with_memory_space_constraint(array, pltpu.VMEM)


class Anywhere:
    def __call__(self, shape, dtype):
        return jax.ShapeDtypeStruct(shape, dtype)

    def pin(self, array):
        return array


def add_rounded(*terms):
    return sum(term.astype(jnp.float32) for term in terms).astype(jnp.bfloat16)


def shards(tokens, expert_ids, gate_weights, w_gate, w_up, w_down):
    local, width = tokens.shape
    top_count = expert_ids.shape[1]
    devices = lax.axis_size("expert")
    ring = chip_ring(devices // 2)
    ways = (ring_pairs(ring, 1), ring_pairs(ring, -1))
    siblings = [(at, at ^ 1) for at in range(devices)]
    hops = (len(ring) // 2, (len(ring) - 1) // 2)
    own = (w_gate, w_up, w_down)
    weight_bytes = 2 * sum(array.size * array.dtype.itemsize for array in own)
    kept_bytes = weight_bytes + len(ring) * local * width * 6
    made = InVmem() if kept_bytes <= KEPT_BYTES else Anywhere()
    run = functools.partial(run_experts, made, top_count)
    after = lax.optimization_barrier

    def outward(block, way):
        return lax.ppermute(block, "expert", ways[way])

    def homeward(block, way):
        return lax.ppermute(block, "expert", ways[1 - way])

    first = pack_rows(tokens, expert_ids, gate_weights, made)
    other = tuple(lax.ppermute(array, "expert", siblings) for array in own)

    rows = {(0, 0): first}
    partial = {}
    if hops[0]:
        rows[0, 1] = outward(first, 0)
    hidden, gate, up = take_inputs_in(made, first, w_gate, w_up)
    if hops[1]:
        later, hidden = after((first, hidden))
        rows[1, 1] = outward(later, 1)
    partial[0, 0], down = take_output_in(made, top_count, first, hidden, w_down)
    own = (gate, up, down)
    if hops[0]:
        rows[0, 1], partial[0, 0] = after((rows[0, 1], partial[0, 0]))
    for hop in range(2, hops[0] + 1):
        rows[0, hop] = outward(rows[0, hop - 1], 0)
        keys = [(0, hop - 1)] + [(1, hop - 2)] * (hop > 2)
        results = run([rows[key] for key in keys], (0,), [own])
        rows[1, hop - 1], results = after((rows[1, hop - 1], results))
        partial.update(zip(keys, results))
        if hop <= hops[1]:
            rows[1, hop] = outward(rows[1, hop - 1], 1)
    keys = [key for key in rows if key not in partial]
    if keys:
        results = run([rows[key] for key in keys], (0, 1), [own, other])
        partial.update(zip(keys, results))

    def sibling_sums(keys, prior, least=PASS_ROWS):
        return run([rows[key] for key in keys], (1,), [other], prior, least)

    if hops[0] < 2:
        partial[0, 0] = sibling_sums([(0, 0)], [partial[0, 0]])[0]
    arrived = [None, None]
    level = list(hops)
    while level[0]:
        values = [None, None]
        values[0] = add_rounded(partial[0, level[0]], *[x for x in arrived[:1] if x is not None])
        arrived[0] = homeward(values[0], 0)
        keys = [(way, at - 1) for way, at in enumerate(level) if at > 1]
        keys = [key for key in keys if key in partial and key != (1, hops[0] - 1)]
        keys += [(0, 0)] * (level[0] == 2)
        waiting = arrived[1] if arrived[1] is not None else partial.get((1, level[1]))
        if keys:
            prior, _ = after(([partial[key] for key in keys], values[0]))
            least = FIRST_ROWS if level[0] == hops[0] else PASS_ROWS
            waiting, results = after((waiting, sibling_sums(keys, prior, least)))
            partial.update(zip(keys, results))
        if level[1]:
            values[1] = add_rounded(*([waiting] if arrived[1] is None else [waiting, partial[1, level[1]]]))
            arrived[1] = homeward(values[1], 1)
        elif arrived[1] is not None:
            arrived[1] = waiting
        level = [max(at - 1, 0) for at in level]
    total = partial[0, 0]
    if arrived[1] is not None:
        total, arrived[0] = after((total + arrived[1].astype(jnp.float32), arrived[0]))
    return add_rounded(total, *[value for value in arrived[:1] if value is not None])


def solution(mesh):
    placed = (
        P(("groups", "expert"), None),
        P(("groups", "expert"), None),
        P(("groups", "expert"), None),
        P("expert", None, None),
        P("expert", None, None),
        P("expert", None, None),
    )
    return jax.shard_map(
        shards, mesh=mesh, in_specs=placed, out_specs=P(("groups", "expert"), None), check_vma=False
    )
```

```python
import functools

import jax
import jax.numpy as jnp
from jax import lax
from jax.experimental import pallas as pl
from jax.experimental.pallas import tpu as pltpu
from jax.sharding import PartitionSpec as P

LANES = 128
IN_VMEM = pl.BlockSpec(memory_space=pltpu.VMEM)
IN_HBM = pl.BlockSpec(memory_space=pltpu.HBM)
DEPTH_STEP = 512
HIDDEN_STEP = 256
PASS_ROWS = 256
SCOPED_BYTES = 8 * 1024 * 1024
KEPT_BYTES = 32 * 1024 * 1024


def in_hbm(array):
    return pltpu.with_memory_space_constraint(array, pltpu.HBM)


def even_split(size, most):
    part = most
    while size % part:
        part //= 2
    return part


def chip_ring(chips):
    across = max(d for d in range(1, chips + 1) if chips % d == 0 and d * d <= chips)
    down = chips // across
    if across == 1 or down % 2:
        return list(range(chips))
    ring = []
    for row in range(down):
        columns = list(range(1, across))
        ring += [row * across + column for column in (columns if row % 2 == 0 else columns[::-1])]
    return [0] + ring + [row * across for row in range(down - 1, 0, -1)]


def ring_pairs(ring, way):
    count = len(ring)
    pairs = []
    for at, chip in enumerate(ring):
        for core in (0, 1):
            step = way if core == at % 2 else -way
            pairs.append((2 * chip + core, 2 * ring[(at + step) % count] + 1 - core))
    return pairs


def pack_kernel(tokens_ref, ids_ref, gates_ref, out_ref, ids_buf, gates_buf, sems):
    width = tokens_ref.shape[1]
    copies = [
        pltpu.make_async_copy(ids_ref, ids_buf, sems.at[0]),
        pltpu.make_async_copy(gates_ref, gates_buf, sems.at[1]),
        pltpu.make_async_copy(tokens_ref, out_ref.at[:, pl.ds(0, width)], sems.at[2]),
    ]
    for copy in copies:
        copy.start()
    for copy in copies[:2]:
        copy.wait()
    rest = gates_buf[...]
    parts = [ids_buf[...].astype(jnp.float32)]
    for _ in range(3):
        parts.append(rest.astype(jnp.bfloat16).astype(jnp.float32))
        rest = rest - parts[-1]
    stacked = jnp.concatenate(parts, axis=0)
    shape = (stacked.shape[0], out_ref.shape[1] - width)
    unit = lax.broadcasted_iota(jnp.int32, shape, 0) == lax.broadcasted_iota(jnp.int32, shape, 1)
    route = lax.dot_general(
        stacked.astype(jnp.bfloat16),
        unit.astype(jnp.float32).astype(jnp.bfloat16),
        (((0,), (0,)), ((), ())),
        preferred_element_type=jnp.float32,
    )
    out_ref[:, width:] = route.astype(jnp.bfloat16)
    copies[2].wait()


def pack_rows(tokens, expert_ids, gate_weights, made):
    rows, width = tokens.shape
    extra = -(-4 * expert_ids.shape[1] // LANES) * LANES
    ids, gates = expert_ids.T, gate_weights.T
    return pl.pallas_call(
        pack_kernel,
        out_shape=made((rows, width + extra), jnp.bfloat16),
        in_specs=[IN_HBM] * 3,
        out_specs=IN_VMEM,
        scratch_shapes=[
            pltpu.VMEM(ids.shape, ids.dtype),
            pltpu.VMEM(gates.shape, gates.dtype),
            pltpu.SemaphoreType.DMA((3,)),
        ],
        compiler_params=pltpu.CompilerParams(vmem_limit_bytes=SCOPED_BYTES),
    )(in_hbm(tokens), in_hbm(ids), in_hbm(gates))


def row_scale(route, expert, top_count):
    route = route.astype(jnp.float32)
    chosen = (route[:, :top_count] == expert.astype(jnp.float32)).astype(jnp.float32)
    weight = sum(route[:, top_count * part : top_count * (part + 1)] for part in (1, 2, 3))
    return jnp.sum(chosen * weight, axis=1, keepdims=True)


def expert_kernel(blocks, flips, with_prior, top_count, *refs):
    row_refs, refs = refs[:blocks], refs[blocks:]
    weight_refs, refs = refs[: 3 * len(flips)], refs[3 * len(flips) :]
    prior_refs, refs = (refs[:blocks], refs[blocks:]) if with_prior else ((), refs)
    out_refs, (rows_buf, total) = refs[:blocks], refs[blocks:]
    block_rows, width = out_refs[0].shape
    real = blocks * block_rows
    me = lax.axis_index("expert")
    for at in range(rows_buf.shape[0] // block_rows):
        rows_buf[pl.ds(at * block_rows, block_rows), :] = row_refs[at % blocks][...]
    for at in range(blocks if with_prior else 0):
        total[pl.ds(at * block_rows, block_rows), :] = prior_refs[at][...]
    rows = rows_buf[:, :width]
    for at, flip in enumerate(flips):
        gate_ref, up_ref, down_ref = weight_refs[3 * at : 3 * at + 3]
        scale = row_scale(rows_buf[:real, width:], me ^ flip, top_count)
        gate_part = jnp.dot(rows, gate_ref[0], preferred_element_type=jnp.float32)
        up_part = jnp.dot(rows, up_ref[0], preferred_element_type=jnp.float32)
        hidden = (gate_part / (1.0 + jnp.exp(-gate_part)) * up_part).astype(jnp.bfloat16)
        result = jnp.dot(hidden, down_ref[0], preferred_element_type=jnp.float32)[:real] * scale
        if at or with_prior:
            total[...] += result
        else:
            total[...] = result
    for at in range(blocks):
        out_refs[at][...] = total[pl.ds(at * block_rows, block_rows), :]


def run_experts(made, top_count, row_blocks, flips, weights, prior=()):
    blocks, experts = len(row_blocks), len(weights)
    block_rows, row_width = row_blocks[0].shape
    _, width, hidden_width = weights[0][0].shape
    total = blocks * block_rows
    padded = max(total, PASS_ROWS // block_rows * block_rows) if experts == 1 else total
    return pl.pallas_call(
        functools.partial(expert_kernel, blocks, flips, bool(prior), top_count),
        out_shape=[made((block_rows, width), jnp.float32)] * blocks,
        in_specs=[IN_VMEM] * (blocks + 3 * experts + len(prior)),
        out_specs=[IN_VMEM] * blocks,
        scratch_shapes=[
            pltpu.VMEM((padded, row_width), jnp.bfloat16),
            pltpu.VMEM((total, width), jnp.float32),
        ],
        compiler_params=pltpu.CompilerParams(vmem_limit_bytes=SCOPED_BYTES),
        cost_estimate=pl.CostEstimate(
            flops=6 * total * width * hidden_width * experts,
            bytes_accessed=2 * (3 * width * hidden_width * experts + 2 * total * width),
            transcendentals=total * hidden_width * experts,
        ),
    )(
        *(made.pin(block) for block in row_blocks),
        *(made.pin(array) for weight in weights for array in weight),
        *(made.pin(block) for block in prior),
    )


def first_kernel(rows_ref, gate_in, up_in, hidden_ref, gate_ref, up_ref, parts, sems):
    width = gate_ref.shape[1]
    deep = even_split(width, DEPTH_STEP)
    sides = ((gate_in, gate_ref), (up_in, up_ref))

    def copies(at):
        span = pl.ds(at * deep, deep)
        return [
            pltpu.make_async_copy(source.at[0, span, :], kept.at[0, span, :], sems.at[side, at])
            for side, (source, kept) in enumerate(sides)
        ]

    steps = width // deep
    for at in range(steps):
        for copy in copies(at):
            copy.start()
    for at in range(steps):
        for copy in copies(at):
            copy.wait()
        span = pl.ds(at * deep, deep)
        for side, (_, kept) in enumerate(sides):
            now = jnp.dot(rows_ref[:, span], kept[0, span, :], preferred_element_type=jnp.float32)
            if at == 0:
                parts[side] = now
            else:
                parts[side] += now
    gate_part, up_part = parts[0], parts[1]
    hidden_ref[...] = (gate_part / (1.0 + jnp.exp(-gate_part)) * up_part).astype(jnp.bfloat16)


def second_kernel(top_count, rows_ref, hidden_ref, down_in, out_ref, down_ref, sems):
    hidden_width, width = down_ref.shape[1:]
    wide = even_split(hidden_width, HIDDEN_STEP)

    def copy(at):
        span = pl.ds(at * wide, wide)
        return pltpu.make_async_copy(down_in.at[0, span, :], down_ref.at[0, span, :], sems.at[at])

    steps = hidden_width // wide
    for at in range(steps):
        copy(at).start()
    scale = row_scale(rows_ref[:, width:], lax.axis_index("expert"), top_count)
    for at in range(steps):
        copy(at).wait()
        span = pl.ds(at * wide, wide)
        now = jnp.dot(hidden_ref[:, span], down_ref[0, span, :], preferred_element_type=jnp.float32)
        if at == 0:
            out_ref[...] = now
        else:
            out_ref[...] += now
    out_ref[...] = out_ref[...] * scale


def take_inputs_in(made, block, gate, up):
    _, width, hidden_width = gate.shape
    rows = block.shape[0]
    hidden, gate, up = pl.pallas_call(
        first_kernel,
        out_shape=[made((rows, hidden_width), jnp.bfloat16)] + [made(gate.shape, gate.dtype)] * 2,
        in_specs=[IN_VMEM] + [IN_HBM] * 2,
        out_specs=[IN_VMEM] * 3,
        scratch_shapes=[
            pltpu.VMEM((2, rows, hidden_width), jnp.float32),
            pltpu.SemaphoreType.DMA((2, width // even_split(width, DEPTH_STEP))),
        ],
        compiler_params=pltpu.CompilerParams(vmem_limit_bytes=SCOPED_BYTES),
        cost_estimate=pl.CostEstimate(
            flops=4 * rows * width * hidden_width,
            bytes_accessed=4 * width * hidden_width,
            transcendentals=rows * hidden_width,
        ),
    )(made.pin(block), in_hbm(gate), in_hbm(up))
    return hidden, gate, up


def take_output_in(made, top_count, block, hidden, down):
    _, hidden_width, width = down.shape
    rows = block.shape[0]
    return pl.pallas_call(
        functools.partial(second_kernel, top_count),
        out_shape=[made((rows, width), jnp.float32), made(down.shape, down.dtype)],
        in_specs=[IN_VMEM] * 2 + [IN_HBM],
        out_specs=[IN_VMEM] * 2,
        scratch_shapes=[
            pltpu.SemaphoreType.DMA((hidden_width // even_split(hidden_width, HIDDEN_STEP),))
        ],
        compiler_params=pltpu.CompilerParams(vmem_limit_bytes=SCOPED_BYTES),
        cost_estimate=pl.CostEstimate(
            flops=2 * rows * width * hidden_width,
            bytes_accessed=2 * width * hidden_width,
            transcendentals=0,
        ),
    )(made.pin(block), made.pin(hidden), in_hbm(down))


class InVmem:
    def __call__(self, shape, dtype):
        return pltpu.VMEM(shape, dtype)

    def pin(self, array):
        return pltpu.with_memory_space_constraint(array, pltpu.VMEM)


class Anywhere:
    def __call__(self, shape, dtype):
        return jax.ShapeDtypeStruct(shape, dtype)

    def pin(self, array):
        return array


def add_rounded(*terms):
    return sum(term.astype(jnp.float32) for term in terms).astype(jnp.bfloat16)


def shards(tokens, expert_ids, gate_weights, w_gate, w_up, w_down):
    local, width = tokens.shape
    top_count = expert_ids.shape[1]
    devices = lax.axis_size("expert")
    ring = chip_ring(devices // 2)
    ways = (ring_pairs(ring, 1), ring_pairs(ring, -1))
    siblings = [(at, at ^ 1) for at in range(devices)]
    hops = (len(ring) // 2, (len(ring) - 1) // 2)
    own = (w_gate, w_up, w_down)
    weight_bytes = 2 * sum(array.size * array.dtype.itemsize for array in own)
    kept_bytes = weight_bytes + len(ring) * local * width * 6
    made = InVmem() if kept_bytes <= KEPT_BYTES else Anywhere()
    run = functools.partial(run_experts, made, top_count)
    after = lax.optimization_barrier

    def outward(block, way):
        return lax.ppermute(block, "expert", ways[way])

    def homeward(block, way):
        return lax.ppermute(block, "expert", ways[1 - way])

    first = pack_rows(tokens, expert_ids, gate_weights, made)
    other = tuple(lax.ppermute(array, "expert", siblings) for array in own)

    rows = {(0, 0): first}
    partial = {}
    if hops[0]:
        rows[0, 1] = outward(first, 0)
    hidden, gate, up = take_inputs_in(made, first, w_gate, w_up)
    if hops[1]:
        later, hidden = after((first, hidden))
        rows[1, 1] = outward(later, 1)
    partial[0, 0], down = take_output_in(made, top_count, first, hidden, w_down)
    own = (gate, up, down)
    if hops[0]:
        rows[0, 1], partial[0, 0] = after((rows[0, 1], partial[0, 0]))
    for hop in range(2, hops[0] + 1):
        rows[0, hop] = outward(rows[0, hop - 1], 0)
        keys = [(0, hop - 1)] + [(1, hop - 2)] * (hop > 2)
        results = run([rows[key] for key in keys], (0,), [own])
        rows[1, hop - 1], results = after((rows[1, hop - 1], results))
        partial.update(zip(keys, results))
        if hop <= hops[1]:
            rows[1, hop] = outward(rows[1, hop - 1], 1)
    keys = [key for key in rows if key not in partial]
    if keys:
        results = run([rows[key] for key in keys], (0, 1), [own, other])
        partial.update(zip(keys, results))

    def sibling_sums(keys, prior):
        return run([rows[key] for key in keys], (1,), [other], prior)

    if hops[0] < 2:
        partial[0, 0] = sibling_sums([(0, 0)], [partial[0, 0]])[0]
    arrived = [None, None]
    level = list(hops)
    while level[0]:
        values = [None, None]
        values[0] = add_rounded(partial[0, level[0]], *[x for x in arrived[:1] if x is not None])
        arrived[0] = homeward(values[0], 0)
        keys = [(way, at - 1) for way, at in enumerate(level) if at > 1]
        keys = [key for key in keys if key in partial and key != (1, hops[0] - 1)]
        keys += [(0, 0)] * (level[0] == 2)
        waiting = arrived[1] if arrived[1] is not None else partial.get((1, level[1]))
        if keys:
            prior, _ = after(([partial[key] for key in keys], values[0]))
            waiting, results = after((waiting, sibling_sums(keys, prior)))
            partial.update(zip(keys, results))
        if level[1]:
            values[1] = add_rounded(*([waiting] if arrived[1] is None else [waiting, partial[1, level[1]]]))
            arrived[1] = homeward(values[1], 1)
        elif arrived[1] is not None:
            arrived[1] = waiting
        level = [max(at - 1, 0) for at in level]
    total = partial[0, 0]
    if arrived[1] is not None:
        total, arrived[0] = after((total + arrived[1].astype(jnp.float32), arrived[0]))
    return add_rounded(total, *[value for value in arrived[:1] if value is not None])


def solution(mesh):
    placed = (
        P(("groups", "expert"), None),
        P(("groups", "expert"), None),
        P(("groups", "expert"), None),
        P("expert", None, None),
        P("expert", None, None),
        P("expert", None, None),
    )
    return jax.shard_map(
        shards, mesh=mesh, in_specs=placed, out_specs=P(("groups", "expert"), None), check_vma=False
    )
```

```python
import functools

import jax
import jax.numpy as jnp
from jax import lax
from jax.experimental import pallas as pl
from jax.experimental.pallas import tpu as pltpu
from jax.sharding import PartitionSpec as P

LANES = 128
IN_VMEM = pl.BlockSpec(memory_space=pltpu.VMEM)
IN_HBM = pl.BlockSpec(memory_space=pltpu.HBM)
DEPTH_STEP = 512
HIDDEN_STEP = 256
PASS_ROWS = 192
SCOPED_BYTES = 8 * 1024 * 1024
KEPT_BYTES = 32 * 1024 * 1024


def in_hbm(array):
    return pltpu.with_memory_space_constraint(array, pltpu.HBM)


def even_split(size, most):
    part = most
    while size % part:
        part //= 2
    return part


def chip_ring(chips):
    across = max(d for d in range(1, chips + 1) if chips % d == 0 and d * d <= chips)
    down = chips // across
    if across == 1 or down % 2:
        return list(range(chips))
    ring = []
    for row in range(down):
        columns = list(range(1, across))
        ring += [row * across + column for column in (columns if row % 2 == 0 else columns[::-1])]
    return [0] + ring + [row * across for row in range(down - 1, 0, -1)]


def ring_pairs(ring, way):
    count = len(ring)
    pairs = []
    for at, chip in enumerate(ring):
        for core in (0, 1):
            step = -way if core == at % 2 else way
            pairs.append((2 * chip + core, 2 * ring[(at + step) % count] + 1 - core))
    return pairs


def pack_kernel(tokens_ref, ids_ref, gates_ref, out_ref, ids_buf, gates_buf, sems):
    width = tokens_ref.shape[1]
    copies = [
        pltpu.make_async_copy(ids_ref, ids_buf, sems.at[0]),
        pltpu.make_async_copy(gates_ref, gates_buf, sems.at[1]),
        pltpu.make_async_copy(tokens_ref, out_ref.at[:, pl.ds(0, width)], sems.at[2]),
    ]
    for copy in copies:
        copy.start()
    for copy in copies[:2]:
        copy.wait()
    rest = gates_buf[...]
    parts = [ids_buf[...].astype(jnp.float32)]
    for _ in range(3):
        parts.append(rest.astype(jnp.bfloat16).astype(jnp.float32))
        rest = rest - parts[-1]
    stacked = jnp.concatenate(parts, axis=0)
    shape = (stacked.shape[0], out_ref.shape[1] - width)
    unit = lax.broadcasted_iota(jnp.int32, shape, 0) == lax.broadcasted_iota(jnp.int32, shape, 1)
    route = lax.dot_general(
        stacked.astype(jnp.bfloat16),
        unit.astype(jnp.float32).astype(jnp.bfloat16),
        (((0,), (0,)), ((), ())),
        preferred_element_type=jnp.float32,
    )
    out_ref[:, width:] = route.astype(jnp.bfloat16)
    copies[2].wait()


def pack_rows(tokens, expert_ids, gate_weights, made):
    rows, width = tokens.shape
    extra = -(-4 * expert_ids.shape[1] // LANES) * LANES
    ids, gates = expert_ids.T, gate_weights.T
    return pl.pallas_call(
        pack_kernel,
        out_shape=made((rows, width + extra), jnp.bfloat16),
        in_specs=[IN_HBM] * 3,
        out_specs=IN_VMEM,
        scratch_shapes=[
            pltpu.VMEM(ids.shape, ids.dtype),
            pltpu.VMEM(gates.shape, gates.dtype),
            pltpu.SemaphoreType.DMA((3,)),
        ],
        compiler_params=pltpu.CompilerParams(vmem_limit_bytes=SCOPED_BYTES),
    )(in_hbm(tokens), in_hbm(ids), in_hbm(gates))


def row_scale(route, expert, top_count):
    route = route.astype(jnp.float32)
    chosen = (route[:, :top_count] == expert.astype(jnp.float32)).astype(jnp.float32)
    weight = sum(route[:, top_count * part : top_count * (part + 1)] for part in (1, 2, 3))
    return jnp.sum(chosen * weight, axis=1, keepdims=True)


def expert_kernel(blocks, flips, with_prior, top_count, *refs):
    row_refs, refs = refs[:blocks], refs[blocks:]
    weight_refs, refs = refs[: 3 * len(flips)], refs[3 * len(flips) :]
    prior_refs, refs = (refs[:blocks], refs[blocks:]) if with_prior else ((), refs)
    out_refs, (rows_buf, total) = refs[:blocks], refs[blocks:]
    block_rows, width = out_refs[0].shape
    real = blocks * block_rows
    me = lax.axis_index("expert")
    for at in range(rows_buf.shape[0] // block_rows):
        rows_buf[pl.ds(at * block_rows, block_rows), :] = row_refs[at % blocks][...]
    for at in range(blocks if with_prior else 0):
        total[pl.ds(at * block_rows, block_rows), :] = prior_refs[at][...]
    rows = rows_buf[:, :width]
    for at, flip in enumerate(flips):
        gate_ref, up_ref, down_ref = weight_refs[3 * at : 3 * at + 3]
        scale = row_scale(rows_buf[:real, width:], me ^ flip, top_count)
        gate_part = jnp.dot(rows, gate_ref[0], preferred_element_type=jnp.float32)
        up_part = jnp.dot(rows, up_ref[0], preferred_element_type=jnp.float32)
        hidden = (gate_part / (1.0 + jnp.exp(-gate_part)) * up_part).astype(jnp.bfloat16)
        result = jnp.dot(hidden, down_ref[0], preferred_element_type=jnp.float32)[:real] * scale
        if at or with_prior:
            total[...] += result
        else:
            total[...] = result
    for at in range(blocks):
        out_refs[at][...] = total[pl.ds(at * block_rows, block_rows), :]


def run_experts(made, top_count, row_blocks, flips, weights, prior=()):
    blocks, experts = len(row_blocks), len(weights)
    block_rows, row_width = row_blocks[0].shape
    _, width, hidden_width = weights[0][0].shape
    total = blocks * block_rows
    padded = max(total, PASS_ROWS // block_rows * block_rows) if experts == 1 else total
    return pl.pallas_call(
        functools.partial(expert_kernel, blocks, flips, bool(prior), top_count),
        out_shape=[made((block_rows, width), jnp.float32)] * blocks,
        in_specs=[IN_VMEM] * (blocks + 3 * experts + len(prior)),
        out_specs=[IN_VMEM] * blocks,
        scratch_shapes=[
            pltpu.VMEM((padded, row_width), jnp.bfloat16),
            pltpu.VMEM((total, width), jnp.float32),
        ],
        compiler_params=pltpu.CompilerParams(vmem_limit_bytes=SCOPED_BYTES),
        cost_estimate=pl.CostEstimate(
            flops=6 * total * width * hidden_width * experts,
            bytes_accessed=2 * (3 * width * hidden_width * experts + 2 * total * width),
            transcendentals=total * hidden_width * experts,
        ),
    )(
        *(made.pin(block) for block in row_blocks),
        *(made.pin(array) for weight in weights for array in weight),
        *(made.pin(block) for block in prior),
    )


def first_kernel(rows_ref, gate_in, up_in, hidden_ref, gate_ref, up_ref, parts, sems):
    width = gate_ref.shape[1]
    deep = even_split(width, DEPTH_STEP)
    sides = ((gate_in, gate_ref), (up_in, up_ref))

    def copies(at):
        span = pl.ds(at * deep, deep)
        return [
            pltpu.make_async_copy(source.at[0, span, :], kept.at[0, span, :], sems.at[side, at])
            for side, (source, kept) in enumerate(sides)
        ]

    steps = width // deep
    for at in range(steps):
        for copy in copies(at):
            copy.start()
    for at in range(steps):
        for copy in copies(at):
            copy.wait()
        span = pl.ds(at * deep, deep)
        for side, (_, kept) in enumerate(sides):
            now = jnp.dot(rows_ref[:, span], kept[0, span, :], preferred_element_type=jnp.float32)
            if at == 0:
                parts[side] = now
            else:
                parts[side] += now
    gate_part, up_part = parts[0], parts[1]
    hidden_ref[...] = (gate_part / (1.0 + jnp.exp(-gate_part)) * up_part).astype(jnp.bfloat16)


def second_kernel(top_count, rows_ref, hidden_ref, down_in, out_ref, down_ref, sems):
    hidden_width, width = down_ref.shape[1:]
    wide = even_split(hidden_width, HIDDEN_STEP)

    def copy(at):
        span = pl.ds(at * wide, wide)
        return pltpu.make_async_copy(down_in.at[0, span, :], down_ref.at[0, span, :], sems.at[at])

    steps = hidden_width // wide
    for at in range(steps):
        copy(at).start()
    scale = row_scale(rows_ref[:, width:], lax.axis_index("expert"), top_count)
    for at in range(steps):
        copy(at).wait()
        span = pl.ds(at * wide, wide)
        now = jnp.dot(hidden_ref[:, span], down_ref[0, span, :], preferred_element_type=jnp.float32)
        if at == 0:
            out_ref[...] = now
        else:
            out_ref[...] += now
    out_ref[...] = out_ref[...] * scale


def take_inputs_in(made, block, gate, up):
    _, width, hidden_width = gate.shape
    rows = block.shape[0]
    hidden, gate, up = pl.pallas_call(
        first_kernel,
        out_shape=[made((rows, hidden_width), jnp.bfloat16)] + [made(gate.shape, gate.dtype)] * 2,
        in_specs=[IN_VMEM] + [IN_HBM] * 2,
        out_specs=[IN_VMEM] * 3,
        scratch_shapes=[
            pltpu.VMEM((2, rows, hidden_width), jnp.float32),
            pltpu.SemaphoreType.DMA((2, width // even_split(width, DEPTH_STEP))),
        ],
        compiler_params=pltpu.CompilerParams(vmem_limit_bytes=SCOPED_BYTES),
        cost_estimate=pl.CostEstimate(
            flops=4 * rows * width * hidden_width,
            bytes_accessed=4 * width * hidden_width,
            transcendentals=rows * hidden_width,
        ),
    )(made.pin(block), in_hbm(gate), in_hbm(up))
    return hidden, gate, up


def take_output_in(made, top_count, block, hidden, down):
    _, hidden_width, width = down.shape
    rows = block.shape[0]
    return pl.pallas_call(
        functools.partial(second_kernel, top_count),
        out_shape=[made((rows, width), jnp.float32), made(down.shape, down.dtype)],
        in_specs=[IN_VMEM] * 2 + [IN_HBM],
        out_specs=[IN_VMEM] * 2,
        scratch_shapes=[
            pltpu.SemaphoreType.DMA((hidden_width // even_split(hidden_width, HIDDEN_STEP),))
        ],
        compiler_params=pltpu.CompilerParams(vmem_limit_bytes=SCOPED_BYTES),
        cost_estimate=pl.CostEstimate(
            flops=2 * rows * width * hidden_width,
            bytes_accessed=2 * width * hidden_width,
            transcendentals=0,
        ),
    )(made.pin(block), made.pin(hidden), in_hbm(down))


class InVmem:
    def __call__(self, shape, dtype):
        return pltpu.VMEM(shape, dtype)

    def pin(self, array):
        return pltpu.with_memory_space_constraint(array, pltpu.VMEM)


class Anywhere:
    def __call__(self, shape, dtype):
        return jax.ShapeDtypeStruct(shape, dtype)

    def pin(self, array):
        return array


def add_rounded(*terms):
    return sum(term.astype(jnp.float32) for term in terms).astype(jnp.bfloat16)


def shards(tokens, expert_ids, gate_weights, w_gate, w_up, w_down):
    local, width = tokens.shape
    top_count = expert_ids.shape[1]
    devices = lax.axis_size("expert")
    ring = chip_ring(devices // 2)
    ways = (ring_pairs(ring, 1), ring_pairs(ring, -1))
    siblings = [(at, at ^ 1) for at in range(devices)]
    hops = (len(ring) // 2, (len(ring) - 1) // 2)
    own = (w_gate, w_up, w_down)
    weight_bytes = 2 * sum(array.size * array.dtype.itemsize for array in own)
    kept_bytes = weight_bytes + len(ring) * local * width * 6
    made = InVmem() if kept_bytes <= KEPT_BYTES else Anywhere()
    run = functools.partial(run_experts, made, top_count)
    after = lax.optimization_barrier

    def outward(block, way):
        return lax.ppermute(block, "expert", ways[way])

    def homeward(block, way):
        return lax.ppermute(block, "expert", ways[1 - way])

    first = pack_rows(tokens, expert_ids, gate_weights, made)
    other = tuple(lax.ppermute(array, "expert", siblings) for array in own)

    rows = {(0, 0): first}
    partial = {}
    if hops[0]:
        rows[0, 1] = outward(first, 0)
    hidden, gate, up = take_inputs_in(made, first, w_gate, w_up)
    if hops[1]:
        later, hidden = after((first, hidden))
        rows[1, 1] = outward(later, 1)
    partial[0, 0], down = take_output_in(made, top_count, first, hidden, w_down)
    own = (gate, up, down)
    if hops[0]:
        rows[0, 1], partial[0, 0] = after((rows[0, 1], partial[0, 0]))
    for hop in range(2, hops[0] + 1):
        rows[0, hop] = outward(rows[0, hop - 1], 0)
        keys = [(0, hop - 1)] + [(1, hop - 2)] * (hop > 2)
        results = run([rows[key] for key in keys], (0,), [own])
        rows[1, hop - 1], results = after((rows[1, hop - 1], results))
        partial.update(zip(keys, results))
        if hop <= hops[1]:
            rows[1, hop] = outward(rows[1, hop - 1], 1)
    keys = [key for key in rows if key not in partial]
    if keys:
        results = run([rows[key] for key in keys], (0, 1), [own, other])
        partial.update(zip(keys, results))

    def sibling_sums(keys, prior):
        return run([rows[key] for key in keys], (1,), [other], prior)

    if hops[0] < 2:
        partial[0, 0] = sibling_sums([(0, 0)], [partial[0, 0]])[0]
    arrived = [None, None]
    level = list(hops)
    while level[0]:
        values = [None, None]
        values[0] = add_rounded(partial[0, level[0]], *[x for x in arrived[:1] if x is not None])
        arrived[0] = homeward(values[0], 0)
        keys = [(way, at - 1) for way, at in enumerate(level) if at > 1]
        keys = [key for key in keys if key in partial and key != (1, hops[0] - 1)]
        keys += [(0, 0)] * (level[0] == 2)
        waiting = arrived[1] if arrived[1] is not None else partial.get((1, level[1]))
        if keys:
            prior, _ = after(([partial[key] for key in keys], values[0]))
            waiting, results = after((waiting, sibling_sums(keys, prior)))
            partial.update(zip(keys, results))
        if level[1]:
            values[1] = add_rounded(*([waiting] if arrived[1] is None else [waiting, partial[1, level[1]]]))
            arrived[1] = homeward(values[1], 1)
        elif arrived[1] is not None:
            arrived[1] = waiting
        level = [max(at - 1, 0) for at in level]
    total = partial[0, 0]
    if arrived[1] is not None:
        total, arrived[0] = after((total + arrived[1].astype(jnp.float32), arrived[0]))
    return add_rounded(total, *[value for value in arrived[:1] if value is not None])


def solution(mesh):
    placed = (
        P(("groups", "expert"), None),
        P(("groups", "expert"), None),
        P(("groups", "expert"), None),
        P("expert", None, None),
        P("expert", None, None),
        P("expert", None, None),
    )
    return jax.shard_map(
        shards, mesh=mesh, in_specs=placed, out_specs=P(("groups", "expert"), None), check_vma=False
    )
```

```python
import functools

import jax
import jax.numpy as jnp
from jax import lax
from jax.experimental import pallas as pl
from jax.experimental.pallas import tpu as pltpu
from jax.sharding import PartitionSpec as P

LANES = 128
IN_VMEM = pl.BlockSpec(memory_space=pltpu.VMEM)
IN_HBM = pl.BlockSpec(memory_space=pltpu.HBM)
DEPTH_STEP = 512
HIDDEN_STEP = 256
PASS_ROWS = 192
SCOPED_BYTES = 8 * 1024 * 1024
KEPT_BYTES = 32 * 1024 * 1024


def in_hbm(array):
    return pltpu.with_memory_space_constraint(array, pltpu.HBM)


def even_split(size, most):
    part = most
    while size % part:
        part //= 2
    return part


def chip_ring(chips):
    across = max(d for d in range(1, chips + 1) if chips % d == 0 and d * d <= chips)
    down = chips // across
    if across == 1 or down % 2:
        return list(range(chips))
    ring = []
    for row in range(down):
        columns = list(range(1, across))
        ring += [row * across + column for column in (columns if row % 2 == 0 else columns[::-1])]
    return [0] + ring + [row * across for row in range(down - 1, 0, -1)]


def ring_pairs(ring, way):
    count = len(ring)
    pairs = []
    for at, chip in enumerate(ring):
        for core in (0, 1):
            step = way if core == at % 2 else -way
            pairs.append((2 * chip + core, 2 * ring[(at + step) % count] + 1 - core))
    return pairs


def pack_kernel(tokens_ref, ids_ref, gates_ref, out_ref, ids_buf, gates_buf, sems):
    width = tokens_ref.shape[1]
    copies = [
        pltpu.make_async_copy(ids_ref, ids_buf, sems.at[0]),
        pltpu.make_async_copy(gates_ref, gates_buf, sems.at[1]),
        pltpu.make_async_copy(tokens_ref, out_ref.at[:, pl.ds(0, width)], sems.at[2]),
    ]
    for copy in copies:
        copy.start()
    for copy in copies[:2]:
        copy.wait()
    rest = gates_buf[...]
    parts = [ids_buf[...].astype(jnp.float32)]
    for _ in range(3):
        parts.append(rest.astype(jnp.bfloat16).astype(jnp.float32))
        rest = rest - parts[-1]
    stacked = jnp.concatenate(parts, axis=0)
    shape = (stacked.shape[0], out_ref.shape[1] - width)
    unit = lax.broadcasted_iota(jnp.int32, shape, 0) == lax.broadcasted_iota(jnp.int32, shape, 1)
    route = lax.dot_general(
        stacked.astype(jnp.bfloat16),
        unit.astype(jnp.float32).astype(jnp.bfloat16),
        (((0,), (0,)), ((), ())),
        preferred_element_type=jnp.float32,
    )
    out_ref[:, width:] = route.astype(jnp.bfloat16)
    copies[2].wait()


def pack_rows(tokens, expert_ids, gate_weights, made):
    rows, width = tokens.shape
    extra = -(-4 * expert_ids.shape[1] // LANES) * LANES
    ids, gates = expert_ids.T, gate_weights.T
    return pl.pallas_call(
        pack_kernel,
        out_shape=made((rows, width + extra), jnp.bfloat16),
        in_specs=[IN_HBM] * 3,
        out_specs=IN_VMEM,
        scratch_shapes=[
            pltpu.VMEM(ids.shape, ids.dtype),
            pltpu.VMEM(gates.shape, gates.dtype),
            pltpu.SemaphoreType.DMA((3,)),
        ],
        compiler_params=pltpu.CompilerParams(vmem_limit_bytes=SCOPED_BYTES),
    )(in_hbm(tokens), in_hbm(ids), in_hbm(gates))


def row_scale(route, expert, top_count):
    route = route.astype(jnp.float32)
    chosen = (route[:, :top_count] == expert.astype(jnp.float32)).astype(jnp.float32)
    weight = sum(route[:, top_count * part : top_count * (part + 1)] for part in (1, 2, 3))
    return jnp.sum(chosen * weight, axis=1, keepdims=True)


def expert_kernel(blocks, flips, with_prior, top_count, *refs):
    row_refs, refs = refs[:blocks], refs[blocks:]
    weight_refs, refs = refs[: 3 * len(flips)], refs[3 * len(flips) :]
    prior_refs, refs = (refs[:blocks], refs[blocks:]) if with_prior else ((), refs)
    out_refs, (rows_buf, total) = refs[:blocks], refs[blocks:]
    block_rows, width = out_refs[0].shape
    real = blocks * block_rows
    me = lax.axis_index("expert")
    for at in range(rows_buf.shape[0] // block_rows):
        rows_buf[pl.ds(at * block_rows, block_rows), :] = row_refs[at % blocks][...]
    for at in range(blocks if with_prior else 0):
        total[pl.ds(at * block_rows, block_rows), :] = prior_refs[at][...]
    rows = rows_buf[:, :width]
    for at, flip in enumerate(flips):
        gate_ref, up_ref, down_ref = weight_refs[3 * at : 3 * at + 3]
        scale = row_scale(rows_buf[:real, width:], me ^ flip, top_count)
        gate_part = jnp.dot(rows, gate_ref[0], preferred_element_type=jnp.float32)
        up_part = jnp.dot(rows, up_ref[0], preferred_element_type=jnp.float32)
        hidden = (gate_part / (1.0 + jnp.exp(-gate_part)) * up_part).astype(jnp.bfloat16)
        result = jnp.dot(hidden, down_ref[0], preferred_element_type=jnp.float32)[:real] * scale
        if at or with_prior:
            total[...] += result
        else:
            total[...] = result
    for at in range(blocks):
        out_refs[at][...] = total[pl.ds(at * block_rows, block_rows), :]


def run_experts(made, top_count, row_blocks, flips, weights, prior=()):
    blocks, experts = len(row_blocks), len(weights)
    block_rows, row_width = row_blocks[0].shape
    _, width, hidden_width = weights[0][0].shape
    total = blocks * block_rows
    padded = max(total, PASS_ROWS // block_rows * block_rows) if experts == 1 else total
    return pl.pallas_call(
        functools.partial(expert_kernel, blocks, flips, bool(prior), top_count),
        out_shape=[made((block_rows, width), jnp.float32)] * blocks,
        in_specs=[IN_VMEM] * (blocks + 3 * experts + len(prior)),
        out_specs=[IN_VMEM] * blocks,
        scratch_shapes=[
            pltpu.VMEM((padded, row_width), jnp.bfloat16),
            pltpu.VMEM((total, width), jnp.float32),
        ],
        compiler_params=pltpu.CompilerParams(vmem_limit_bytes=SCOPED_BYTES),
        cost_estimate=pl.CostEstimate(
            flops=6 * total * width * hidden_width * experts,
            bytes_accessed=2 * (3 * width * hidden_width * experts + 2 * total * width),
            transcendentals=total * hidden_width * experts,
        ),
    )(
        *(made.pin(block) for block in row_blocks),
        *(made.pin(array) for weight in weights for array in weight),
        *(made.pin(block) for block in prior),
    )


def staged(sources, width, step, sems):
    part = even_split(width, step)
    spans = [pl.ds(at, part) for at in range(0, width, part)]
    copies = [
        [
            pltpu.make_async_copy(source.at[0, span, :], kept.at[0, span, :], sems.at[side, at])
            for side, (source, kept) in enumerate(sources)
        ]
        for at, span in enumerate(spans)
    ]
    return spans, copies


def add_product(total, at, left, right):
    now = jnp.dot(left, right, preferred_element_type=jnp.float32)
    if at == 0:
        total[...] = now
    else:
        total[...] += now


def first_kernel(rows_ref, gate_in, active_ref, gate_ref, sems):
    spans, copies = staged([(gate_in, gate_ref)], gate_ref.shape[1], DEPTH_STEP, sems)
    for (copy,) in copies:
        copy.start()
    for at, span in enumerate(spans):
        copies[at][0].wait()
        add_product(active_ref, at, rows_ref[:, span], gate_ref[0, span, :])
    gate_part = active_ref[...]
    active_ref[...] = gate_part / (1.0 + jnp.exp(-gate_part))


def second_kernel(
    top_count, rows_ref, active_ref, up_in, down_in, out_ref, up_ref, down_ref, up_part, up_sems, down_sems
):
    width, hidden_width = up_ref.shape[1:]
    up_spans, up_copies = staged([(up_in, up_ref)], width, DEPTH_STEP, up_sems)
    down_spans, down_copies = staged([(down_in, down_ref)], hidden_width, HIDDEN_STEP, down_sems)
    for (copy,) in up_copies + down_copies:
        copy.start()
    for at, span in enumerate(up_spans):
        up_copies[at][0].wait()
        add_product(up_part, at, rows_ref[:, span], up_ref[0, span, :])
    hidden = (active_ref[...] * up_part[...]).astype(jnp.bfloat16)
    scale = row_scale(rows_ref[:, width:], lax.axis_index("expert"), top_count)
    for at, span in enumerate(down_spans):
        down_copies[at][0].wait()
        left = hidden[:, span.start : span.start + span.size]
        add_product(out_ref, at, left, down_ref[0, span, :])
    out_ref[...] = out_ref[...] * scale


def take_gate_in(made, block, gate):
    _, width, hidden_width = gate.shape
    rows = block.shape[0]
    return pl.pallas_call(
        first_kernel,
        out_shape=[made((rows, hidden_width), jnp.float32), made(gate.shape, gate.dtype)],
        in_specs=[IN_VMEM, IN_HBM],
        out_specs=[IN_VMEM] * 2,
        scratch_shapes=[pltpu.SemaphoreType.DMA((1, width // even_split(width, DEPTH_STEP)))],
        compiler_params=pltpu.CompilerParams(vmem_limit_bytes=SCOPED_BYTES),
        cost_estimate=pl.CostEstimate(
            flops=2 * rows * width * hidden_width,
            bytes_accessed=2 * width * hidden_width,
            transcendentals=rows * hidden_width,
        ),
    )(made.pin(block), in_hbm(gate))


def take_rest_in(made, top_count, block, active, up, down):
    _, hidden_width, width = down.shape
    rows = block.shape[0]
    return pl.pallas_call(
        functools.partial(second_kernel, top_count),
        out_shape=[
            made((rows, width), jnp.float32),
            made(up.shape, up.dtype),
            made(down.shape, down.dtype),
        ],
        in_specs=[IN_VMEM] * 2 + [IN_HBM] * 2,
        out_specs=[IN_VMEM] * 3,
        scratch_shapes=[
            pltpu.VMEM((rows, hidden_width), jnp.float32),
            pltpu.SemaphoreType.DMA((1, width // even_split(width, DEPTH_STEP))),
            pltpu.SemaphoreType.DMA((1, hidden_width // even_split(hidden_width, HIDDEN_STEP))),
        ],
        compiler_params=pltpu.CompilerParams(vmem_limit_bytes=SCOPED_BYTES),
        cost_estimate=pl.CostEstimate(
            flops=4 * rows * width * hidden_width,
            bytes_accessed=4 * width * hidden_width,
            transcendentals=0,
        ),
    )(made.pin(block), made.pin(active), in_hbm(up), in_hbm(down))


class InVmem:
    def __call__(self, shape, dtype):
        return pltpu.VMEM(shape, dtype)

    def pin(self, array):
        return pltpu.with_memory_space_constraint(array, pltpu.VMEM)


class Anywhere:
    def __call__(self, shape, dtype):
        return jax.ShapeDtypeStruct(shape, dtype)

    def pin(self, array):
        return array


def add_rounded(*terms):
    return sum(term.astype(jnp.float32) for term in terms).astype(jnp.bfloat16)


def shards(tokens, expert_ids, gate_weights, w_gate, w_up, w_down):
    local, width = tokens.shape
    top_count = expert_ids.shape[1]
    devices = lax.axis_size("expert")
    ring = chip_ring(devices // 2)
    ways = (ring_pairs(ring, 1), ring_pairs(ring, -1))
    siblings = [(at, at ^ 1) for at in range(devices)]
    hops = (len(ring) // 2, (len(ring) - 1) // 2)
    own = (w_gate, w_up, w_down)
    weight_bytes = 2 * sum(array.size * array.dtype.itemsize for array in own)
    kept_bytes = weight_bytes + len(ring) * local * width * 6
    made = InVmem() if kept_bytes <= KEPT_BYTES else Anywhere()
    run = functools.partial(run_experts, made, top_count)
    after = lax.optimization_barrier

    def outward(block, way):
        return lax.ppermute(block, "expert", ways[way])

    def homeward(block, way):
        return lax.ppermute(block, "expert", ways[1 - way])

    first = pack_rows(tokens, expert_ids, gate_weights, made)
    first, ready = after((first, own))
    other = tuple(lax.ppermute(array, "expert", siblings) for array in ready)

    rows = {(0, 0): first}
    partial = {}
    if hops[0]:
        rows[0, 1] = outward(first, 0)
    active, gate = take_gate_in(made, first, w_gate)
    if hops[1]:
        later, active = after((first, active))
        rows[1, 1] = outward(later, 1)
    partial[0, 0], up, down = take_rest_in(made, top_count, first, active, w_up, w_down)
    own = (gate, up, down)
    if hops[0]:
        rows[0, 1], partial[0, 0] = after((rows[0, 1], partial[0, 0]))
    for hop in range(2, hops[0] + 1):
        rows[0, hop] = outward(rows[0, hop - 1], 0)
        keys = [(0, hop - 1)] + [(1, hop - 2)] * (hop > 2)
        results = run([rows[key] for key in keys], (0,), [own])
        rows[1, hop - 1], results = after((rows[1, hop - 1], results))
        partial.update(zip(keys, results))
        if hop <= hops[1]:
            rows[1, hop] = outward(rows[1, hop - 1], 1)
    keys = [key for key in rows if key not in partial]
    if keys:
        results = run([rows[key] for key in keys], (0, 1), [own, other])
        partial.update(zip(keys, results))

    def sibling_sums(keys, prior):
        return run([rows[key] for key in keys], (1,), [other], prior)

    if hops[0] < 2:
        partial[0, 0] = sibling_sums([(0, 0)], [partial[0, 0]])[0]
    arrived = [None, None]
    level = list(hops)
    while level[0]:
        values = [None, None]
        values[0] = add_rounded(partial[0, level[0]], *[x for x in arrived[:1] if x is not None])
        arrived[0] = homeward(values[0], 0)
        keys = [(way, at - 1) for way, at in enumerate(level) if at > 1]
        keys = [key for key in keys if key in partial and key != (1, hops[0] - 1)]
        keys += [(0, 0)] * (level[0] == 2)
        waiting = arrived[1] if arrived[1] is not None else partial.get((1, level[1]))
        if keys:
            prior, _ = after(([partial[key] for key in keys], values[0]))
            waiting, results = after((waiting, sibling_sums(keys, prior)))
            partial.update(zip(keys, results))
        if level[1]:
            values[1] = add_rounded(*([waiting] if arrived[1] is None else [waiting, partial[1, level[1]]]))
            arrived[1] = homeward(values[1], 1)
        elif arrived[1] is not None:
            arrived[1] = waiting
        level = [max(at - 1, 0) for at in level]
    return add_rounded(partial[0, 0], *[value for value in arrived if value is not None])


def solution(mesh):
    placed = (
        P(("groups", "expert"), None),
        P(("groups", "expert"), None),
        P(("groups", "expert"), None),
        P("expert", None, None),
        P("expert", None, None),
        P("expert", None, None),
    )
    return jax.shard_map(
        shards, mesh=mesh, in_specs=placed, out_specs=P(("groups", "expert"), None), check_vma=False
    )
```

```python
import functools

import jax
import jax.numpy as jnp
from jax import lax
from jax.experimental import pallas as pl
from jax.experimental.pallas import tpu as pltpu
from jax.sharding import PartitionSpec as P

LANES = 128
IN_VMEM = pl.BlockSpec(memory_space=pltpu.VMEM)
IN_HBM = pl.BlockSpec(memory_space=pltpu.HBM)
DEPTH_STEP = 512
HIDDEN_STEP = 256
PASS_ROWS = 192
SCOPED_BYTES = 8 * 1024 * 1024
KEPT_BYTES = 32 * 1024 * 1024


def in_hbm(array):
    return pltpu.with_memory_space_constraint(array, pltpu.HBM)


def even_split(size, most):
    part = most
    while size % part:
        part //= 2
    return part


def chip_ring(chips):
    across = max(d for d in range(1, chips + 1) if chips % d == 0 and d * d <= chips)
    down = chips // across
    if across == 1 or down % 2:
        return list(range(chips))
    ring = []
    for row in range(down):
        columns = list(range(1, across))
        ring += [row * across + column for column in (columns if row % 2 == 0 else columns[::-1])]
    return [0] + ring + [row * across for row in range(down - 1, 0, -1)]


def ring_pairs(ring, way):
    count = len(ring)
    pairs = []
    for at, chip in enumerate(ring):
        for core in (0, 1):
            step = way if core == at % 2 else -way
            pairs.append((2 * chip + core, 2 * ring[(at + step) % count] + 1 - core))
    return pairs


def pack_kernel(tokens_ref, ids_ref, gates_ref, out_ref, ids_buf, gates_buf, sems):
    width = tokens_ref.shape[1]
    copies = [
        pltpu.make_async_copy(ids_ref, ids_buf, sems.at[0]),
        pltpu.make_async_copy(gates_ref, gates_buf, sems.at[1]),
        pltpu.make_async_copy(tokens_ref, out_ref.at[:, pl.ds(0, width)], sems.at[2]),
    ]
    for copy in copies:
        copy.start()
    for copy in copies[:2]:
        copy.wait()
    rest = gates_buf[...]
    parts = [ids_buf[...].astype(jnp.float32)]
    for _ in range(3):
        parts.append(rest.astype(jnp.bfloat16).astype(jnp.float32))
        rest = rest - parts[-1]
    stacked = jnp.concatenate(parts, axis=0)
    shape = (stacked.shape[0], out_ref.shape[1] - width)
    unit = lax.broadcasted_iota(jnp.int32, shape, 0) == lax.broadcasted_iota(jnp.int32, shape, 1)
    route = lax.dot_general(
        stacked.astype(jnp.bfloat16),
        unit.astype(jnp.float32).astype(jnp.bfloat16),
        (((0,), (0,)), ((), ())),
        preferred_element_type=jnp.float32,
    )
    out_ref[:, width:] = route.astype(jnp.bfloat16)
    copies[2].wait()


def pack_rows(tokens, expert_ids, gate_weights, made):
    rows, width = tokens.shape
    extra = -(-4 * expert_ids.shape[1] // LANES) * LANES
    ids, gates = expert_ids.T, gate_weights.T
    return pl.pallas_call(
        pack_kernel,
        out_shape=made((rows, width + extra), jnp.bfloat16),
        in_specs=[IN_HBM] * 3,
        out_specs=IN_VMEM,
        scratch_shapes=[
            pltpu.VMEM(ids.shape, ids.dtype),
            pltpu.VMEM(gates.shape, gates.dtype),
            pltpu.SemaphoreType.DMA((3,)),
        ],
        compiler_params=pltpu.CompilerParams(vmem_limit_bytes=SCOPED_BYTES),
    )(in_hbm(tokens), in_hbm(ids), in_hbm(gates))


def row_scale(route, expert, top_count):
    route = route.astype(jnp.float32)
    chosen = (route[:, :top_count] == expert.astype(jnp.float32)).astype(jnp.float32)
    weight = sum(route[:, top_count * part : top_count * (part + 1)] for part in (1, 2, 3))
    return jnp.sum(chosen * weight, axis=1, keepdims=True)


def expert_kernel(blocks, flips, with_prior, top_count, *refs):
    row_refs, refs = refs[:blocks], refs[blocks:]
    weight_refs, refs = refs[: 3 * len(flips)], refs[3 * len(flips) :]
    prior_refs, refs = (refs[:blocks], refs[blocks:]) if with_prior else ((), refs)
    out_refs, (rows_buf, total) = refs[:blocks], refs[blocks:]
    block_rows, width = out_refs[0].shape
    real = blocks * block_rows
    me = lax.axis_index("expert")
    for at in range(rows_buf.shape[0] // block_rows):
        rows_buf[pl.ds(at * block_rows, block_rows), :] = row_refs[at % blocks][...]
    for at in range(blocks if with_prior else 0):
        total[pl.ds(at * block_rows, block_rows), :] = prior_refs[at][...]
    rows = rows_buf[:, :width]
    for at, flip in enumerate(flips):
        gate_ref, up_ref, down_ref = weight_refs[3 * at : 3 * at + 3]
        scale = row_scale(rows_buf[:real, width:], me ^ flip, top_count)
        gate_part = jnp.dot(rows, gate_ref[0], preferred_element_type=jnp.float32)
        up_part = jnp.dot(rows, up_ref[0], preferred_element_type=jnp.float32)
        hidden = (gate_part / (1.0 + jnp.exp(-gate_part)) * up_part).astype(jnp.bfloat16)
        result = jnp.dot(hidden, down_ref[0], preferred_element_type=jnp.float32)[:real] * scale
        if at or with_prior:
            total[...] += result
        else:
            total[...] = result
    for at in range(blocks):
        out_refs[at][...] = total[pl.ds(at * block_rows, block_rows), :]


def run_experts(made, top_count, row_blocks, flips, weights, prior=()):
    blocks, experts = len(row_blocks), len(weights)
    block_rows, row_width = row_blocks[0].shape
    _, width, hidden_width = weights[0][0].shape
    total = blocks * block_rows
    padded = max(total, PASS_ROWS // block_rows * block_rows) if experts == 1 else total
    return pl.pallas_call(
        functools.partial(expert_kernel, blocks, flips, bool(prior), top_count),
        out_shape=[made((block_rows, width), jnp.float32)] * blocks,
        in_specs=[IN_VMEM] * (blocks + 3 * experts + len(prior)),
        out_specs=[IN_VMEM] * blocks,
        scratch_shapes=[
            pltpu.VMEM((padded, row_width), jnp.bfloat16),
            pltpu.VMEM((total, width), jnp.float32),
        ],
        compiler_params=pltpu.CompilerParams(vmem_limit_bytes=SCOPED_BYTES),
        cost_estimate=pl.CostEstimate(
            flops=6 * total * width * hidden_width * experts,
            bytes_accessed=2 * (3 * width * hidden_width * experts + 2 * total * width),
            transcendentals=total * hidden_width * experts,
        ),
    )(
        *(made.pin(block) for block in row_blocks),
        *(made.pin(array) for weight in weights for array in weight),
        *(made.pin(block) for block in prior),
    )


def first_kernel(rows_ref, gate_in, up_in, hidden_ref, gate_ref, up_ref, parts, sems):
    width = gate_ref.shape[1]
    deep = even_split(width, DEPTH_STEP)
    sides = ((gate_in, gate_ref), (up_in, up_ref))

    def copies(at):
        span = pl.ds(at * deep, deep)
        return [
            pltpu.make_async_copy(source.at[0, span, :], kept.at[0, span, :], sems.at[side, at])
            for side, (source, kept) in enumerate(sides)
        ]

    steps = width // deep
    for at in range(steps):
        for copy in copies(at):
            copy.start()
    for at in range(steps):
        for copy in copies(at):
            copy.wait()
        span = pl.ds(at * deep, deep)
        for side, (_, kept) in enumerate(sides):
            now = jnp.dot(rows_ref[:, span], kept[0, span, :], preferred_element_type=jnp.float32)
            if at == 0:
                parts[side] = now
            else:
                parts[side] += now
    gate_part, up_part = parts[0], parts[1]
    hidden_ref[...] = (gate_part / (1.0 + jnp.exp(-gate_part)) * up_part).astype(jnp.bfloat16)


def second_kernel(top_count, rows_ref, hidden_ref, down_in, out_ref, down_ref, sems):
    hidden_width, width = down_ref.shape[1:]
    wide = even_split(hidden_width, HIDDEN_STEP)

    def copy(at):
        span = pl.ds(at * wide, wide)
        return pltpu.make_async_copy(down_in.at[0, span, :], down_ref.at[0, span, :], sems.at[at])

    steps = hidden_width // wide
    for at in range(steps):
        copy(at).start()
    scale = row_scale(rows_ref[:, width:], lax.axis_index("expert"), top_count)
    for at in range(steps):
        copy(at).wait()
        span = pl.ds(at * wide, wide)
        now = jnp.dot(hidden_ref[:, span], down_ref[0, span, :], preferred_element_type=jnp.float32)
        if at == 0:
            out_ref[...] = now
        else:
            out_ref[...] += now
    out_ref[...] = out_ref[...] * scale


def take_inputs_in(made, block, gate, up):
    _, width, hidden_width = gate.shape
    rows = block.shape[0]
    hidden, gate, up = pl.pallas_call(
        first_kernel,
        out_shape=[made((rows, hidden_width), jnp.bfloat16)] + [made(gate.shape, gate.dtype)] * 2,
        in_specs=[IN_VMEM] + [IN_HBM] * 2,
        out_specs=[IN_VMEM] * 3,
        scratch_shapes=[
            pltpu.VMEM((2, rows, hidden_width), jnp.float32),
            pltpu.SemaphoreType.DMA((2, width // even_split(width, DEPTH_STEP))),
        ],
        compiler_params=pltpu.CompilerParams(vmem_limit_bytes=SCOPED_BYTES),
        cost_estimate=pl.CostEstimate(
            flops=4 * rows * width * hidden_width,
            bytes_accessed=4 * width * hidden_width,
            transcendentals=rows * hidden_width,
        ),
    )(made.pin(block), in_hbm(gate), in_hbm(up))
    return hidden, gate, up


def take_output_in(made, top_count, block, hidden, down):
    _, hidden_width, width = down.shape
    rows = block.shape[0]
    return pl.pallas_call(
        functools.partial(second_kernel, top_count),
        out_shape=[made((rows, width), jnp.float32), made(down.shape, down.dtype)],
        in_specs=[IN_VMEM] * 2 + [IN_HBM],
        out_specs=[IN_VMEM] * 2,
        scratch_shapes=[
            pltpu.SemaphoreType.DMA((hidden_width // even_split(hidden_width, HIDDEN_STEP),))
        ],
        compiler_params=pltpu.CompilerParams(vmem_limit_bytes=SCOPED_BYTES),
        cost_estimate=pl.CostEstimate(
            flops=2 * rows * width * hidden_width,
            bytes_accessed=2 * width * hidden_width,
            transcendentals=0,
        ),
    )(made.pin(block), made.pin(hidden), in_hbm(down))


class InVmem:
    def __call__(self, shape, dtype):
        return pltpu.VMEM(shape, dtype)

    def pin(self, array):
        return pltpu.with_memory_space_constraint(array, pltpu.VMEM)


class Anywhere:
    def __call__(self, shape, dtype):
        return jax.ShapeDtypeStruct(shape, dtype)

    def pin(self, array):
        return array


def add_rounded(*terms):
    return sum(term.astype(jnp.float32) for term in terms).astype(jnp.bfloat16)


def shards(tokens, expert_ids, gate_weights, w_gate, w_up, w_down):
    local, width = tokens.shape
    top_count = expert_ids.shape[1]
    devices = lax.axis_size("expert")
    ring = chip_ring(devices // 2)
    ways = (ring_pairs(ring, 1), ring_pairs(ring, -1))
    siblings = [(at, at ^ 1) for at in range(devices)]
    hops = (len(ring) // 2, (len(ring) - 1) // 2)
    own = (w_gate, w_up, w_down)
    weight_bytes = 2 * sum(array.size * array.dtype.itemsize for array in own)
    kept_bytes = weight_bytes + len(ring) * local * width * 6
    made = InVmem() if kept_bytes <= KEPT_BYTES else Anywhere()
    run = functools.partial(run_experts, made, top_count)
    after = lax.optimization_barrier

    def outward(block, way):
        return lax.ppermute(block, "expert", ways[way])

    def homeward(block, way):
        return lax.ppermute(block, "expert", ways[1 - way])

    first = pack_rows(tokens, expert_ids, gate_weights, made)
    first, ready = after((first, own))
    other = tuple(lax.ppermute(array, "expert", siblings) for array in ready)

    rows = {(0, 0): first}
    partial = {}
    if hops[0]:
        rows[0, 1] = outward(first, 0)
    hidden, gate, up = take_inputs_in(made, first, w_gate, w_up)
    if hops[1]:
        later, hidden = after((first, hidden))
        rows[1, 1] = outward(later, 1)
    partial[0, 0], down = take_output_in(made, top_count, first, hidden, w_down)
    own = (gate, up, down)
    if hops[0]:
        rows[0, 1], partial[0, 0] = after((rows[0, 1], partial[0, 0]))
    for hop in range(2, hops[0] + 1):
        rows[0, hop] = outward(rows[0, hop - 1], 0)
        keys = [(0, hop - 1)] + [(1, hop - 2)] * (hop > 2)
        results = run([rows[key] for key in keys], (0,), [own])
        rows[1, hop - 1], results = after((rows[1, hop - 1], results))
        partial.update(zip(keys, results))
        if hop <= hops[1]:
            rows[1, hop] = outward(rows[1, hop - 1], 1)
    keys = [key for key in rows if key not in partial]
    if keys:
        results = run([rows[key] for key in keys], (0, 1), [own, other])
        partial.update(zip(keys, results))

    def sibling_sums(keys, prior):
        return run([rows[key] for key in keys], (1,), [other], prior)

    if hops[0] < 2:
        partial[0, 0] = sibling_sums([(0, 0)], [partial[0, 0]])[0]
    arrived = [None, None]
    level = list(hops)
    while level[0]:
        values = [None, None]
        values[0] = add_rounded(partial[0, level[0]], *[x for x in arrived[:1] if x is not None])
        arrived[0] = homeward(values[0], 0)
        keys = [(way, at - 1) for way, at in enumerate(level) if at > 1]
        keys = [key for key in keys if key in partial and key != (1, hops[0] - 1)]
        keys += [(0, 0)] * (level[0] == 2)
        waiting = arrived[1] if arrived[1] is not None else partial.get((1, level[1]))
        if keys:
            prior, _ = after(([partial[key] for key in keys], values[0]))
            waiting, results = after((waiting, sibling_sums(keys, prior)))
            partial.update(zip(keys, results))
        if level[1]:
            values[1] = add_rounded(*([waiting] if arrived[1] is None else [waiting, partial[1, level[1]]]))
            arrived[1] = homeward(values[1], 1)
        elif arrived[1] is not None:
            arrived[1] = waiting
        level = [max(at - 1, 0) for at in level]
    total = partial[0, 0]
    if arrived[1] is not None:
        total, arrived[0] = after((total + arrived[1].astype(jnp.float32), arrived[0]))
    return add_rounded(total, *[value for value in arrived[:1] if value is not None])


def solution(mesh):
    placed = (
        P(("groups", "expert"), None),
        P(("groups", "expert"), None),
        P(("groups", "expert"), None),
        P("expert", None, None),
        P("expert", None, None),
        P("expert", None, None),
    )
    return jax.shard_map(
        shards, mesh=mesh, in_specs=placed, out_specs=P(("groups", "expert"), None), check_vma=False
    )
```
